32 devices in a mesh: groups: 2 (over x), tm: 8 (over z, y), site: 2 (over core).
Axes of the slice: x: 2, y: 2, z: 4, core: 2. Of those that a mesh axis runs over, the one named last changes fastest.
Arguments:
- features: float32 [4, 4096, 128], P(('groups', 'site'), 'tm'), parts along dimension 0, may hold values from -18 to 18
- forget: float32 [4, 4096, 128], P(('groups', 'site'), 'tm'), parts along dimension 0, may hold values from 1.2207031e-05 to 0.5, as said below
- labels: int32 [4, 4096], P(('groups', 'site'), 'tm'), parts along dimension 0, may hold values from 0 to 127
- lengths: int32 [4], P(('groups', 'site')), parts along dimension 0, may hold values from 2048 to 4096, as said below
- w_conv: bfloat16 [2, 1024, 1024], P(None, ('tm', 'site')), may hold values from -0.1875 to 0.1875
- w_res: bfloat16 [2, 512, 512], P(None, ('tm', 'site')), may hold values from -0.25 to 0.25
- w_in: bfloat16 [128, 512], P(('tm', 'site')), may hold values from -0.5 to 0.5
- w_out: bfloat16 [512, 128], P(('tm', 'site')), may hold values from -0.25 to 0.25
Outputs:
- row_loss: float32 [4, 4096], P(('groups', 'site'), 'tm'), parts along dimension 0
- grad_conv: float32 [4, 1024, 1024], P('groups', ('tm', 'site')), parts along dimension 0
- grad_res: float32 [4, 512, 512], P('groups', ('tm', 'site')), parts along dimension 0
- grad_in: float32 [128, 1024], P(('tm', 'site'), 'groups'), parts along dimension 1
- grad_out: float32 [512, 256], P(('tm', 'site'), 'groups'), parts along dimension 1
The draws below stay inside these ranges and needn't reach their ends.
There are 2 independent parts, one for each index of `groups`. The reference program is written for one: setup_inputs(seed, part) draws one part's arguments, and reference() takes and returns one part's arrays. A program takes and returns all parts, laid end to end along the dimension named above; an argument that names none is the same for every part. Nothing has to cross between parts.
Inputs may be any that keep to these rules, and one draw needn't show every extreme that they name: `forget`: every entry is positive. `lengths`: at least one site is valid over all 4096 steps.
All inputs are finite; a program needn't handle non-finite values.
Results may differ from the reference program's by a relative error of at most 0.02.
Values may be sent and summed in bfloat16 or wider, within the bound.
No kernel may reach another device: no remote copies, remote signals or barrier semaphores. Data moves between devices by JAX's collectives and lax.ppermute only.
A program may use at most 128 MiB of HBM per device.

```python
import math
import jax
import jax.numpy as jnp
from jax import lax

C = 512
F = 128
K = 128
LAYERS = 2
BASE_DILATION = 256
T_DEV = 512
SITE_TOTAL = 2
TIME_STEPS = 4096


def draw_features(key, part):
    key_values, key_scales = jax.random.split(key)
    blocks = TIME_STEPS // T_DEV
    raw_values = jnp.clip(jax.random.normal(key_values, (SITE_TOTAL, TIME_STEPS, F), jnp.float32), -6.0, 6.0)
    scales = jnp.exp(jax.random.uniform(key_scales, (SITE_TOTAL, blocks, 1, F), jnp.float32, math.log(0.3), math.log(3.0)))
    return (raw_values.reshape(SITE_TOTAL, blocks, T_DEV, F) * scales).reshape(SITE_TOTAL, TIME_STEPS, F)


def draw_forget(key, part):
    random_subkeys = jax.random.split(key, 6)
    blocks = TIME_STEPS // T_DEV
    share_slow = 0.5
    slow_mask = jax.random.bernoulli(random_subkeys[0], share_slow, (SITE_TOTAL, 1, 1, F))
    fast_rate = jnp.exp(jax.random.uniform(random_subkeys[1], (SITE_TOTAL, 1, 1, F), jnp.float32, math.log(10.0), math.log(17.0))) / T_DEV
    slow_rate = jnp.exp(jax.random.uniform(random_subkeys[2], (SITE_TOTAL, 1, 1, F), jnp.float32, math.log(0.1), math.log(1.0))) / TIME_STEPS
    factors = jnp.exp(jax.random.uniform(random_subkeys[3], (SITE_TOTAL, blocks, 1, F), jnp.float32, math.log(0.5), math.log(2.0)))
    decay_rates = jnp.minimum(jnp.where(slow_mask, slow_rate, fast_rate) * factors, 0.5)
    decay_rates = jnp.broadcast_to(decay_rates, (SITE_TOTAL, blocks, T_DEV, F)).reshape(SITE_TOTAL, TIME_STEPS, F)
    spike_start = jax.random.randint(random_subkeys[4], (SITE_TOTAL, 2), 0, TIME_STEPS)
    spike_active = jnp.any(jnp.arange(TIME_STEPS)[None, :, None] == spike_start[:, None, :], axis=2)
    spike_length = jax.random.uniform(random_subkeys[5], (SITE_TOTAL, TIME_STEPS, 1), jnp.float32, 0.2, 0.5)
    return jnp.where(spike_active[:, :, None], spike_length, decay_rates)


def draw_lengths(key, part):
    key_base = jax.random.fold_in(key, 11)
    key_pick = jax.random.fold_in(key, 12)
    base_lengths = jax.random.randint(key_base, (SITE_TOTAL,), TIME_STEPS // 2, TIME_STEPS + 1)
    chosen_site = jax.random.randint(key_pick, (), 0, SITE_TOTAL)
    return jnp.where(jnp.arange(SITE_TOTAL) == chosen_site, TIME_STEPS, base_lengths).astype(jnp.int32)


def plant(result, key, least, high):
    index_at = [jax.random.randint(jax.random.fold_in(key, axis), (), 0, length) for axis, length in enumerate(result.shape)]
    main_axis = result.shape.index(max(result.shape))
    beside = index_at[:main_axis] + [(index_at[main_axis] + 1) % result.shape[main_axis]] + index_at[main_axis + 1:]
    return result.at[tuple(index_at)].set(least).at[tuple(beside)].set(high)


def block_scale(key, shape, cuts, low, top_value):
    loudness = 1.0
    for position, blocks in cuts:
        draws = jax.random.uniform(jax.random.fold_in(jax.random.fold_in(key, 6), position), (blocks,), jnp.float32, low / len(cuts), top_value / len(cuts))
        loudness = loudness * jnp.repeat(jnp.exp(draws), shape[position] // blocks).reshape((-1,) + (1,) * (len(shape) - 1 - position))
    return loudness


def noise(own_key, shape, deviation, most, cuts=(), held_as=jnp.bfloat16):
    values = deviation * jax.random.normal(own_key, shape, jnp.float32)
    if cuts:
        values = values * block_scale(own_key, shape, cuts, -0.22, 0.18)
    return jnp.clip(values, -most, most).astype(held_as)


def setup_inputs(seed: int = 0, part: int = 0) -> dict:
    key_list = jax.random.split(jax.random.key(seed), 9)
    part_splits = jax.random.split(jax.random.fold_in(key_list[8], part), 9)
    return {
        "features": draw_features(jax.random.fold_in(jax.random.fold_in(key_list[8], part), 71), part),
        "forget": draw_forget(jax.random.fold_in(jax.random.fold_in(key_list[8], part), 71), part),
        "labels": plant(jax.random.randint(part_splits[2], (SITE_TOTAL, TIME_STEPS), 0, K), jax.random.fold_in(part_splits[2], 1), 0, K - 1).astype(jnp.int32),
        "lengths": draw_lengths(jax.random.fold_in(jax.random.fold_in(key_list[8], part), 71), part),
        "w_conv": noise(key_list[4], (LAYERS, 2 * C, 2 * C), (2 * C) ** -0.5, 0.1875, ((1, 16),)),
        "w_res": noise(key_list[5], (LAYERS, C, C), C ** -0.5, 0.25, ((1, 16),)),
        "w_in": noise(key_list[6], (F, C), F ** -0.5, 0.5, ((0, 16),)),
        "w_out": noise(key_list[7], (C, K), C ** -0.5, 0.25, ((0, 16),)),
    }


level_floor = 0.1

def reference(features, forget, labels, lengths, w_conv, w_res, w_in, w_out):
    retain = 1.0 - forget
    inflow = forget * (features * features)

    def advance(carried, inputs):
        mass_sum, weight_sum = carried
        keep_now, inflow_now, forget_now = inputs
        mass_sum = keep_now * mass_sum + inflow_now
        weight_sum = keep_now * weight_sum + forget_now
        return ((mass_sum, weight_sum), mass_sum / weight_sum)
    initial = (jnp.zeros((SITE_TOTAL, F), jnp.float32), jnp.zeros((SITE_TOTAL, F), jnp.float32))
    _, smoothed = lax.scan(advance, initial, (jnp.swapaxes(retain, 0, 1), jnp.swapaxes(inflow, 0, 1), jnp.swapaxes(forget, 0, 1)))
    smoothed = jnp.swapaxes(smoothed, 0, 1)
    normed = (features / jnp.sqrt(smoothed + level_floor)).astype(jnp.bfloat16)
    row_count = SITE_TOTAL * TIME_STEPS
    flat_normed = normed.reshape(row_count, F)
    hidden_now = jnp.dot(flat_normed, w_in, preferred_element_type=jnp.float32).astype(jnp.bfloat16)
    hidden_now = hidden_now.reshape(SITE_TOTAL, TIME_STEPS, C)
    saved_layers = []
    for index_of_layer in range(LAYERS):
        dilation_step = BASE_DILATION * 2 ** index_of_layer
        shifted = jnp.pad(hidden_now, ((0, 0), (dilation_step, 0), (0, 0)))[:, :TIME_STEPS]
        joined = jnp.concatenate([shifted, hidden_now], axis=2).reshape(row_count, 2 * C)
        preact = jnp.dot(joined, w_conv[index_of_layer], preferred_element_type=jnp.float32)
        tanh_part = jnp.tanh(preact[:, :C])
        sigm_part = jax.nn.sigmoid(preact[:, C:])
        gated_out = (tanh_part * sigm_part).astype(jnp.bfloat16)
        updated = hidden_now.reshape(row_count, C).astype(jnp.float32) + jnp.dot(gated_out, w_res[index_of_layer], preferred_element_type=jnp.float32)
        saved_layers.append((joined, tanh_part, sigm_part, gated_out))
        hidden_now = updated.astype(jnp.bfloat16).reshape(SITE_TOTAL, TIME_STEPS, C)
    flat_hidden = hidden_now.reshape(row_count, C)
    logits = jnp.dot(flat_hidden, w_out, preferred_element_type=jnp.float32)
    log_total = jnp.log(lax.optimization_barrier(jnp.sum(jnp.exp(logits), axis=1)))
    target_hot = (labels.reshape(row_count)[:, None] == jnp.arange(K)[None, :]).astype(jnp.float32)
    picked = lax.optimization_barrier(jnp.sum(logits * target_hot, axis=1))
    validity = (jnp.arange(TIME_STEPS)[None, :] < lengths[:, None]).astype(jnp.float32)
    row_loss = (log_total - picked).reshape(SITE_TOTAL, TIME_STEPS) * validity
    loss_scale = 1.0 / math.sqrt(SITE_TOTAL * TIME_STEPS)
    class_probs = jnp.exp(logits - log_total[:, None])
    logit_grad = ((class_probs - target_hot) * (validity.reshape(row_count, 1) * loss_scale)).astype(jnp.bfloat16)
    grad_out = jnp.dot(flat_hidden.T, logit_grad, preferred_element_type=jnp.float32)
    gradient = jnp.dot(logit_grad, w_out.T, preferred_element_type=jnp.float32)
    conv_terms = []
    res_terms = []
    for index_of_layer in reversed(range(LAYERS)):
        dilation_step = BASE_DILATION * 2 ** index_of_layer
        joined, tanh_part, sigm_part, gated_out = saved_layers[index_of_layer]
        rounded = gradient.astype(jnp.bfloat16)
        res_terms.append(jnp.dot(gated_out.T, rounded, preferred_element_type=jnp.float32))
        gated_grad = jnp.dot(rounded, w_res[index_of_layer].T, preferred_element_type=jnp.float32)
        filter_grad = gated_grad * sigm_part * (1.0 - tanh_part * tanh_part)
        gate_grad = gated_grad * tanh_part * sigm_part * (1.0 - sigm_part)
        preact_grad = jnp.concatenate([filter_grad, gate_grad], axis=1).astype(jnp.bfloat16)
        conv_terms.append(jnp.dot(joined.T, preact_grad, preferred_element_type=jnp.float32))
        joined_grad = jnp.dot(preact_grad, w_conv[index_of_layer].T, preferred_element_type=jnp.float32)
        past_grad = joined_grad[:, :C].reshape(SITE_TOTAL, TIME_STEPS, C)
        advanced = jnp.pad(past_grad, ((0, 0), (0, dilation_step), (0, 0)))[:, dilation_step:]
        gradient = gradient + joined_grad[:, C:] + advanced.reshape(row_count, C)
    grad_in = jnp.dot(flat_normed.T, gradient.astype(jnp.bfloat16), preferred_element_type=jnp.float32)
    grad_conv = jnp.stack(conv_terms[::-1])
    grad_res = jnp.stack(res_terms[::-1])
    return (row_loss, grad_conv, grad_res, grad_in, grad_out)
```

```python
import functools
import math

import jax
import jax.numpy as jnp
from jax import lax
from jax.experimental import pallas as pl
from jax.experimental.pallas import tpu as pltpu
from jax.sharding import PartitionSpec as P

BASE_DILATION = 256
LEVEL_FLOOR = 0.1
F32 = jnp.float32
BF16 = jnp.bfloat16
TILE = 256
VMEM_LIMIT = 56 * 1024 * 1024
PARAMS = pltpu.CompilerParams(vmem_limit_bytes=VMEM_LIMIT)
WHOLE = pl.BlockSpec(memory_space=pltpu.VMEM)


def dot(a, b):
    return lax.dot_general(a, b, (((1,), (0,)), ((), ())), preferred_element_type=F32)


def dot_t(a, b):
    return lax.dot_general(a, b, (((1,), (1,)), ((), ())), preferred_element_type=F32)


def t_dot(a, b):
    return lax.dot_general(a, b, (((0,), (0,)), ((), ())), preferred_element_type=F32)


def call(kernel, outs, scratch, flops, *args):
    moved = sum(a.size * a.dtype.itemsize for a in args)
    moved += sum(math.prod(s) * jnp.dtype(d).itemsize for s, d in outs)
    return pl.pallas_call(
        kernel,
        out_shape=[jax.ShapeDtypeStruct(s, d) for s, d in outs],
        in_specs=[WHOLE] * len(args),
        out_specs=[WHOLE] * len(outs),
        scratch_shapes=scratch,
        compiler_params=PARAMS,
        cost_estimate=pl.CostEstimate(flops=flops, bytes_accessed=moved, transcendentals=0),
    )(*args)


def scan_kernel(feat_ref, forget_ref, keep_ref, mass_ref, weight_ref, sum_ref):
    feat, forget = feat_ref[...], forget_ref[...]
    rows = feat.shape[0]
    keep, mass, weight = 1.0 - forget, forget * (feat * feat), forget
    row = lax.broadcasted_iota(jnp.int32, feat.shape, 0)
    step = 1
    while step < rows:
        inside = row >= step
        before = jnp.where(inside, pltpu.roll(mass, step, 0), 0.0)
        mass = keep * before + mass
        before = jnp.where(inside, pltpu.roll(weight, step, 0), 0.0)
        weight = keep * before + weight
        keep = keep * jnp.where(inside, pltpu.roll(keep, step, 0), 1.0)
        step *= 2
    keep_ref[...], mass_ref[...], weight_ref[...] = keep, mass, weight
    sum_ref[0:1, :] = keep[rows - 1 :]
    sum_ref[1:2, :] = mass[rows - 1 :]
    sum_ref[2:3, :] = weight[rows - 1 :]


def norm_kernel(feat_ref, keep_ref, mass_ref, weight_ref, carry_ref, out_ref):
    keep = keep_ref[...]
    mass = keep * carry_ref[1:2, :] + mass_ref[...]
    weight = keep * carry_ref[2:3, :] + weight_ref[...]
    out_ref[...] = (feat_ref[...] / jnp.sqrt(mass / weight + LEVEL_FLOOR)).astype(BF16)


def compose(earlier, later):
    keep = later[0:1] * earlier[0:1]
    rest = later[0:1] * earlier[1:3] + later[1:3]
    return jnp.concatenate([keep, rest], axis=0)


def forward_first(before, kept, norm_ref, w_in_ref, filt_ref, gate_ref, res_ref,
                  h0_ref, h1_ref, tanh_ref, sigm_ref):
    rows, c = h0_ref.shape
    d = rows - h1_ref.shape[0]

    def enter(i, _):
        at = pl.ds(pl.multiple_of(i * TILE, TILE), TILE)
        h0_ref[at, :] = dot(norm_ref[at, :], w_in_ref[...]).astype(BF16)
        return 0

    lax.fori_loop(0, rows // TILE, enter, 0)

    def tile(i):
        past = h0_ref[pl.ds(pl.multiple_of(i * TILE, TILE), TILE), :]
        now = h0_ref[pl.ds(pl.multiple_of(i * TILE + d, TILE), TILE), :]
        filt = dot(past, filt_ref[:c, :]) + dot(now, filt_ref[c:, :])
        gate = dot(past, gate_ref[:c, :]) + dot(now, gate_ref[c:, :])
        t, s = jnp.tanh(filt), 0.5 + 0.5 * jnp.tanh(0.5 * gate)
        out = now.astype(F32) + dot((t * s).astype(BF16), res_ref[...])
        h1_ref[pl.ds(pl.multiple_of(i * TILE, TILE), TILE), :] = out.astype(BF16)
        return t, s

    def plain(i, _):
        tile(i)
        return 0

    def saving(i, _):
        t, s = tile(i)
        at = pl.ds(pl.multiple_of(i * TILE - before, TILE), TILE)
        tanh_ref[at, :], sigm_ref[at, :] = t, s
        return 0

    lax.fori_loop(0, before // TILE, plain, 0)
    lax.fori_loop(before // TILE, (before + kept) // TILE, saving, 0)
    lax.fori_loop((before + kept) // TILE, h1_ref.shape[0] // TILE, plain, 0)


def second_kernel(steps, scale, h1_ref, filt_ref, gate_ref, res_ref, w_out_ref, label_ref, valid_ref,
                  loss_ref, cf_ref, cg_ref, cr_ref, co_ref, pf_ref, pg_ref, grad_ref,
                  gated_ref, h2_ref, lgrad_ref, round_ref):
    rows, c = pf_ref.shape
    d = h1_ref.shape[0] - rows
    classes = w_out_ref.shape[1]

    def tile(i, _):
        at = pl.ds(pl.multiple_of(i * TILE, TILE), TILE)
        past = h1_ref[at, :]
        now = h1_ref[pl.ds(pl.multiple_of(i * TILE + d, TILE), TILE), :]
        filt = dot(past, filt_ref[:c, :]) + dot(now, filt_ref[c:, :])
        gate = dot(past, gate_ref[:c, :]) + dot(now, gate_ref[c:, :])
        t, s = jnp.tanh(filt), 0.5 + 0.5 * jnp.tanh(0.5 * gate)
        gated = (t * s).astype(BF16)
        h2 = (now.astype(F32) + dot(gated, res_ref[...])).astype(BF16)
        logits = dot(h2, w_out_ref[...])
        total = jnp.log(jnp.sum(jnp.exp(logits), axis=1, keepdims=True))
        hot = (label_ref[at, :] == lax.broadcasted_iota(jnp.int32, (TILE, classes), 1)).astype(F32)
        valid = valid_ref[at, :]
        loss_ref[at, :] = (total - jnp.sum(logits * hot, axis=1, keepdims=True)) * valid
        lgrad = ((jnp.exp(logits - total) - hot) * (valid * scale)).astype(BF16)
        grad = dot_t(lgrad, w_out_ref[...])
        rounded = grad.astype(BF16)
        back = dot_t(rounded, res_ref[...])
        pf_ref[at, :] = (back * s * (1.0 - t * t)).astype(BF16)
        pg_ref[at, :] = (back * t * s * (1.0 - s)).astype(BF16)
        grad_ref[at, :] = grad
        gated_ref[at, :] = gated
        h2_ref[at, :] = h2
        lgrad_ref[at, :] = lgrad
        round_ref[at, :] = rounded
        return 0

    lax.fori_loop(0, rows // TILE, tile, 0)
    own = slice(0, steps)

    def conv(i, _):
        at = pl.ds(pl.multiple_of(i * TILE, TILE), TILE)
        low = pl.ds(pl.multiple_of(c + i * TILE, TILE), TILE)
        past, now = h1_ref[0:steps, at], h1_ref[d : d + steps, at]
        cf_ref[at, :] = t_dot(past, pf_ref[own, :]).astype(BF16)
        cg_ref[at, :] = t_dot(past, pg_ref[own, :]).astype(BF16)
        cf_ref[low, :] = t_dot(now, pf_ref[own, :]).astype(BF16)
        cg_ref[low, :] = t_dot(now, pg_ref[own, :]).astype(BF16)
        cr_ref[at, :] = t_dot(gated_ref[own, at], round_ref[own, :]).astype(BF16)
        co_ref[at, :] = t_dot(h2_ref[own, at], lgrad_ref[own, :]).astype(BF16)
        return 0

    lax.fori_loop(0, c // TILE, conv, 0)


def first_back_kernel(steps, start, pf1_ref, pg1_ref, grad2_ref, filt1_ref, gate1_ref,
                      h0_ref, tanh_ref, sigm_ref, norm_ref, filt_ref, gate_ref, res_ref,
                      cf_ref, cg_ref, cr_ref, ci_ref, grad_ref, round_ref, pf_ref, pg_ref):
    rows, c = pf_ref.shape
    d1 = pf1_ref.shape[0] - rows
    d0 = rows - steps

    def tile(i, _):
        at = pl.ds(pl.multiple_of(i * TILE, TILE), TILE)
        later = pl.ds(pl.multiple_of(i * TILE + d1, TILE), TILE)
        grad = grad2_ref[at, :] + dot_t(pf1_ref[at, :], filt1_ref[c:, :]) + dot_t(pg1_ref[at, :], gate1_ref[c:, :])
        grad += dot_t(pf1_ref[later, :], filt1_ref[:c, :]) + dot_t(pg1_ref[later, :], gate1_ref[:c, :])
        rounded = grad.astype(BF16)
        t, s = tanh_ref[at, :], sigm_ref[at, :]
        back = dot_t(rounded, res_ref[...])
        pf_ref[at, :] = (back * s * (1.0 - t * t)).astype(BF16)
        pg_ref[at, :] = (back * t * s * (1.0 - s)).astype(BF16)
        grad_ref[at, :] = grad
        round_ref[at, :] = rounded
        return 0

    lax.fori_loop(0, rows // TILE, tile, 0)
    own = slice(0, steps)

    def conv(i, _):
        at = pl.ds(pl.multiple_of(i * TILE, TILE), TILE)
        low = pl.ds(pl.multiple_of(c + i * TILE, TILE), TILE)
        past, now = h0_ref[start - d0 : start - d0 + steps, at], h0_ref[start : start + steps, at]
        cf_ref[at, :] = t_dot(past, pf_ref[own, :]).astype(BF16)
        cg_ref[at, :] = t_dot(past, pg_ref[own, :]).astype(BF16)
        cf_ref[low, :] = t_dot(now, pf_ref[own, :]).astype(BF16)
        cg_ref[low, :] = t_dot(now, pg_ref[own, :]).astype(BF16)
        gated = (tanh_ref[own, at] * sigm_ref[own, at]).astype(BF16)
        cr_ref[at, :] = t_dot(gated, round_ref[own, :]).astype(BF16)
        return 0

    lax.fori_loop(0, c // TILE, conv, 0)

    def last(i, _):
        at = pl.ds(pl.multiple_of(i * TILE, TILE), TILE)
        later = pl.ds(pl.multiple_of(i * TILE + d0, TILE), TILE)
        grad = grad_ref[at, :] + dot_t(pf_ref[at, :], filt_ref[c:, :]) + dot_t(pg_ref[at, :], gate_ref[c:, :])
        grad += dot_t(pf_ref[later, :], filt_ref[:c, :]) + dot_t(pg_ref[later, :], gate_ref[:c, :])
        round_ref[at, :] = grad.astype(BF16)
        return 0

    lax.fori_loop(0, steps // TILE, last, 0)
    ci_ref[...] = t_dot(norm_ref[start : start + steps, :], round_ref[own, :]).astype(BF16)


def swap(value, axis, bit):
    return lax.ppermute(value, axis, [(i, i ^ (1 << bit)) for i in range(lax.axis_size(axis))])


def my_bit(axis, bit):
    return (lax.axis_index(axis) >> bit) & 1


def stages(flip):
    bits = lax.axis_size("tm").bit_length() - 1
    order = list(range(bits))
    if flip and bits > 1:
        order[0], order[1] = order[1], order[0]
    return [(bits, "site", 0)] + [(bits - 1 - b, "tm", b) for b in order]


def gather(piece, flip):
    bits = lax.axis_size("tm").bit_length() - 1
    held = piece.reshape((1,) * (bits + 1) + piece.shape)
    for dim, axis, bit in reversed(stages(flip)):
        other = swap(held, axis, bit)
        held = jnp.where(
            my_bit(axis, bit) == 0,
            jnp.concatenate([held, other], axis=dim),
            jnp.concatenate([other, held], axis=dim),
        )
    return held.reshape((-1,) + piece.shape)


def scatter_sum(terms, flip):
    bits = lax.axis_size("tm").bit_length() - 1
    held = terms.reshape((2,) * (bits + 1) + terms.shape[1:])
    for dim, axis, bit in stages(flip):
        mine = my_bit(axis, bit)
        other = swap(lax.dynamic_index_in_dim(held, 1 - mine, dim), axis, bit)
        total = lax.dynamic_index_in_dim(held, mine, dim).astype(F32) + other.astype(F32)
        held = total.astype(BF16)
    return total.reshape(terms.shape[1:])


def hop(value, by):
    size = lax.axis_size("tm")
    return lax.ppermute(value, "tm", [(i, i + by) for i in range(size) if 0 <= i + by < size])


def rows_before(value, count):
    steps, parts, by = value.shape[0], [], 1
    while count > 0:
        take = min(count, steps)
        parts.insert(0, hop(value[steps - take :], by))
        count, by = count - take, by + 1
    return parts


def rows_after(value, count):
    steps, parts, by = value.shape[0], [], 1
    while count > 0:
        take = min(count, steps)
        parts.append(hop(value[:take], -by))
        count, by = count - take, by + 1
    return parts


def on_device(features, forget, labels, lengths, w_conv, w_res, w_in, w_out):
    _, steps, bands = features.shape
    time_devices, site_devices = lax.axis_size("tm"), lax.axis_size("site")
    c = w_res.shape[2]
    classes = w_out.shape[1]
    conv_rows, res_rows, in_rows, out_rows = w_conv.shape[1], w_res.shape[1], w_in.shape[0], w_out.shape[0]
    half_res = res_rows // 2
    out_pack = out_rows * classes // c
    d0, d1 = BASE_DILATION, 2 * BASE_DILATION
    reach = d0 + d1
    position = lax.axis_index("tm")

    pieces = []
    for layer in range(2):
        filt = [w_conv[layer, :, :c], w_res[layer, :half_res]]
        gate = [w_conv[layer, :, c:], w_res[layer, half_res:]]
        if layer == 0:
            filt.append(w_in)
        else:
            filt.append(w_out.reshape(out_pack, c))
        pieces.append((jnp.concatenate(filt), jnp.concatenate(gate)))
    weights = []
    for layer in range(2):
        filt, gate = gather(pieces[layer][0], False), gather(pieces[layer][1], True)
        res = jnp.concatenate([filt[:, conv_rows : conv_rows + half_res], gate[:, conv_rows:]], axis=1)
        weights.append((
            filt[:, :conv_rows].reshape(-1, c),
            gate[:, :conv_rows].reshape(-1, c),
            res.reshape(-1, c),
            filt[:, conv_rows + half_res :],
        ))
    filt0, gate0, res0, in_all = weights[0]
    filt1, gate1, res1, out_all = weights[1]
    in_all = in_all.reshape(-1, c)
    out_all = out_all.reshape(-1, classes)

    block = ((steps, bands), F32)
    feat = features[0]
    keep, mass, weight, summary = call(
        scan_kernel, [block] * 3 + [((3, bands), F32)], [], 40 * steps * bands, feat, forget[0])
    neutral = jnp.concatenate([jnp.ones((1, bands), F32), jnp.zeros((2, bands), F32)])
    carry, total = neutral, summary
    for bit in range(time_devices.bit_length() - 1):
        other = swap(total, "tm", bit)
        upper = my_bit("tm", bit) == 1
        carry = jnp.where(upper, compose(other, carry), carry)
        total = jnp.where(upper, compose(other, total), compose(total, other))
    (normed,) = call(norm_kernel, [((steps, bands), BF16)], [], 10 * steps * bands,
                     feat, keep, mass, weight, carry)

    window = jnp.concatenate(rows_before(normed, reach) + [normed] + rows_after(normed, reach))
    labels_here = labels[0][:, None]
    label_window = jnp.concatenate([labels_here] + rows_after(labels_here, reach))
    at = position * steps + lax.broadcasted_iota(jnp.int32, (steps + reach, 1), 0)
    valid = (at < lengths[0]).astype(F32)

    total_rows = steps + 2 * reach
    h0, h1, tanh0, sigm0 = call(
        functools.partial(forward_first, d1, steps + d0),
        [((total_rows, c), BF16), ((total_rows - d0, c), BF16), ((steps + d0, c), F32), ((steps + d0, c), F32)],
        [], 2 * total_rows * c * (bands + 5 * c), window, in_all, filt0, gate0, res0)

    scale = 1.0 / math.sqrt(site_devices * steps * time_devices)
    rows1 = steps + reach
    loss, cf1, cg1, cr1, co, pf1, pg1, grad2 = call(
        functools.partial(second_kernel, steps, scale),
        [((rows1, 1), F32), ((2 * c, c), BF16), ((2 * c, c), BF16), ((c, c), BF16), ((c, classes), BF16),
         ((rows1, c), BF16), ((rows1, c), BF16), ((rows1, c), F32)],
        [pltpu.VMEM((rows1, c), BF16), pltpu.VMEM((rows1, c), BF16),
         pltpu.VMEM((rows1, classes), BF16), pltpu.VMEM((rows1, c), BF16)],
        2 * rows1 * c * 6 * c + 2 * steps * 5 * c * c,
        h1, filt1, gate1, res1, out_all, label_window, valid)

    rows0 = steps + d0
    cf0, cg0, cr0, ci = call(
        functools.partial(first_back_kernel, steps, reach),
        [((2 * c, c), BF16), ((2 * c, c), BF16), ((c, c), BF16), ((bands, c), BF16)],
        [pltpu.VMEM((rows0, c), F32), pltpu.VMEM((rows0, c), BF16),
         pltpu.VMEM((rows0, c), BF16), pltpu.VMEM((rows0, c), BF16)],
        2 * rows0 * c * 5 * c + 2 * steps * 9 * c * c,
        pf1, pg1, grad2, filt1, gate1, h0, tanh0, sigm0, window, filt0, gate0, res0)

    devices = time_devices * site_devices
    grads = []
    for cf, cg, cr, extra in ((cf1, cg1, cr1, co), (cf0, cg0, cr0, ci)):
        cr = cr.reshape(devices, res_rows, c)
        filt = jnp.concatenate(
            [cf.reshape(devices, conv_rows, c), cr[:, :half_res], extra.reshape(devices, -1, c)], axis=1)
        gate = jnp.concatenate([cg.reshape(devices, conv_rows, c), cr[:, half_res:]], axis=1)
        filt, gate = scatter_sum(filt, False), scatter_sum(gate, True)
        grads.append((
            jnp.concatenate([filt[:conv_rows], gate[:conv_rows]], axis=1),
            jnp.concatenate([filt[conv_rows : conv_rows + half_res], gate[conv_rows:]]),
            filt[conv_rows + half_res :],
        ))
    (conv1, res1, grad_out), (conv0, res0, grad_in) = grads
    return (
        loss[:steps, 0][None],
        jnp.stack([conv0, conv1]),
        jnp.stack([res0, res1]),
        grad_in,
        grad_out.reshape(out_rows, classes),
    )


def solution(mesh):
    return jax.shard_map(
        on_device,
        mesh=mesh,
        in_specs=(
            P(("groups", "site"), "tm", None),
            P(("groups", "site"), "tm", None),
            P(("groups", "site"), "tm"),
            P(("groups", "site")),
            P(None, ("tm", "site"), None),
            P(None, ("tm", "site"), None),
            P(("tm", "site"), None),
            P(("tm", "site"), None),
        ),
        out_specs=(
            P(("groups", "site"), "tm"),
            P("groups", ("tm", "site"), None),
            P("groups", ("tm", "site"), None),
            P(("tm", "site"), "groups"),
            P(("tm", "site"), "groups"),
        ),
        check_vma=False,
    )
```

```python
import functools
import math

import jax
import jax.numpy as jnp
from jax import lax
from jax.experimental import pallas as pl
from jax.experimental.pallas import tpu as pltpu
from jax.sharding import PartitionSpec as P

BASE_DILATION = 256
LEVEL_FLOOR = 0.1
F32 = jnp.float32
BF16 = jnp.bfloat16
TILE = 256
VMEM_LIMIT = 56 * 1024 * 1024
PARAMS = pltpu.CompilerParams(vmem_limit_bytes=VMEM_LIMIT)
WHOLE = pl.BlockSpec(memory_space=pltpu.VMEM)
SCALAR = pl.BlockSpec(memory_space=pltpu.SMEM)


def dot(a, b):
    return lax.dot_general(a, b, (((1,), (0,)), ((), ())), preferred_element_type=F32)


def dot_t(a, b):
    return lax.dot_general(a, b, (((1,), (1,)), ((), ())), preferred_element_type=F32)


def t_dot(a, b):
    return lax.dot_general(a, b, (((0,), (0,)), ((), ())), preferred_element_type=F32)


def call(kernel, outs, scratch, flops, *args):
    moved = sum(a.size * a.dtype.itemsize for a in args)
    moved += sum(math.prod(s) * jnp.dtype(d).itemsize for s, d in outs)
    return pl.pallas_call(
        kernel,
        out_shape=[jax.ShapeDtypeStruct(s, d) for s, d in outs],
        in_specs=[SCALAR if a.dtype == jnp.int32 and a.shape == (1,) else WHOLE for a in args],
        out_specs=[WHOLE] * len(outs),
        scratch_shapes=scratch,
        compiler_params=PARAMS,
        cost_estimate=pl.CostEstimate(flops=flops, bytes_accessed=moved, transcendentals=0),
    )(*args)


def scan_kernel(feat_ref, forget_ref, keep_ref, mass_ref, weight_ref, sum_ref):
    feat, forget = feat_ref[...], forget_ref[...]
    rows = feat.shape[0]
    keep, mass, weight = 1.0 - forget, forget * (feat * feat), forget
    row = lax.broadcasted_iota(jnp.int32, feat.shape, 0)
    step = 1
    while step < rows:
        inside = row >= step
        before = jnp.where(inside, pltpu.roll(mass, step, 0), 0.0)
        mass = keep * before + mass
        before = jnp.where(inside, pltpu.roll(weight, step, 0), 0.0)
        weight = keep * before + weight
        keep = keep * jnp.where(inside, pltpu.roll(keep, step, 0), 1.0)
        step *= 2
    keep_ref[...], mass_ref[...], weight_ref[...] = keep, mass, weight
    sum_ref[0:1, :] = keep[rows - 1 :]
    sum_ref[1:2, :] = mass[rows - 1 :]
    sum_ref[2:3, :] = weight[rows - 1 :]


def norm_kernel(feat_ref, keep_ref, mass_ref, weight_ref, carry_ref, out_ref):
    keep = keep_ref[...]
    mass = keep * carry_ref[1:2, :] + mass_ref[...]
    weight = keep * carry_ref[2:3, :] + weight_ref[...]
    out_ref[...] = (feat_ref[...] / jnp.sqrt(mass / weight + LEVEL_FLOOR)).astype(BF16)


def compose(earlier, later):
    keep = later[0:1] * earlier[0:1]
    rest = later[0:1] * earlier[1:3] + later[1:3]
    return jnp.concatenate([keep, rest], axis=0)


def rows_of(ref, part=None):
    half = ref.shape[0] // 2
    value = ref[...] if part is None else ref[part * half : (part + 1) * half]
    return value.reshape(-1, value.shape[-1]).astype(BF16)


def place(site_ref, copies):
    mine = site_ref[0]

    def body(tm, _):
        for target, row, own, other, half, at, count in copies:
            target[2 * tm + mine, row : row + count, :] = own[tm, half, at : at + count, :]
            target[2 * tm + 1 - mine, row : row + count, :] = other[tm, half, at : at + count, :]
        return 0

    lax.fori_loop(0, copies[0][2].shape[0], body, 0)


def activate(past, now, filt_ref, gate_ref):
    joined = jnp.concatenate([past, now], axis=1)
    t = jnp.tanh(dot(joined, rows_of(filt_ref)))
    s = 0.5 + 0.5 * jnp.tanh(0.5 * dot(joined, rows_of(gate_ref)))
    return t, s


def tile_at(i, offset=0):
    return pl.ds(pl.multiple_of(i * TILE + offset, TILE), TILE)


def forward_first(before, site_ref, norm_ref, w_in_ref, a_ref, a2_ref, b_ref, b2_ref, c_ref, c2_ref,
                  h0_ref, h1_ref, tanh_ref, sigm_ref, filt_ref, gate_ref, res_ref):
    rows, c = h0_ref.shape
    kept = tanh_ref.shape[0]
    d = rows - h1_ref.shape[0]
    n, r = a_ref.shape[2], res_ref.shape[1] // 2
    place(site_ref, [
        (filt_ref, 0, a_ref, a2_ref, 0, 0, n), (gate_ref, 0, a_ref, a2_ref, 1, 0, n),
        (filt_ref, n, b_ref, b2_ref, 0, 0, n), (gate_ref, n, b_ref, b2_ref, 1, 0, n),
        (res_ref, 0, c_ref, c2_ref, 0, 0, r), (res_ref, r, c_ref, c2_ref, 1, 0, r)])

    def enter(i, _):
        h0_ref[tile_at(i), :] = dot(norm_ref[tile_at(i), :], w_in_ref[...]).astype(BF16)
        return 0

    lax.fori_loop(0, rows // TILE, enter, 0)

    def tile(i):
        now = h0_ref[tile_at(i, d), :]
        t, s = activate(h0_ref[tile_at(i), :], now, filt_ref, gate_ref)
        out = now.astype(F32) + dot((t * s).astype(BF16), rows_of(res_ref))
        h1_ref[tile_at(i), :] = out.astype(BF16)
        return t, s

    def plain(i, _):
        tile(i)
        return 0

    def saving(i, _):
        t, s = tile(i)
        tanh_ref[tile_at(i, -before), :], sigm_ref[tile_at(i, -before), :] = t, s
        return 0

    lax.fori_loop(0, before // TILE, plain, 0)
    lax.fori_loop(before // TILE, (before + kept) // TILE, saving, 0)
    lax.fori_loop((before + kept) // TILE, h1_ref.shape[0] // TILE, plain, 0)


def store_terms(site_ref, keep_ref, send_ref, row, value, first, size, start, count, lane=0):
    mine = site_ref[0] == 0
    at = (slice(row, row + count), slice(lane, lane + value.shape[1]))
    for k in range(value.shape[0] // (2 * size)):
        low = value[2 * k * size + start : 2 * k * size + start + count]
        high = value[(2 * k + 1) * size + start : (2 * k + 1) * size + start + count]
        keep_ref[(first + k,) + at] = jnp.where(mine, low, high).astype(keep_ref.dtype)
        send_ref[(first + k,) + at] = jnp.where(mine, high, low).astype(send_ref.dtype)


def conv_terms(site_ref, keep_ref, send_ref, first, size, res, value):
    c = value.shape[1] // 2
    store_terms(site_ref, keep_ref, send_ref, 0, value[:, c:], first, size, 0, size)
    store_terms(site_ref, keep_ref, send_ref, size + res, value[:, :c], first, size, 0, size)


def res_terms(site_ref, keep_ref, send_ref, first, conv, size, value):
    half = size // 2
    store_terms(site_ref, keep_ref, send_ref, conv, value, first, size, half, half)
    store_terms(site_ref, keep_ref, send_ref, 2 * conv + half, value, first, size, 0, half)


def second_kernel(steps, scale, sizes, site_ref, h1_ref, w_out_ref, label_ref, valid_ref,
                  a_ref, a2_ref, b_ref, b2_ref, c_ref, c2_ref,
                  loss_ref, keep_ref, send_ref, back_ref, grad_ref, filt_ref, gate_ref,
                  res_ref, gated_ref, h2_ref, lgrad_ref, round_ref):
    rows, c = grad_ref.shape
    d = h1_ref.shape[0] - rows
    classes = w_out_ref.shape[1]
    conv, res, _, out = sizes
    n, r = conv // 2, res // 2
    place(site_ref, [
        (res_ref, 0, a_ref, a2_ref, 0, 0, r), (res_ref, r, a_ref, a2_ref, 1, 0, r),
        (filt_ref, 0, b_ref, b2_ref, 0, 0, n), (gate_ref, 0, b_ref, b2_ref, 1, 0, n),
        (filt_ref, n, c_ref, c2_ref, 0, 0, n), (gate_ref, n, c_ref, c2_ref, 1, 0, n)])

    def tile(i, _):
        at = tile_at(i)
        now = h1_ref[tile_at(i, d), :]
        t, s = activate(h1_ref[at, :], now, filt_ref, gate_ref)
        gated = (t * s).astype(BF16)
        h2 = (now.astype(F32) + dot(gated, rows_of(res_ref))).astype(BF16)
        logits = dot(h2, w_out_ref[...])
        total = jnp.log(jnp.sum(jnp.exp(logits), axis=1, keepdims=True))
        hot = (label_ref[at, :] == lax.broadcasted_iota(jnp.int32, (TILE, classes), 1)).astype(F32)
        valid = valid_ref[at, :]
        loss_ref[at, :] = (total - jnp.sum(logits * hot, axis=1, keepdims=True)) * valid
        lgrad = ((jnp.exp(logits - total) - hot) * (valid * scale)).astype(BF16)
        grad = dot_t(lgrad, w_out_ref[...])
        rounded = grad.astype(BF16)
        back = dot_t(rounded, rows_of(res_ref))
        back_ref[at, :c] = (back * s * (1.0 - t * t)).astype(BF16)
        back_ref[at, c:] = (back * t * s * (1.0 - s)).astype(BF16)
        grad_ref[at, :] = grad
        gated_ref[at, :] = gated
        h2_ref[at, :] = h2
        lgrad_ref[at, :] = lgrad
        round_ref[at, :] = rounded
        return 0

    lax.fori_loop(0, rows // TILE, tile, 0)
    own = slice(0, steps)
    targets = (site_ref, keep_ref, send_ref)

    def terms(i, _):
        at = tile_at(i)
        first = i * (TILE // (2 * conv))
        conv_terms(*targets, first, conv, r, t_dot(h1_ref[0:steps, at], back_ref[own, :]))
        conv_terms(*targets, first + c // (2 * conv), conv, r, t_dot(h1_ref[d : d + steps, at], back_ref[own, :]))
        res_terms(*targets, i * (TILE // (2 * res)), conv, res, t_dot(gated_ref[own, at], round_ref[own, :]))
        value = t_dot(h2_ref[own, at], lgrad_ref[own, :])
        count = out * classes // c
        for q in range(c // classes):
            store_terms(*targets, 2 * conv + res, value, i * (TILE // (2 * out)), out, q * count, count, q * classes)
        return 0

    lax.fori_loop(0, c // TILE, terms, 0)


def grad_first(back1_ref, grad2_ref, filt1_ref, gate1_ref, tanh_ref, sigm_ref, res_ref,
               grad_ref, round_ref, back_ref):
    rows, c = grad_ref.shape
    d1 = back1_ref.shape[0] - rows

    def tile(i, _):
        at, later = tile_at(i), tile_at(i, d1)
        grad = grad2_ref[at, :] + dot_t(back1_ref[at, :c], rows_of(filt1_ref, 1))
        grad += dot_t(back1_ref[at, c:], rows_of(gate1_ref, 1))
        grad += dot_t(back1_ref[later, :c], rows_of(filt1_ref, 0))
        grad += dot_t(back1_ref[later, c:], rows_of(gate1_ref, 0))
        rounded = grad.astype(BF16)
        t, s = tanh_ref[at, :], sigm_ref[at, :]
        back = dot_t(rounded, rows_of(res_ref))
        back_ref[at, :c] = (back * s * (1.0 - t * t)).astype(BF16)
        back_ref[at, c:] = (back * t * s * (1.0 - s)).astype(BF16)
        grad_ref[at, :] = grad
        round_ref[at, :] = rounded
        return 0

    lax.fori_loop(0, rows // TILE, tile, 0)


def terms_first(steps, start, sizes, site_ref, back_ref, grad_ref, round_ref, h0_ref, tanh_ref, sigm_ref,
                norm_ref, filt_ref, gate_ref, keep_ref, send_ref, last_ref):
    rows, c = grad_ref.shape
    d0 = rows - steps
    conv, res, enter, _ = sizes
    own = slice(0, steps)
    targets = (site_ref, keep_ref, send_ref)

    def terms(i, _):
        at = tile_at(i)
        first = i * (TILE // (2 * conv))
        past, now = h0_ref[start - d0 : start - d0 + steps, at], h0_ref[start : start + steps, at]
        conv_terms(*targets, first, conv, res // 2, t_dot(past, back_ref[own, :]))
        conv_terms(*targets, first + c // (2 * conv), conv, res // 2, t_dot(now, back_ref[own, :]))
        gated = (tanh_ref[own, at] * sigm_ref[own, at]).astype(BF16)
        res_terms(*targets, i * (TILE // (2 * res)), conv, res, t_dot(gated, round_ref[own, :]))
        return 0

    lax.fori_loop(0, c // TILE, terms, 0)

    def last(i, _):
        at, later = tile_at(i), tile_at(i, d0)
        grad = grad_ref[at, :] + dot_t(back_ref[at, :c], rows_of(filt_ref, 1))
        grad += dot_t(back_ref[at, c:], rows_of(gate_ref, 1))
        grad += dot_t(back_ref[later, :c], rows_of(filt_ref, 0))
        grad += dot_t(back_ref[later, c:], rows_of(gate_ref, 0))
        last_ref[at, :] = grad.astype(BF16)
        return 0

    lax.fori_loop(0, steps // TILE, last, 0)
    value = t_dot(norm_ref[start : start + steps, :], last_ref[...])
    store_terms(*targets, 2 * conv + res, value, 0, enter, 0, enter)


NEAR, FAR, ACROSS = ("tm", 0), ("tm", 1), ("groups", 0)


def swap(value, link):
    axis, bit = link
    return lax.ppermute(value, axis, [(i, i ^ (1 << bit)) for i in range(lax.axis_size(axis))])


def my_bit(link):
    return (lax.axis_index(link[0]) >> link[1]) & 1


def time_bits():
    return lax.axis_size("tm").bit_length() - 1


def dim_of(link):
    return time_bits() if link == ACROSS else time_bits() - 1 - link[1]


def join(held, other, link):
    dim = dim_of(link)
    return jnp.where(
        my_bit(link) == 0,
        jnp.concatenate([held, other], axis=dim),
        jnp.concatenate([other, held], axis=dim),
    )


def together(*values):
    return lax.optimization_barrier(values)


def sum_step(held, link):
    dim, mine = dim_of(link), my_bit(link)
    other = swap(lax.dynamic_index_in_dim(held, 1 - mine, dim), link)
    return lax.dynamic_index_in_dim(held, mine, dim).astype(F32) + other.astype(F32)


def sum_rest(held, gate_rows):
    shape = held.shape[1:]
    held = held.reshape((2,) * time_bits() + shape)
    gate, filt = held[..., :gate_rows, :], held[..., gate_rows:, :]
    filt, gate = sum_step(filt, NEAR).astype(BF16), sum_step(gate, FAR).astype(BF16)
    filt, gate = sum_step(filt, FAR).astype(BF16), sum_step(gate, NEAR).astype(BF16)
    held = jnp.concatenate([gate, filt], axis=-2)
    for bit in range(2, time_bits()):
        total = sum_step(held, ("tm", bit))
        held = total.astype(BF16)
    return total.reshape(shape)


def hop(value, by):
    size = lax.axis_size("tm")
    return lax.ppermute(value, "tm", [(i, i + by) for i in range(size) if 0 <= i + by < size])


def rows_before(value, count):
    steps, parts, by = value.shape[0], [], 1
    while count > 0:
        take = min(count, steps)
        parts.insert(0, hop(value[steps - take :], by))
        count, by = count - take, by + 1
    return parts


def rows_after(value, count):
    steps, parts, by = value.shape[0], [], 1
    while count > 0:
        take = min(count, steps)
        parts.append(hop(value[:take], -by))
        count, by = count - take, by + 1
    return parts


def on_device(features, forget, labels, lengths, w_conv, w_res, w_in, w_out):
    _, steps, bands = features.shape
    time_devices, site_devices = lax.axis_size("tm"), lax.axis_size("site")
    devices = time_devices * site_devices
    c = w_res.shape[2]
    classes = w_out.shape[1]
    conv, res, enter, out = sizes = (w_conv.shape[1], w_res.shape[1], w_in.shape[0], w_out.shape[0])
    half, extra = res // 2, out * classes // c
    aligned = conv % 32 == 0 and res % 32 == 0
    kind = BF16 if aligned else F32
    d0, d1 = BASE_DILATION, 2 * BASE_DILATION
    reach = d0 + d1
    position, site = lax.axis_index("tm"), lax.axis_index("site")
    site_arg = site.astype(jnp.int32)[None]
    core = ("site", 0)

    def own_half(across):
        cols = slice(across * c, (across + 1) * c)
        part = slice(across * half, (across + 1) * half)
        more = w_in if across == 0 else w_out.reshape(extra, c)
        first, second = w_conv[0, :, cols], w_conv[1, :, cols]
        n = conv // 2
        return jnp.concatenate([
            first[:n], w_res[1, part], first[n:], second[:n], w_res[0, part], more, second[n:]])

    n = conv // 2
    cuts = [n, half, n, n, half + enter, n]
    held = jnp.where(my_bit(ACROSS) == 0, own_half(0), own_half(1))
    held = held.reshape((1,) * (time_bits() + 1) + held.shape)

    block = ((steps, bands), F32)
    feat = features[0]
    keep, mass, weight, summary = call(
        scan_kernel, [block] * 3 + [((3, bands), F32)], [], 40 * steps * bands, feat, forget[0])
    labels_here = labels[0][:, None]
    label_window = jnp.concatenate([labels_here] + rows_after(labels_here, reach))
    for bit in reversed(range(2, time_bits())):
        held = join(held, swap(held, ("tm", bit)), ("tm", bit))
    carry = jnp.concatenate([jnp.ones((1, bands), F32), jnp.zeros((2, bands), F32)])
    total = summary

    def carry_step(carry, total, bit):
        other = swap(total, ("tm", bit))
        upper = my_bit(("tm", bit)) == 1
        carry = jnp.where(upper, compose(other, carry), carry)
        return carry, jnp.where(upper, compose(other, total), compose(total, other))

    orders = [(FAR, NEAR, ACROSS), (NEAR, ACROSS, FAR), (ACROSS, FAR, NEAR)]
    bounds = [0, cuts[0] + cuts[1], sum(cuts[:4]), sum(cuts)]
    pieces = [held[..., bounds[k] : bounds[k + 1], :] for k in range(3)]
    bits = list(range(time_bits()))
    for step in range(2):
        take = bits if step == 1 else bits[:1]
        bits = bits[len(take):]
        *pieces, carry, total = together(*pieces, carry, total)
        pieces = [join(p, swap(p, order[step]), order[step]) for p, order in zip(pieces, orders)]
        for bit in take:
            carry, total = carry_step(carry, total, bit)
    (normed,) = call(norm_kernel, [((steps, bands), BF16)], [], 10 * steps * bands,
                     feat, keep, mass, weight, carry)
    *pieces, normed = together(*pieces, normed)
    layers = [[p[..., :cut, :] for p, cut in zip(pieces, cuts[::2])],
              [p[..., cut:, :] for p, cut in zip(pieces, cuts[::2])]]
    first = [join(p, swap(p, order[2]), order[2]) for p, order in zip(layers[0], orders)]
    window = jnp.concatenate(rows_before(normed, reach) + [normed] + rows_after(normed, reach))
    *rest, window = together(*first, *layers[1], window)
    first, second = rest[:3], rest[3:]
    second = [join(p, swap(p, order[2]), order[2]) for p, order in zip(second, orders)]

    def both_cores(parts):
        parts = [p.reshape((time_devices, 2) + p.shape[-2:]) for p in parts]
        pairs = [(p, swap(p, core)) for p in parts]
        return pairs

    def kernel_args(pairs):
        return [v.astype(kind) for pair in pairs for v in pair]

    first = both_cores(first)
    own, other = (v[:, :, half:] for v in first[2])
    extras = jnp.where(site == 0, jnp.stack([own, other], axis=1), jnp.stack([other, own], axis=1))
    in_all = extras[:, :, 0].reshape(-1, c)
    out_all = extras[:, :, 1].reshape(-1, classes)

    at = position * steps + lax.broadcasted_iota(jnp.int32, (steps + reach, 1), 0)
    valid = (at < lengths[0]).astype(F32)

    total_rows, rows0, rows1 = steps + 2 * reach, steps + d0, steps + reach
    conv_all, res_all = ((devices, conv, c), kind), ((devices, res, c), kind)
    h0, h1, tanh0, sigm0, filt0, gate0, res0 = call(
        functools.partial(forward_first, d1),
        [((total_rows, c), BF16), ((total_rows - d0, c), BF16), ((rows0, c), F32), ((rows0, c), F32),
         conv_all, conv_all, res_all],
        [], 2 * total_rows * c * (bands + 5 * c), site_arg, window, in_all, *kernel_args(first))

    second = both_cores(second)
    scale = 1.0 / math.sqrt(site_devices * steps * time_devices)
    package = [((time_devices, 2 * conv + res + extra, c), kind)] * 2
    loss, keep1, send1, back1, grad2, filt1, gate1 = call(
        functools.partial(second_kernel, steps, scale, sizes),
        [((rows1, 1), F32)] + package + [((rows1, 2 * c), BF16), ((rows1, c), F32), conv_all, conv_all],
        [pltpu.VMEM((devices, res, c), kind), pltpu.VMEM((rows1, c), BF16), pltpu.VMEM((rows1, c), BF16),
         pltpu.VMEM((rows1, classes), BF16), pltpu.VMEM((rows1, c), BF16)],
        2 * rows1 * c * 6 * c + 2 * steps * 5 * c * c,
        site_arg, h1, out_all, label_window, valid, *kernel_args(second))

    sum1 = (keep1.astype(F32) + swap(send1.astype(BF16), core).astype(F32)).astype(BF16)
    grad1, round0, back0 = call(
        grad_first, [((rows0, c), F32), ((rows0, c), BF16), ((rows0, 2 * c), BF16)], [],
        2 * rows0 * c * 5 * c, back1, grad2, filt1, gate1, tanh0, sigm0, res0)
    sum1, back0 = together(sum1, back0)
    keep0, send0 = call(
        functools.partial(terms_first, steps, reach, sizes), package, [pltpu.VMEM((steps, c), BF16)],
        2 * steps * 9 * c * c,
        site_arg, back0, grad1, round0, h0, tanh0, sigm0, window, filt0, gate0)
    sum0 = (keep0.astype(F32) + swap(send0.astype(BF16), core).astype(F32)).astype(BF16)

    grads = []
    for held in (sum0, sum1):
        total = sum_rest(held, conv + half)
        gate, filt = total[: conv + half], total[conv + half :]
        grads.append((
            jnp.concatenate([filt[:conv], gate[:conv]], axis=1),
            jnp.concatenate([filt[conv : conv + half], gate[conv:]]),
            filt[conv + half :],
        ))
    (conv0, res0, grad_in), (conv1, res1, grad_out) = grads
    return (
        loss[:steps, 0][None],
        jnp.stack([conv0, conv1]),
        jnp.stack([res0, res1]),
        grad_in,
        unpack_out(grad_out, classes),
    )


def unpack_out(value, classes):
    q = value.shape[1] // classes
    return jnp.concatenate([value[:, k * classes : (k + 1) * classes] for k in range(q)])


def solution(mesh):
    return jax.shard_map(
        on_device,
        mesh=mesh,
        in_specs=(
            P(("groups", "site"), "tm", None),
            P(("groups", "site"), "tm", None),
            P(("groups", "site"), "tm"),
            P(("groups", "site")),
            P(None, ("tm", "site"), None),
            P(None, ("tm", "site"), None),
            P(("tm", "site"), None),
            P(("tm", "site"), None),
        ),
        out_specs=(
            P(("groups", "site"), "tm"),
            P("groups", ("tm", "site"), None),
            P("groups", ("tm", "site"), None),
            P(("tm", "site"), "groups"),
            P(("tm", "site"), "groups"),
        ),
        check_vma=False,
    )
```

```python
import functools
import math

import jax
import jax.numpy as jnp
from jax import lax
from jax.experimental import pallas as pl
from jax.experimental.pallas import tpu as pltpu
from jax.sharding import PartitionSpec as P

BASE_DILATION = 256
LEVEL_FLOOR = 0.1
F32 = jnp.float32
BF16 = jnp.bfloat16
TILE = 256
VMEM_LIMIT = 20 * 1024 * 1024
PARAMS = pltpu.CompilerParams(vmem_limit_bytes=VMEM_LIMIT)
WHOLE = pl.BlockSpec(memory_space=pltpu.VMEM)
SCALAR = pl.BlockSpec(memory_space=pltpu.SMEM)


def dot(a, b):
    return lax.dot_general(a, b, (((1,), (0,)), ((), ())), preferred_element_type=F32)


def dot_t(a, b):
    return lax.dot_general(a, b, (((1,), (1,)), ((), ())), preferred_element_type=F32)


def t_dot(a, b):
    return lax.dot_general(a, b, (((0,), (0,)), ((), ())), preferred_element_type=F32)


def call(kernel, outs, scratch, flops, *args):
    moved = sum(a.size * a.dtype.itemsize for a in args)
    moved += sum(math.prod(s) * jnp.dtype(d).itemsize for s, d in outs)
    return pl.pallas_call(
        kernel,
        out_shape=[jax.ShapeDtypeStruct(s, d) for s, d in outs],
        in_specs=[SCALAR if a.dtype == jnp.int32 and a.ndim == 1 else WHOLE for a in args],
        out_specs=[WHOLE] * len(outs),
        scratch_shapes=scratch,
        compiler_params=PARAMS,
        cost_estimate=pl.CostEstimate(flops=flops, bytes_accessed=moved, transcendentals=0),
    )(*args)


CARRY_ROWS = 8
LABEL_ROWS = 16


def scan(feat, forget):
    rows = feat.shape[0]
    keep, mass, weight = 1.0 - forget, forget * (feat * feat), forget
    row = lax.broadcasted_iota(jnp.int32, feat.shape, 0)
    step = 1
    while step < rows:
        inside = row >= step
        before = jnp.where(inside, pltpu.roll(mass, step, 0), 0.0)
        mass = keep * before + mass
        before = jnp.where(inside, pltpu.roll(weight, step, 0), 0.0)
        weight = keep * before + weight
        keep = keep * jnp.where(inside, pltpu.roll(keep, step, 0), 1.0)
        step *= 2
    return keep, mass, weight


def scan_kernel(feat_ref, forget_ref, keep_ref, mass_ref, weight_ref, carry_ref):
    rows, bands = feat_ref.shape
    values = scan(feat_ref[...], forget_ref[...])
    carry_ref[...] = jnp.zeros_like(carry_ref)
    for k, (ref, value) in enumerate(zip((keep_ref, mass_ref, weight_ref), values)):
        ref[...] = value
        rest = value[rows - 1 :]
        for part in range(3):
            rounded = rest.astype(BF16).astype(F32)
            carry_ref[part : part + 1, k * bands : (k + 1) * bands] = rounded
            rest = rest - rounded


def pack_kernel(scalar_ref, feat_ref, forget_ref, conv_ref, res_ref, in_ref, out_ref,
                keep_ref, mass_ref, weight_ref, pack_ref, carry_ref):
    scan_kernel(feat_ref, forget_ref, keep_ref, mass_ref, weight_ref, carry_ref)
    c = pack_ref.shape[1]
    n, half, more = conv_ref.shape[1] // 2, res_ref.shape[1] // 2, in_ref.shape[0]

    def fill(across):
        cols = slice(across * c, (across + 1) * c)
        part = slice(across * half, (across + 1) * half)
        at = 0

        def put(value):
            nonlocal at
            pack_ref[at : at + value.shape[0], :] = value
            at += value.shape[0]

        put(conv_ref[0, :n, cols])
        put(res_ref[1, part, :])
        put(conv_ref[0, n:, cols])
        put(conv_ref[1, :n, cols])
        put(res_ref[0, part, :])
        put((out_ref if across else in_ref)[...])
        put(carry_ref[...].astype(BF16))
        put(conv_ref[1, n:, cols])

    pl.when(scalar_ref[1] == 0)(lambda: fill(0))
    pl.when(scalar_ref[1] == 1)(lambda: fill(1))


def norm_kernel(scalar_ref, feat_ref, keep_ref, mass_ref, weight_ref, carry_ref, label_ref, out_ref):
    bands = feat_ref.shape[1]
    mass0 = jnp.zeros((1, bands), F32)
    weight0 = jnp.zeros((1, bands), F32)
    for j in range(carry_ref.shape[0]):
        parts = carry_ref[j].astype(F32)
        value = (parts[0:1] + parts[1:2]) + parts[2:3]
        before = j < scalar_ref[2]
        keep = value[:, :bands]
        mass0 = jnp.where(before, keep * mass0 + value[:, bands : 2 * bands], mass0)
        weight0 = jnp.where(before, keep * weight0 + value[:, 2 * bands : 3 * bands], weight0)
    keep = keep_ref[...]
    mass = keep * mass0 + mass_ref[...]
    weight = keep * weight0 + weight_ref[...]
    normed = (feat_ref[...] / jnp.sqrt(mass / weight + LEVEL_FLOOR)).astype(BF16)
    out_ref[LABEL_ROWS:, :] = normed
    out_ref[:LABEL_ROWS, :] = jnp.zeros((LABEL_ROWS, bands), BF16)
    out_ref[: label_ref.shape[0], :] = label_ref[...].astype(F32).astype(BF16)


def rows_of(ref, part=None):
    half = ref.shape[0] // 2
    value = ref[...] if part is None else ref[part * half : (part + 1) * half]
    return value.reshape(-1, value.shape[-1]).astype(BF16)


def place(site_ref, copies):
    mine = site_ref[0]

    def body(tm, _):
        for target, row, own, other, half, at, count in copies:
            target[2 * tm + mine, row : row + count, :] = own[tm, half, at : at + count, :]
            target[2 * tm + 1 - mine, row : row + count, :] = other[tm, half, at : at + count, :]
        return 0

    lax.fori_loop(0, copies[0][2].shape[0], body, 0)


def activate(past, now, filt_ref, gate_ref):
    joined = jnp.concatenate([past, now], axis=1)
    t = jnp.tanh(dot(joined, rows_of(filt_ref)))
    s = 0.5 + 0.5 * jnp.tanh(0.5 * dot(joined, rows_of(gate_ref)))
    return t, s


def slopes(t, s):
    return s * (1.0 - t * t), t * s * (1.0 - s)


def tile_at(i, offset=0):
    return pl.ds(pl.multiple_of(i * TILE + offset, TILE), TILE)


def forward_first(before, site_ref, norm_ref, w_in_ref, a_ref, a2_ref, b_ref, b2_ref, c_ref, c2_ref,
                  h0_ref, h1_ref, gated_ref, filtd_ref, gated_d_ref, filt_ref, gate_ref, res_ref):
    rows, c = h0_ref.shape
    kept, steps = filtd_ref.shape[0], gated_ref.shape[0]
    d = rows - h1_ref.shape[0]
    n, r = a_ref.shape[2], res_ref.shape[1] // 2
    place(site_ref, [
        (filt_ref, 0, a_ref, a2_ref, 0, 0, n), (gate_ref, 0, a_ref, a2_ref, 1, 0, n),
        (filt_ref, n, b_ref, b2_ref, 0, 0, n), (gate_ref, n, b_ref, b2_ref, 1, 0, n),
        (res_ref, 0, c_ref, c2_ref, 0, 0, r), (res_ref, r, c_ref, c2_ref, 1, 0, r)])

    for i in range(rows // TILE):
        at = slice(i * TILE, (i + 1) * TILE)
        h0_ref[at, :] = dot(norm_ref[at, :], w_in_ref[...]).astype(BF16)
    for i in range(h1_ref.shape[0] // TILE):
        at = slice(i * TILE, (i + 1) * TILE)
        now = h0_ref[i * TILE + d : (i + 1) * TILE + d, :]
        t, s = activate(h0_ref[at, :], now, filt_ref, gate_ref)
        gated = (t * s).astype(BF16)
        h1_ref[at, :] = (now.astype(F32) + dot(gated, rows_of(res_ref))).astype(BF16)
        first = i * TILE - before
        if 0 <= first < kept:
            own = slice(first, first + TILE)
            filtd_ref[own, :], gated_d_ref[own, :] = (v.astype(BF16) for v in slopes(t, s))
            if first < steps:
                gated_ref[own, :] = gated


def store_terms(site_ref, keep_ref, send_ref, row, value, first, size, start, count, lane=0):
    mine = site_ref[0] == 0
    at = (slice(row, row + count), slice(lane, lane + value.shape[1]))
    for k in range(value.shape[0] // (2 * size)):
        low = value[2 * k * size + start : 2 * k * size + start + count]
        high = value[(2 * k + 1) * size + start : (2 * k + 1) * size + start + count]
        keep_ref[(first + k,) + at] = jnp.where(mine, low, high).astype(keep_ref.dtype)
        send_ref[(first + k,) + at] = jnp.where(mine, high, low).astype(send_ref.dtype)


def conv_terms(site_ref, keep_ref, send_ref, first, size, res, value):
    c = value.shape[1] // 2
    store_terms(site_ref, keep_ref, send_ref, 0, value[:, c:], first, size, 0, size)
    store_terms(site_ref, keep_ref, send_ref, size + res, value[:, :c], first, size, 0, size)


def res_terms(site_ref, keep_ref, send_ref, first, conv, size, value):
    half = size // 2
    store_terms(site_ref, keep_ref, send_ref, conv, value, first, size, half, half)
    store_terms(site_ref, keep_ref, send_ref, 2 * conv + half, value, first, size, 0, half)


def second_kernel(steps, scale, sizes, site_ref, h1_ref, w_out_ref, label_ref,
                  a_ref, a2_ref, b_ref, b2_ref, c_ref, c2_ref,
                  loss_ref, keep_ref, send_ref, back_ref, grad_ref, filt_ref, gate_ref,
                  res_ref, gated_ref, h2_ref, lgrad_ref, round_ref):
    rows, c = back_ref.shape[0], grad_ref.shape[1]
    d = h1_ref.shape[0] - rows
    classes = w_out_ref.shape[1]
    conv, res, _, out = sizes
    n, r = conv // 2, res // 2
    place(site_ref, [
        (res_ref, 0, a_ref, a2_ref, 0, 0, r), (res_ref, r, a_ref, a2_ref, 1, 0, r),
        (filt_ref, 0, b_ref, b2_ref, 0, 0, n), (gate_ref, 0, b_ref, b2_ref, 1, 0, n),
        (filt_ref, n, c_ref, c2_ref, 0, 0, n), (gate_ref, n, c_ref, c2_ref, 1, 0, n)])

    lanes = label_ref.shape[1]
    class_row = lax.broadcasted_iota(jnp.int32, (classes, lanes), 0).astype(F32)
    unit = class_row == lax.broadcasted_iota(jnp.int32, (lanes, lanes), 1).astype(F32)
    row = lax.broadcasted_iota(jnp.int32, (TILE, 1), 0)
    left = site_ref[3] - site_ref[2] * steps

    for i in range(rows // TILE):
        at = slice(i * TILE, (i + 1) * TILE)
        now = h1_ref[i * TILE + d : (i + 1) * TILE + d, :]
        t, s = activate(h1_ref[at, :], now, filt_ref, gate_ref)
        gated = (t * s).astype(BF16)
        h2 = (now.astype(F32) + dot(gated, rows_of(res_ref))).astype(BF16)
        logits = dot(h2, w_out_ref[...])
        total = jnp.log(jnp.sum(jnp.exp(logits), axis=1, keepdims=True))
        groups = range(i * TILE // lanes, (i + 1) * TILE // lanes)
        hot = jnp.concatenate(
            [(class_row == label_ref[k : k + 1, :].astype(F32)).astype(F32).T for k in groups])
        valid = (row + i * TILE < left).astype(F32)
        lgrad = ((jnp.exp(logits - total) - hot) * (valid * scale)).astype(BF16)
        grad = dot_t(lgrad, w_out_ref[...])
        rounded = grad.astype(BF16)
        back = dot_t(rounded, rows_of(res_ref))
        filtd, gated_d = slopes(t, s)
        back_ref[at, :c] = (back * filtd).astype(BF16)
        back_ref[at, c:] = (back * gated_d).astype(BF16)
        if i * TILE < grad_ref.shape[0]:
            grad_ref[at, :] = grad
        if i * TILE < steps:
            loss = (total - jnp.sum(logits * hot, axis=1, keepdims=True)) * valid
            for j, k in enumerate(groups):
                part = jnp.where(unit, loss[j * lanes : (j + 1) * lanes], 0.0)
                loss_ref[k : k + 1, :] = jnp.sum(part, axis=0, keepdims=True)
            gated_ref[at, :] = gated
            h2_ref[at, :] = h2
            lgrad_ref[at, :] = lgrad
            round_ref[at, :] = rounded

    own = slice(0, steps)
    targets = (site_ref, keep_ref, send_ref)

    def terms(i, _):
        at = tile_at(i)
        first = i * (TILE // (2 * conv))
        conv_terms(*targets, first, conv, r, t_dot(h1_ref[0:steps, at], back_ref[own, :]))
        conv_terms(*targets, first + c // (2 * conv), conv, r, t_dot(h1_ref[d : d + steps, at], back_ref[own, :]))
        res_terms(*targets, i * (TILE // (2 * res)), conv, res, t_dot(gated_ref[own, at], round_ref[own, :]))
        value = t_dot(h2_ref[own, at], lgrad_ref[own, :])
        count = out * classes // c
        for q in range(c // classes):
            store_terms(*targets, 2 * conv + res, value, i * (TILE // (2 * out)), out, q * count, count, q * classes)
        return 0

    lax.fori_loop(0, c // TILE, terms, 0, unroll=True)


def grad_first(back1_ref, grad2_ref, filt1_ref, gate1_ref, filtd_ref, gated_d_ref, res_ref,
               grad_ref, round_ref, back_ref):
    rows, c = grad_ref.shape
    d1 = back1_ref.shape[0] - rows

    def tile(i, _):
        at, later = tile_at(i), tile_at(i, d1)
        grad = grad2_ref[at, :] + dot_t(back1_ref[at, :c], rows_of(filt1_ref, 1))
        grad += dot_t(back1_ref[at, c:], rows_of(gate1_ref, 1))
        grad += dot_t(back1_ref[later, :c], rows_of(filt1_ref, 0))
        grad += dot_t(back1_ref[later, c:], rows_of(gate1_ref, 0))
        rounded = grad.astype(BF16)
        back = dot_t(rounded, rows_of(res_ref))
        back_ref[at, :c] = (back * filtd_ref[at, :].astype(F32)).astype(BF16)
        back_ref[at, c:] = (back * gated_d_ref[at, :].astype(F32)).astype(BF16)
        grad_ref[at, :] = grad
        round_ref[at, :] = rounded
        return 0

    lax.fori_loop(0, rows // TILE, tile, 0, unroll=True)


def terms_first(steps, start, sizes, site_ref, back_ref, grad_ref, round_ref, h0_ref, gated_ref,
                norm_ref, filt_ref, gate_ref, keep_ref, send_ref, last_ref):
    rows, c = grad_ref.shape
    d0 = rows - steps
    conv, res, enter, _ = sizes
    own = slice(0, steps)
    targets = (site_ref, keep_ref, send_ref)

    def terms(i, _):
        at = tile_at(i)
        first = i * (TILE // (2 * conv))
        past, now = h0_ref[start - d0 : start - d0 + steps, at], h0_ref[start : start + steps, at]
        conv_terms(*targets, first, conv, res // 2, t_dot(past, back_ref[own, :]))
        conv_terms(*targets, first + c // (2 * conv), conv, res // 2, t_dot(now, back_ref[own, :]))
        res_terms(*targets, i * (TILE // (2 * res)), conv, res, t_dot(gated_ref[own, at], round_ref[own, :]))
        return 0

    lax.fori_loop(0, c // TILE, terms, 0, unroll=True)

    def last(i, _):
        at, later = tile_at(i), tile_at(i, d0)
        grad = grad_ref[at, :] + dot_t(back_ref[at, :c], rows_of(filt_ref, 1))
        grad += dot_t(back_ref[at, c:], rows_of(gate_ref, 1))
        grad += dot_t(back_ref[later, :c], rows_of(filt_ref, 0))
        grad += dot_t(back_ref[later, c:], rows_of(gate_ref, 0))
        last_ref[at, :] = grad.astype(BF16)
        return 0

    lax.fori_loop(0, steps // TILE, last, 0, unroll=True)
    value = t_dot(norm_ref[start : start + steps, :], last_ref[...])
    store_terms(*targets, 2 * conv + res, value, 0, enter, 0, enter)


NEAR, FAR, ACROSS = ("tm", 0), ("tm", 1), ("groups", 0)


def swap(value, link):
    axis, bit = link
    return lax.ppermute(value, axis, [(i, i ^ (1 << bit)) for i in range(lax.axis_size(axis))])


def my_bit(link):
    return (lax.axis_index(link[0]) >> link[1]) & 1


def time_bits():
    return lax.axis_size("tm").bit_length() - 1


def dim_of(link):
    return time_bits() if link == ACROSS else time_bits() - 1 - link[1]


def join(held, other, link):
    dim = dim_of(link)
    return jnp.where(
        my_bit(link) == 0,
        jnp.concatenate([held, other], axis=dim),
        jnp.concatenate([other, held], axis=dim),
    )


def together(*values):
    return lax.optimization_barrier(values)


def sum_step(held, link):
    dim, mine = dim_of(link), my_bit(link)
    other = swap(lax.dynamic_index_in_dim(held, 1 - mine, dim), link)
    return lax.dynamic_index_in_dim(held, mine, dim).astype(F32) + other.astype(F32)


def sum_rest(held, gate_rows):
    shape = held.shape[1:]
    held = held.reshape((2,) * time_bits() + shape)
    gate, filt = held[..., :gate_rows, :], held[..., gate_rows:, :]
    filt, gate = sum_step(filt, NEAR).astype(BF16), sum_step(gate, FAR).astype(BF16)
    filt, gate = sum_step(filt, FAR).astype(BF16), sum_step(gate, NEAR).astype(BF16)
    held = jnp.concatenate([gate, filt], axis=-2)
    for bit in range(2, time_bits()):
        total = sum_step(held, ("tm", bit))
        held = total.astype(BF16)
    return total.reshape(shape)


def hop(value, by):
    size = lax.axis_size("tm")
    return lax.ppermute(value, "tm", [(i, i + by) for i in range(size) if 0 <= i + by < size])


def rows_before(value, count):
    steps, parts, by = value.shape[0] - LABEL_ROWS, [], 1
    while count > 0:
        take = min(count, steps)
        parts.insert(0, hop(value[LABEL_ROWS + steps - take :], by))
        count, by = count - take, by + 1
    return parts


def rows_after(value, count):
    steps, parts, by = value.shape[0] - LABEL_ROWS, [], 1
    while count > 0:
        take = min(count, steps)
        parts.append(hop(value[: LABEL_ROWS + take], -by))
        count, by = count - take, by + 1
    return parts


def on_device(features, forget, labels, lengths, w_conv, w_res, w_in, w_out):
    _, steps, bands = features.shape
    time_devices, site_devices = lax.axis_size("tm"), lax.axis_size("site")
    devices = time_devices * site_devices
    c = w_res.shape[2]
    classes = w_out.shape[1]
    conv, res, enter, out = sizes = (w_conv.shape[1], w_res.shape[1], w_in.shape[0], w_out.shape[0])
    half, extra = res // 2, out * classes // c
    aligned = conv % 32 == 0 and res % 32 == 0
    kind = BF16 if aligned else F32
    d0, d1 = BASE_DILATION, 2 * BASE_DILATION
    reach = d0 + d1
    position, site = lax.axis_index("tm"), lax.axis_index("site")
    across = my_bit(ACROSS)
    scalars = jnp.stack([site, across, position, lengths[0]]).astype(jnp.int32)
    core = ("site", 0)

    block = ((steps, bands), F32)
    feat = features[0]
    out_rows = w_out.reshape(extra, c)
    if aligned:
        packed = 2 * (conv + half) + enter + CARRY_ROWS
        keep, mass, weight, held, _ = call(
            pack_kernel, [block] * 3 + [((packed, c), BF16), ((CARRY_ROWS, c), F32)], [], 40 * steps * bands,
            scalars, feat, forget[0], w_conv, w_res, w_in, out_rows)
    else:
        keep, mass, weight, carry = call(
            scan_kernel, [block] * 3 + [((CARRY_ROWS, c), F32)], [], 40 * steps * bands, feat, forget[0])
        n = conv // 2
        conv_own = jnp.where(across == 0, w_conv[:, :, :c], w_conv[:, :, c:])
        res_own = jnp.where(across == 0, w_res[:, :half], w_res[:, half:])
        held = jnp.concatenate([
            conv_own[0, :n], res_own[1], conv_own[0, n:], conv_own[1, :n], res_own[0],
            jnp.where(across == 0, w_in, out_rows), carry.astype(BF16), conv_own[1, n:]])
    n = conv // 2
    cuts = [n, half, n, n, half + enter + CARRY_ROWS, n]
    held = held.reshape((1,) * (time_bits() + 1) + held.shape)
    for bit in reversed(range(2, time_bits())):
        held = join(held, swap(held, ("tm", bit)), ("tm", bit))

    orders = [(ACROSS, FAR, NEAR), (NEAR, ACROSS, FAR), (FAR, NEAR, ACROSS)]
    bounds = [0, cuts[0] + cuts[1], sum(cuts[:4]), sum(cuts)]
    pieces = [held[..., bounds[k] : bounds[k + 1], :] for k in range(3)]
    for step in range(2):
        pieces = together(*pieces)
        pieces = [join(p, swap(p, order[step]), order[step]) for p, order in zip(pieces, orders)]
    at = half + enter
    carries = pieces[2][..., at : at + CARRY_ROWS, :].reshape(time_devices, CARRY_ROWS, c)
    pieces[2] = jnp.concatenate([pieces[2][..., :at, :], pieces[2][..., at + CARRY_ROWS :, :]], axis=-2)
    cuts[4] = at
    label_rows = steps // bands
    (normed,) = call(norm_kernel, [((LABEL_ROWS + steps, bands), BF16)], [], 10 * steps * bands,
                     scalars, feat, keep, mass, weight, carries, labels[0].reshape(label_rows, bands))
    pieces = together(*pieces)
    layers = [[p[..., :cut, :] for p, cut in zip(pieces, cuts[::2])],
              [p[..., cut:, :] for p, cut in zip(pieces, cuts[::2])]]
    first = [join(p, swap(p, order[2]), order[2]) for p, order in zip(layers[0], orders)]
    past, future = rows_before(normed, reach), rows_after(normed, reach)
    window = jnp.concatenate(past + [normed[LABEL_ROWS:]] + [v[LABEL_ROWS:] for v in future])
    label_window = jnp.concatenate(
        [v[: (v.shape[0] - LABEL_ROWS) // bands] for v in [normed] + future])
    *rest, window = together(*first, *layers[1], window)
    first, second = rest[:3], rest[3:]
    second = [join(p, swap(p, order[2]), order[2]) for p, order in zip(second, orders)]

    def both_cores(parts):
        parts = [p.reshape((time_devices, 2) + p.shape[-2:]) for p in parts]
        pairs = [(p, swap(p, core)) for p in parts]
        return pairs

    def kernel_args(pairs):
        return [v.astype(kind) for pair in pairs for v in pair]

    first = both_cores(first)
    own, other = (v[:, :, half:] for v in first[2])
    extras = jnp.where(site == 0, jnp.stack([own, other], axis=1), jnp.stack([other, own], axis=1))
    in_all = extras[:, :, 0].reshape(-1, c)
    out_all = extras[:, :, 1].reshape(-1, classes)

    total_rows, rows0, rows1 = steps + 2 * reach, steps + d0, steps + reach
    conv_all, res_all = ((devices, conv, c), kind), ((devices, res, c), kind)
    h0, h1, gated0, filtd0, gated_d0, filt0, gate0, res0 = call(
        functools.partial(forward_first, d1),
        [((total_rows, c), BF16), ((total_rows - d0, c), BF16), ((steps, c), BF16), ((rows0, c), BF16), ((rows0, c), BF16),
         conv_all, conv_all, res_all],
        [], 2 * total_rows * c * (bands + 5 * c), scalars, window, in_all, *kernel_args(first))

    second = both_cores(second)
    scale = 1.0 / math.sqrt(site_devices * steps * time_devices)
    package = [((time_devices, 2 * conv + res + extra, c), kind)] * 2
    loss, keep1, send1, back1, grad2, filt1, gate1 = call(
        functools.partial(second_kernel, steps, scale, sizes),
        [((label_rows, bands), F32)] + package + [((rows1, 2 * c), BF16), ((rows0, c), F32), conv_all, conv_all],
        [pltpu.VMEM((devices, res, c), kind), pltpu.VMEM((steps, c), BF16), pltpu.VMEM((steps, c), BF16),
         pltpu.VMEM((steps, classes), BF16), pltpu.VMEM((steps, c), BF16)],
        2 * rows1 * c * 6 * c + 2 * steps * 5 * c * c,
        scalars, h1, out_all, label_window, *kernel_args(second))

    sum1 = (keep1.astype(F32) + swap(send1.astype(BF16), core).astype(F32)).astype(BF16)
    grad1, round0, back0 = call(
        grad_first, [((rows0, c), F32), ((rows0, c), BF16), ((rows0, 2 * c), BF16)], [],
        2 * rows0 * c * 5 * c, back1, grad2, filt1, gate1, filtd0, gated_d0, res0)
    sum1, back0 = together(sum1, back0)
    keep0, send0 = call(
        functools.partial(terms_first, steps, reach, sizes), package, [pltpu.VMEM((steps, c), BF16)],
        2 * steps * 9 * c * c,
        scalars, back0, grad1, round0, h0, gated0, window, filt0, gate0)
    sum0 = (keep0.astype(F32) + swap(send0.astype(BF16), core).astype(F32)).astype(BF16)

    grads = []
    for held in (sum0, sum1):
        total = sum_rest(held, conv + half)
        gate, filt = total[: conv + half], total[conv + half :]
        grads.append((
            jnp.concatenate([filt[:conv], gate[:conv]], axis=1),
            jnp.concatenate([filt[conv : conv + half], gate[conv:]]),
            filt[conv + half :],
        ))
    (conv0, res0, grad_in), (conv1, res1, grad_out) = grads
    return (
        loss.reshape(1, steps),
        jnp.stack([conv0, conv1]),
        jnp.stack([res0, res1]),
        grad_in,
        unpack_out(grad_out, classes),
    )


def unpack_out(value, classes):
    q = value.shape[1] // classes
    return jnp.concatenate([value[:, k * classes : (k + 1) * classes] for k in range(q)])


def solution(mesh):
    return jax.shard_map(
        on_device,
        mesh=mesh,
        in_specs=(
            P(("groups", "site"), "tm", None),
            P(("groups", "site"), "tm", None),
            P(("groups", "site"), "tm"),
            P(("groups", "site")),
            P(None, ("tm", "site"), None),
            P(None, ("tm", "site"), None),
            P(("tm", "site"), None),
            P(("tm", "site"), None),
        ),
        out_specs=(
            P(("groups", "site"), "tm"),
            P("groups", ("tm", "site"), None),
            P("groups", ("tm", "site"), None),
            P(("tm", "site"), "groups"),
            P(("tm", "site"), "groups"),
        ),
        check_vma=False,
    )
```

```python
import functools
import itertools
import math

import jax
import jax.numpy as jnp
from jax import lax
from jax.experimental import pallas as pl
from jax.experimental.pallas import tpu as pltpu
from jax.sharding import PartitionSpec as P

BASE_DILATION = 256
LEVEL_FLOOR = 0.1
F32 = jnp.float32
BF16 = jnp.bfloat16
TILE = 256
VMEM_LIMIT = 24 * 1024 * 1024
FIRST_LIMIT = 56 * 1024 * 1024
WHOLE = pl.BlockSpec(memory_space=pltpu.VMEM)
SCALAR = pl.BlockSpec(memory_space=pltpu.SMEM)
STAYS = pl.BlockSpec(memory_space=pltpu.HBM)


def dot(a, b):
    return lax.dot_general(a, b, (((1,), (0,)), ((), ())), preferred_element_type=F32)


def dot_t(a, b):
    return lax.dot_general(a, b, (((1,), (1,)), ((), ())), preferred_element_type=F32)


def t_dot(a, b):
    return lax.dot_general(a, b, (((0,), (0,)), ((), ())), preferred_element_type=F32)


def call(kernel, outs, scratch, flops, *args, far=0, limit=VMEM_LIMIT):
    outs = [o + (False,) * (3 - len(o)) for o in outs]
    moved = sum(a.size * a.dtype.itemsize for a in args)
    moved += sum(math.prod(s) * jnp.dtype(d).itemsize for s, d, _ in outs)
    near = args[: len(args) - far]
    return pl.pallas_call(
        kernel,
        out_shape=[jax.ShapeDtypeStruct(s, d) for s, d, _ in outs],
        in_specs=[SCALAR if a.dtype == jnp.int32 and a.ndim == 1 else WHOLE for a in near] + [STAYS] * far,
        out_specs=[STAYS if stays else WHOLE for _, _, stays in outs],
        scratch_shapes=scratch,
        compiler_params=pltpu.CompilerParams(vmem_limit_bytes=limit),
        cost_estimate=pl.CostEstimate(flops=flops, bytes_accessed=moved, transcendentals=0),
    )(*args)


def by_core(core, first, second):
    return first + core * (second - first)


def spots(tm, count):
    near, far, rest, step = tm & 1, (tm >> 1) & 1, tm >> 2, count // 4
    return (2 * near + far) * step + rest, (2 * far + near) * step + rest


CARRY_ROWS = 8
LABEL_ROWS = 16


def scan(feat, forget):
    rows = feat.shape[0]
    keep, mass, weight = 1.0 - forget, forget * (feat * feat), forget
    row = lax.broadcasted_iota(jnp.int32, feat.shape, 0)
    step = 1
    while step < rows:
        inside = row >= step
        before = jnp.where(inside, pltpu.roll(mass, step, 0), 0.0)
        mass = keep * before + mass
        before = jnp.where(inside, pltpu.roll(weight, step, 0), 0.0)
        weight = keep * before + weight
        keep = keep * jnp.where(inside, pltpu.roll(keep, step, 0), 1.0)
        step *= 2
    return keep, mass, weight


def scan_kernel(feat_ref, forget_ref, keep_ref, mass_ref, weight_ref, carry_ref):
    rows, bands = feat_ref.shape
    values = scan(feat_ref[...], forget_ref[...])
    carry_ref[...] = jnp.zeros_like(carry_ref)
    for k, (ref, value) in enumerate(zip((keep_ref, mass_ref, weight_ref), values)):
        ref[...] = value
        rest = value[rows - 1 :]
        for part in range(3):
            rounded = rest.astype(BF16).astype(F32)
            carry_ref[part : part + 1, k * bands : (k + 1) * bands] = rounded
            rest = rest - rounded


def pack_kernel(scalar_ref, feat_ref, forget_ref, conv_ref, res_ref, in_ref, out_ref,
                keep_ref, mass_ref, weight_ref, pack_ref, carry_ref):
    scan_kernel(feat_ref, forget_ref, keep_ref, mass_ref, weight_ref, carry_ref)
    c = pack_ref.shape[1]
    cut, half, more = conv_ref.shape[1] * 3 // 4, res_ref.shape[1] // 2, in_ref.shape[0]

    def fill(across):
        cols = slice(across * c, (across + 1) * c)
        part = slice(across * half, (across + 1) * half)
        at = 0

        def put(value):
            nonlocal at
            pack_ref[at : at + value.shape[0], :] = value
            at += value.shape[0]

        put(conv_ref[0, :, cols])
        put(carry_ref[...].astype(BF16))
        put(conv_ref[1, :cut, cols])
        put(res_ref[0, part, :])
        if across:
            put(jnp.concatenate([out_ref[k * more : (k + 1) * more, :] for k in range(c // out_ref.shape[1])], axis=1))
        else:
            put(in_ref[...])
        put(res_ref[1, part, :])
        put(conv_ref[1, cut:, cols])

    pl.when(scalar_ref[1] == 0)(lambda: fill(0))
    pl.when(scalar_ref[1] == 1)(lambda: fill(1))


def norm_kernel(scalar_ref, feat_ref, keep_ref, mass_ref, weight_ref, carry_ref, label_ref, out_ref):
    bands = feat_ref.shape[1]
    mass0 = jnp.zeros((1, bands), F32)
    weight0 = jnp.zeros((1, bands), F32)
    for tm in range(carry_ref.shape[0]):
        first, second = spots(tm, carry_ref.shape[0])
        parts = carry_ref[by_core(scalar_ref[0], first, second)].astype(F32)
        value = (parts[0:1] + parts[1:2]) + parts[2:3]
        before = tm < scalar_ref[2]
        keep = value[:, :bands]
        mass0 = jnp.where(before, keep * mass0 + value[:, bands : 2 * bands], mass0)
        weight0 = jnp.where(before, keep * weight0 + value[:, 2 * bands : 3 * bands], weight0)
    keep = keep_ref[...]
    mass = keep * mass0 + mass_ref[...]
    weight = keep * weight0 + weight_ref[...]
    normed = (feat_ref[...] / jnp.sqrt(mass / weight + LEVEL_FLOOR)).astype(BF16)
    out_ref[LABEL_ROWS:, :] = normed
    out_ref[:LABEL_ROWS, :] = jnp.zeros((LABEL_ROWS, bands), BF16)
    out_ref[: label_ref.shape[0], :] = label_ref[...].astype(F32).astype(BF16)


def rows_of(value):
    return value.reshape(-1, value.shape[-1]).astype(BF16)


def halves(conv_ref, gate):
    half = conv_ref.shape[1] // 2
    return rows_of(conv_ref[gate, :half]), rows_of(conv_ref[gate, half:])


def place(core, pair, puts):
    for ref, own in zip(pair, (True, False)):
        s = core if own else 1 - core
        rest = ref.shape[0] // 8
        bits = rest.bit_length() - 1
        for steps in itertools.product((0, 1), repeat=3):
            base = (4 * steps[0] + 2 * steps[1] + steps[2]) * rest

            def put(p, _):
                high = sum(((p >> (bits - 1 - b)) & 1) << b for b in range(bits))
                puts(s, steps, high, ref, base + p)
                return 0

            if rest <= 2:
                for p in range(rest):
                    put(p, 0)
            else:
                lax.fori_loop(0, rest, put, 0)


def place_main(conv_ref, row):
    def put(s, steps, high, ref, k):
        third, second, first = steps
        across = by_core(s, third, second)
        tm = 4 * high + 2 * by_core(s, second, first) + by_core(s, first, third)
        conv_ref[across, 2 * tm + s, row : row + ref.shape[1], :] = ref[k].astype(conv_ref.dtype)

    return put


def place_side(layer, conv_ref, res_ref, *extra):
    def put(s, steps, high, ref, k):
        far, near, across = steps
        device = 2 * (4 * high + 2 * far + near) + s
        half = res_ref.shape[1] // 2
        res_ref[device, across * half : (across + 1) * half, :] = ref[k, :half, :].astype(res_ref.dtype)
        value = ref[k, half:, :]
        if layer == 1:
            conv_ref[across, device, conv_ref.shape[2] - value.shape[0] :, :] = value.astype(conv_ref.dtype)
            return
        in_ref, out_ref = extra
        value = value.astype(F32)
        if across == 0:
            in_ref[device] = value
            return
        count, classes = value.shape[0], out_ref.shape[2]
        for q in range(value.shape[1] // classes):
            out_ref[device, q * count : (q + 1) * count, :] = value[:, q * classes : (q + 1) * classes]

    return put


def activate(past, now, conv_ref):
    joined = jnp.concatenate([past, now], axis=1)
    t = jnp.tanh(dot(joined, rows_of(conv_ref[0])))
    s = 0.5 + 0.5 * jnp.tanh(0.5 * dot(joined, rows_of(conv_ref[1])))
    return t, s


def slopes(t, s):
    return s * (1.0 - t * t), t * s * (1.0 - s)


def tile_of(i, offset=0):
    return slice(i * TILE + offset, (i + 1) * TILE + offset)


def copies(pairs, sems):
    return [pltpu.make_async_copy(a, b, sems.at[k]) for k, (a, b) in enumerate(pairs)]


def forward_first(before, steps, scalar_ref, norm_ref, a_ref, a2_ref, b_ref, b2_ref,
                  h1_ref, w_out_ref, h0_far, gated_far, slope_far, conv_far, res_far,
                  h0_ref, gated_ref, slope_ref, conv_ref, res_ref, in_ref, out_ref, sems):
    rows = h0_ref.shape[0]
    kept = slope_ref.shape[1]
    d = rows - h1_ref.shape[0]
    core = scalar_ref[0]
    place(core, (a_ref, a2_ref), place_main(conv_ref, 0))
    place(core, (b_ref, b2_ref), place_side(0, conv_ref, res_ref, in_ref, out_ref))
    w_out_ref[...] = rows_of(out_ref[...])
    w_in = rows_of(in_ref[...])
    for i in range(rows // TILE):
        h0_ref[tile_of(i), :] = dot(norm_ref[tile_of(i), :], w_in).astype(BF16)
    moves = copies([(conv_ref, conv_far), (res_ref, res_far), (h0_ref.at[before : before + kept], h0_far),
                    (gated_ref, gated_far), (slope_ref, slope_far)], sems)
    for move in moves[:3]:
        move.start()
    for i in range(h1_ref.shape[0] // TILE):
        now = h0_ref[tile_of(i, d), :]
        t, s = activate(h0_ref[tile_of(i), :], now, conv_ref)
        gated = (t * s).astype(BF16)
        h1_ref[tile_of(i), :] = (now.astype(F32) + dot(gated, rows_of(res_ref[...]))).astype(BF16)
        first = i * TILE - before
        if 0 <= first < kept:
            own = slice(first, first + TILE)
            slope_ref[0, own, :], slope_ref[1, own, :] = (v.astype(BF16) for v in slopes(t, s))
            if first < steps:
                gated_ref[own, :] = gated
            if first + TILE == kept:
                for move in moves[3:]:
                    move.start()
    for move in moves:
        move.wait()


def store_terms(core, keep_ref, send_ref, row, value, first, size, start, count, lane=0):
    at = (slice(row, row + count), slice(lane, lane + value.shape[1]))
    for k in range(value.shape[0] // (2 * size)):
        low = value[2 * k * size + start : 2 * k * size + start + count]
        high = value[(2 * k + 1) * size + start : (2 * k + 1) * size + start + count]
        one, two = spots(first + k, keep_ref.shape[0])
        keep_ref[(by_core(core, one, two),) + at] = jnp.where(core == 0, low, high).astype(keep_ref.dtype)
        send_ref[(by_core(core, two, one),) + at] = jnp.where(core == 0, high, low).astype(send_ref.dtype)


def conv_terms(targets, first, size, value):
    c = value.shape[1] // 2
    store_terms(*targets, 0, value[:, :c], first, size, 0, size)
    store_terms(*targets, size, value[:, c:], first, size, 0, size)


def second_kernel(steps, scale, sizes, scalar_ref, h1_ref, w_out_ref, label_ref, a_ref, a2_ref, b_ref, b2_ref,
                  loss_ref, keep_ref, send_ref, back_ref, grad_ref, conv_ref,
                  res_ref, gated_ref, h2_ref, lgrad_ref, round_ref):
    rows, c = back_ref.shape[0], grad_ref.shape[1]
    d = h1_ref.shape[0] - rows
    classes = w_out_ref.shape[1]
    conv, res, _, out = sizes
    core = scalar_ref[0]
    place(core, (a_ref, a2_ref), place_main(conv_ref, 0))
    place(core, (b_ref, b2_ref), place_side(1, conv_ref, res_ref))

    lanes = label_ref.shape[1]
    class_row = lax.broadcasted_iota(jnp.int32, (classes, lanes), 0).astype(F32)
    unit = class_row == lax.broadcasted_iota(jnp.int32, (lanes, lanes), 1).astype(F32)
    row = lax.broadcasted_iota(jnp.int32, (TILE, 1), 0)
    left = scalar_ref[3] - scalar_ref[2] * steps

    for i in range(rows // TILE):
        at = tile_of(i)
        now = h1_ref[tile_of(i, d), :]
        t, s = activate(h1_ref[at, :], now, conv_ref)
        gated = (t * s).astype(BF16)
        h2 = (now.astype(F32) + dot(gated, rows_of(res_ref[...]))).astype(BF16)
        logits = dot(h2, w_out_ref[...])
        total = jnp.log(jnp.sum(jnp.exp(logits), axis=1, keepdims=True))
        groups = range(i * TILE // lanes, (i + 1) * TILE // lanes)
        hot = jnp.concatenate(
            [(class_row == label_ref[k : k + 1, :].astype(F32)).astype(F32).T for k in groups])
        valid = (row + i * TILE < left).astype(F32)
        lgrad = ((jnp.exp(logits - total) - hot) * (valid * scale)).astype(BF16)
        grad = dot_t(lgrad, w_out_ref[...])
        rounded = grad.astype(BF16)
        back = dot_t(rounded, rows_of(res_ref[...]))
        filter_slope, gate_slope = slopes(t, s)
        back_ref[at, :c] = (back * filter_slope).astype(BF16)
        back_ref[at, c:] = (back * gate_slope).astype(BF16)
        if i * TILE < grad_ref.shape[0]:
            grad_ref[at, :] = grad
        if i * TILE < steps:
            loss = (total - jnp.sum(logits * hot, axis=1, keepdims=True)) * valid
            for j, k in enumerate(groups):
                part = jnp.where(unit, loss[j * lanes : (j + 1) * lanes], 0.0)
                loss_ref[k : k + 1, :] = jnp.sum(part, axis=0, keepdims=True)
            gated_ref[at, :] = gated
            h2_ref[at, :] = h2
            lgrad_ref[at, :] = lgrad
            round_ref[at, :] = rounded

    own = slice(0, steps)
    targets = (core, keep_ref, send_ref)
    for i in range(c // TILE):
        at = tile_of(i)
        first, per = i * (TILE // (2 * conv)), c // (2 * conv)
        conv_terms(targets, first, conv, t_dot(h1_ref[0:steps, at], back_ref[own, :]))
        conv_terms(targets, first + per, conv, t_dot(h1_ref[d : d + steps, at], back_ref[own, :]))
        value = t_dot(gated_ref[own, at], round_ref[own, :])
        store_terms(*targets, 2 * conv, value, i * (TILE // (2 * res)), res, 0, res)
        value = t_dot(h2_ref[own, at], lgrad_ref[own, :])
        count = out * classes // c
        for q in range(c // classes):
            store_terms(*targets, 2 * conv + res, value, i * (TILE // (2 * out)), out, q * count, count, q * classes)


def grad_below(grad, back_ref, i, d, weights):
    c = back_ref.shape[1] // 2
    (filt_past, filt_now), (gate_past, gate_now) = weights
    grad = grad + dot_t(back_ref[tile_of(i), :c], filt_now) + dot_t(back_ref[tile_of(i), c:], gate_now)
    return grad + dot_t(back_ref[tile_of(i, d), :c], filt_past) + dot_t(back_ref[tile_of(i, d), c:], gate_past)


def grad_first(back1_ref, grad2_ref, conv1_ref, slope_far, res_far,
               grad_ref, round_ref, back_ref, slope_ref, res_ref, sems):
    rows, c = back_ref.shape[0], grad_ref.shape[1]
    d1 = back1_ref.shape[0] - rows
    moves = copies([(slope_far, slope_ref), (res_far, res_ref)], sems)
    for move in moves:
        move.start()
    weights = halves(conv1_ref, 0), halves(conv1_ref, 1)
    for i in range(rows // TILE):
        at = tile_of(i)
        grad = grad_below(grad2_ref[at, :], back1_ref, i, d1, weights)
        rounded = grad.astype(BF16)
        if i == 0:
            for move in moves:
                move.wait()
        back = dot_t(rounded, rows_of(res_ref[...]))
        back_ref[at, :c] = (back * slope_ref[0, at, :].astype(F32)).astype(BF16)
        back_ref[at, c:] = (back * slope_ref[1, at, :].astype(F32)).astype(BF16)
        if i * TILE < grad_ref.shape[0]:
            grad_ref[at, :] = grad
            round_ref[at, :] = rounded


def terms_first(sizes, scalar_ref, back_ref, grad_ref, round_ref, norm_ref, h0_far, gated_far, conv_far,
                keep_ref, send_ref, h0_ref, gated_ref, conv_ref, last_ref, sems):
    steps, c = grad_ref.shape
    d0 = back_ref.shape[0] - steps
    conv, res, enter, _ = sizes
    moves = copies([(h0_far, h0_ref), (gated_far, gated_ref), (conv_far, conv_ref)], sems)
    for move in moves:
        move.start()
    own = slice(0, steps)
    targets = (scalar_ref[0], keep_ref, send_ref)
    moves[0].wait()
    for i in range(c // TILE):
        at = tile_of(i)
        first, per = i * (TILE // (2 * conv)), c // (2 * conv)
        conv_terms(targets, first, conv, t_dot(h0_ref[0:steps, at], back_ref[own, :]))
        conv_terms(targets, first + per, conv, t_dot(h0_ref[d0 : d0 + steps, at], back_ref[own, :]))
        if i == 0:
            moves[1].wait()
        value = t_dot(gated_ref[:, at], round_ref[...])
        store_terms(*targets, 2 * conv, value, i * (TILE // (2 * res)), res, 0, res)
    moves[2].wait()
    weights = halves(conv_ref, 0), halves(conv_ref, 1)
    for i in range(steps // TILE):
        last_ref[tile_of(i), :] = grad_below(grad_ref[tile_of(i), :], back_ref, i, d0, weights).astype(BF16)
    value = t_dot(norm_ref[...], last_ref[...])
    store_terms(*targets, 2 * conv + res, value, 0, enter, 0, enter)


NEAR, FAR, ACROSS = ("tm", 0), ("tm", 1), ("groups", 0)
CORE = ("site", 0)


def swap(value, links):
    names = ("groups", "tm", "site")
    sizes = [lax.axis_size(name) for name in names]
    pairs = []
    for at in itertools.product(*(range(size) for size in sizes)):
        axis, bit = links[at[2]]
        to = tuple(i ^ (1 << bit) if name == axis else i for name, i in zip(names, at))
        pairs.append(tuple((p[0] * sizes[1] + p[1]) * sizes[2] + p[2] for p in (at, to)))
    return lax.ppermute(value, names, pairs)


def my_bit(links):
    first, second = ((lax.axis_index(axis) >> bit) & 1 for axis, bit in links)
    return jnp.where(lax.axis_index("site") == 0, first, second)


def time_bits():
    return lax.axis_size("tm").bit_length() - 1


def grow(held, links):
    other = swap(held, links)
    return jnp.where(
        my_bit(links) == 0, jnp.concatenate([held, other]), jnp.concatenate([other, held]))


def together(*values):
    return lax.optimization_barrier(values)


def sum_step(held, links, dim=0):
    mine = my_bit(links)
    other = swap(lax.dynamic_index_in_dim(held, 1 - mine, dim), links)
    return lax.dynamic_index_in_dim(held, mine, dim).astype(F32) + other.astype(F32)


def sum_rest(held):
    shape, bits = held.shape[1:], time_bits()
    held = held.reshape((2,) * bits + shape)
    held = sum_step(held, (NEAR, FAR)).astype(BF16)
    total = sum_step(held, (FAR, NEAR), 1)
    for bit in range(2, bits):
        total = sum_step(total.astype(BF16), (("tm", bit),) * 2, 2 + bits - 1 - bit)
    return total.reshape(shape)


def hop(value, by):
    size = lax.axis_size("tm")
    return lax.ppermute(value, "tm", [(i, i + by) for i in range(size) if 0 <= i + by < size])


def rows_before(value, count):
    steps, parts, by = value.shape[0] - LABEL_ROWS, [], 1
    while count > 0:
        take = min(count, steps)
        parts.insert(0, hop(value[LABEL_ROWS + steps - take :], by))
        count, by = count - take, by + 1
    return parts


def rows_after(value, count):
    steps, parts, by = value.shape[0] - LABEL_ROWS, [], 1
    while count > 0:
        take = min(count, steps)
        parts.append(hop(value[: LABEL_ROWS + take], -by))
        count, by = count - take, by + 1
    return parts


def on_device(features, forget, labels, lengths, w_conv, w_res, w_in, w_out):
    _, steps, bands = features.shape
    time_devices, site_devices = lax.axis_size("tm"), lax.axis_size("site")
    devices = time_devices * site_devices
    c = w_res.shape[2]
    classes = w_out.shape[1]
    conv, res, enter, out = sizes = (w_conv.shape[1], w_res.shape[1], w_in.shape[0], w_out.shape[0])
    half, cut = res // 2, conv * 3 // 4
    aligned = conv % 64 == 0 and res % 32 == 0
    kind = BF16 if aligned else F32
    d0, d1 = BASE_DILATION, 2 * BASE_DILATION
    reach = d0 + d1
    across = my_bit((ACROSS, ACROSS))
    scalars = jnp.stack(
        [lax.axis_index("site"), across, lax.axis_index("tm"), lengths[0]]).astype(jnp.int32)

    block = ((steps, bands), F32)
    feat = features[0]
    if aligned:
        packed = 2 * (conv + half) + enter + CARRY_ROWS
        keep, mass, weight, held, _ = call(
            pack_kernel, [block] * 3 + [((packed, c), BF16), ((CARRY_ROWS, c), F32)], [], 40 * steps * bands,
            scalars, feat, forget[0], w_conv, w_res, w_in, w_out, limit=FIRST_LIMIT)
    else:
        keep, mass, weight, carry = call(
            scan_kernel, [block] * 3 + [((CARRY_ROWS, c), F32)], [], 40 * steps * bands, feat, forget[0])
        conv_own = jnp.where(across == 0, w_conv[:, :, :c], w_conv[:, :, c:])
        res_own = jnp.where(across == 0, w_res[:, :half], w_res[:, half:])
        out_own = jnp.concatenate([w_out[k * enter : (k + 1) * enter] for k in range(c // classes)], axis=1)
        held = jnp.concatenate([
            conv_own[0], carry.astype(BF16), conv_own[1, :cut], res_own[0],
            jnp.where(across == 0, w_in, out_own), res_own[1], conv_own[1, cut:]])
    held = held[None]
    for bit in reversed(range(2, time_bits())):
        held = grow(held, (("tm", bit),) * 2)

    main_links = [(NEAR, FAR), (FAR, ACROSS), (ACROSS, NEAR)]
    side_links = [(ACROSS, ACROSS), (NEAR, NEAR), (FAR, FAR)]
    ends = conv + CARRY_ROWS + cut
    main, side = held[:, :ends], held[:, ends:]
    main, side = grow(main, main_links[0]), grow(side, side_links[0])
    carry = main[:, conv : conv + CARRY_ROWS]
    main = jnp.concatenate([main[:, :conv], main[:, conv + CARRY_ROWS :]], axis=1)
    main, side, carry = together(main, side, carry)
    carry = grow(carry, (FAR, NEAR))
    main, side = grow(main, main_links[1]), grow(side, side_links[1])
    label_rows = steps // bands
    bits = time_bits()
    carry = carry.reshape((2,) * bits + (CARRY_ROWS, c))
    carry = carry.transpose((1, 0) + tuple(range(bits - 1, 1, -1)) + (bits, bits + 1))
    (normed,) = call(norm_kernel, [((LABEL_ROWS + steps, bands), BF16)], [], 10 * steps * bands,
                     scalars, feat, keep, mass, weight, carry.reshape(time_devices, CARRY_ROWS, c),
                     labels[0].reshape(label_rows, bands))
    main, side = together(main, side)
    first = [main[:, :conv], side[:, : half + enter]]
    second = [main[:, conv:], side[:, half + enter :]]

    def last_step(parts):
        return [grow(p, links[2]) for p, links in zip(parts, (main_links, side_links))]

    def both_cores(parts):
        return [v.astype(kind) for p in parts for v in (p, swap(p, (CORE, CORE)))]

    first = both_cores(last_step(first))
    past, future = rows_before(normed, reach), rows_after(normed, reach)
    own_normed = normed[LABEL_ROWS:]
    window = jnp.concatenate(past + [own_normed] + [v[LABEL_ROWS:] for v in future])
    label_window = jnp.concatenate(
        [v[: (v.shape[0] - LABEL_ROWS) // bands] for v in [normed] + future])
    *first, window, second[0], second[1] = together(*first, window, *second)

    total_rows, rows0, rows1 = steps + 2 * reach, steps + d0, steps + reach
    conv_all, res_all = ((2, devices, conv, c), kind), ((devices, res, c), kind)
    V, sems = pltpu.VMEM, pltpu.SemaphoreType.DMA
    h1, out_all, *kept = call(
        functools.partial(forward_first, d1, steps),
        [((total_rows - d0, c), BF16), ((c, classes), BF16), ((rows0, c), BF16, True), ((steps, c), BF16, True),
         ((2, rows0, c), BF16, True), conv_all + (True,), res_all + (True,)],
        [V((total_rows, c), BF16), V((steps, c), BF16), V((2, rows0, c), BF16), V(*conv_all), V(*res_all),
         V((devices, enter, c), F32), V((devices, out, classes), F32), sems((5,))],
        2 * total_rows * c * (bands + 5 * c), scalars, window, *first)
    h0, gated0, slope0, conv0, res0 = kept

    second = both_cores(last_step(second))
    scale = 1.0 / math.sqrt(site_devices * steps * time_devices)
    package = [((time_devices, 2 * conv + res + enter, c), kind)] * 2
    loss, keep1, send1, back1, grad2, conv1 = call(
        functools.partial(second_kernel, steps, scale, sizes),
        [((label_rows, bands), F32)] + package + [((rows1, 2 * c), BF16), ((rows0, c), F32), conv_all],
        [V(*res_all), V((steps, c), BF16), V((steps, c), BF16), V((steps, classes), BF16), V((steps, c), BF16)],
        2 * rows1 * c * 6 * c + 2 * steps * 5 * c * c,
        scalars, h1, out_all, label_window, *second)

    core = (CORE, CORE)
    sum1 = (keep1.astype(F32) + swap(send1.astype(BF16), core).astype(F32)).astype(BF16)
    grad1, round0, back0 = call(
        grad_first, [((steps, c), F32), ((steps, c), BF16), ((rows0, 2 * c), BF16)],
        [V((2, rows0, c), BF16), V(*res_all), sems((2,))],
        2 * rows0 * c * 5 * c, back1, grad2, conv1, slope0, res0, far=2)
    sum1, back0 = together(sum1, back0)
    keep0, send0 = call(
        functools.partial(terms_first, sizes), package,
        [V((rows0, c), BF16), V((steps, c), BF16), V(*conv_all), V((steps, c), BF16), sems((3,))],
        2 * steps * 9 * c * c,
        scalars, back0, grad1, round0, own_normed, h0, gated0, conv0, far=3)
    sum0 = (keep0.astype(F32) + swap(send0.astype(BF16), core).astype(F32)).astype(BF16)

    convs, ress, extras = [], [], []
    for held in (sum0, sum1):
        total = sum_rest(held)
        convs.append(jnp.concatenate([total[:conv], total[conv : 2 * conv]], axis=1))
        ress.append(total[2 * conv : 2 * conv + res])
        extras.append(total[2 * conv + res :])
    grad_in, grad_out = extras
    return (
        loss.reshape(1, steps),
        jnp.stack(convs),
        jnp.stack(ress),
        grad_in,
        jnp.concatenate([grad_out[:, k * classes : (k + 1) * classes] for k in range(c // classes)]),
    )


def solution(mesh):
    return jax.shard_map(
        on_device,
        mesh=mesh,
        in_specs=(
            P(("groups", "site"), "tm", None),
            P(("groups", "site"), "tm", None),
            P(("groups", "site"), "tm"),
            P(("groups", "site")),
            P(None, ("tm", "site"), None),
            P(None, ("tm", "site"), None),
            P(("tm", "site"), None),
            P(("tm", "site"), None),
        ),
        out_specs=(
            P(("groups", "site"), "tm"),
            P("groups", ("tm", "site"), None),
            P("groups", ("tm", "site"), None),
            P(("tm", "site"), "groups"),
            P(("tm", "site"), "groups"),
        ),
        check_vma=False,
    )
```

```python
import functools
import itertools
import math

import jax
import jax.numpy as jnp
from jax import lax
from jax.experimental import pallas as pl
from jax.experimental.pallas import tpu as pltpu
from jax.sharding import PartitionSpec as P

BASE_DILATION = 256
LEVEL_FLOOR = 0.1
F32 = jnp.float32
BF16 = jnp.bfloat16
TILE = 256
VMEM_LIMIT = 24 * 1024 * 1024
FIRST_LIMIT = 56 * 1024 * 1024
WHOLE = pl.BlockSpec(memory_space=pltpu.VMEM)
SCALAR = pl.BlockSpec(memory_space=pltpu.SMEM)


def dot(a, b):
    return lax.dot_general(a, b, (((1,), (0,)), ((), ())), preferred_element_type=F32)


def dot_t(a, b):
    return lax.dot_general(a, b, (((1,), (1,)), ((), ())), preferred_element_type=F32)


def t_dot(a, b):
    return lax.dot_general(a, b, (((0,), (0,)), ((), ())), preferred_element_type=F32)


def call(kernel, outs, scratch, flops, *args, limit=VMEM_LIMIT):
    moved = sum(a.size * a.dtype.itemsize for a in args)
    moved += sum(math.prod(s) * jnp.dtype(d).itemsize for s, d in outs)
    return pl.pallas_call(
        kernel,
        out_shape=[jax.ShapeDtypeStruct(s, d) for s, d in outs],
        in_specs=[SCALAR if a.dtype == jnp.int32 and a.ndim == 1 else WHOLE for a in args],
        out_specs=[WHOLE] * len(outs),
        scratch_shapes=scratch,
        compiler_params=pltpu.CompilerParams(vmem_limit_bytes=limit),
        cost_estimate=pl.CostEstimate(flops=flops, bytes_accessed=moved, transcendentals=0),
    )(*args)


def by_core(core, first, second):
    return first + core * (second - first)


def spots(tm, count):
    near, far, rest, step = tm & 1, (tm >> 1) & 1, tm >> 2, count // 4
    return (2 * near + far) * step + rest, (2 * far + near) * step + rest


CARRY_ROWS = 8
LABEL_ROWS = 16


def scan(feat, forget):
    rows = feat.shape[0]
    keep, mass, weight = 1.0 - forget, forget * (feat * feat), forget
    row = lax.broadcasted_iota(jnp.int32, feat.shape, 0)
    step = 1
    while step < rows:
        inside = row >= step
        before = jnp.where(inside, pltpu.roll(mass, step, 0), 0.0)
        mass = keep * before + mass
        before = jnp.where(inside, pltpu.roll(weight, step, 0), 0.0)
        weight = keep * before + weight
        keep = keep * jnp.where(inside, pltpu.roll(keep, step, 0), 1.0)
        step *= 2
    return keep, mass, weight


def scan_kernel(feat_ref, forget_ref, keep_ref, mass_ref, weight_ref, carry_ref):
    rows, bands = feat_ref.shape
    values = scan(feat_ref[...], forget_ref[...])
    carry_ref[...] = jnp.zeros_like(carry_ref)
    for k, (ref, value) in enumerate(zip((keep_ref, mass_ref, weight_ref), values)):
        ref[...] = value
        rest = value[rows - 1 :]
        for part in range(3):
            rounded = rest.astype(BF16).astype(F32)
            carry_ref[part : part + 1, k * bands : (k + 1) * bands] = rounded
            rest = rest - rounded


def pack_kernel(scalar_ref, feat_ref, forget_ref, conv_ref, res_ref, in_ref, out_ref,
                keep_ref, mass_ref, weight_ref, pack_ref, carry_ref):
    scan_kernel(feat_ref, forget_ref, keep_ref, mass_ref, weight_ref, carry_ref)
    c = pack_ref.shape[1]
    cut, half, more = conv_ref.shape[1] * 3 // 4, res_ref.shape[1] // 2, in_ref.shape[0]

    def fill(across):
        cols = slice(across * c, (across + 1) * c)
        part = slice(across * half, (across + 1) * half)
        at = 0

        def put(value):
            nonlocal at
            pack_ref[at : at + value.shape[0], :] = value
            at += value.shape[0]

        put(conv_ref[0, :, cols])
        put(carry_ref[...].astype(BF16))
        put(conv_ref[1, :cut, cols])
        put(res_ref[0, part, :])
        if across:
            put(jnp.concatenate([out_ref[k * more : (k + 1) * more, :] for k in range(c // out_ref.shape[1])], axis=1))
        else:
            put(in_ref[...])
        put(res_ref[1, part, :])
        put(conv_ref[1, cut:, cols])

    pl.when(scalar_ref[1] == 0)(lambda: fill(0))
    pl.when(scalar_ref[1] == 1)(lambda: fill(1))


def norm_kernel(scalar_ref, feat_ref, keep_ref, mass_ref, weight_ref, carry_ref, label_ref, out_ref):
    bands = feat_ref.shape[1]
    mass0 = jnp.zeros((1, bands), F32)
    weight0 = jnp.zeros((1, bands), F32)
    for tm in range(carry_ref.shape[0]):
        first, second = spots(tm, carry_ref.shape[0])
        parts = carry_ref[by_core(scalar_ref[0], first, second)].astype(F32)
        value = (parts[0:1] + parts[1:2]) + parts[2:3]
        before = tm < scalar_ref[2]
        keep = value[:, :bands]
        mass0 = jnp.where(before, keep * mass0 + value[:, bands : 2 * bands], mass0)
        weight0 = jnp.where(before, keep * weight0 + value[:, 2 * bands : 3 * bands], weight0)
    keep = keep_ref[...]
    mass = keep * mass0 + mass_ref[...]
    weight = keep * weight0 + weight_ref[...]
    normed = (feat_ref[...] / jnp.sqrt(mass / weight + LEVEL_FLOOR)).astype(BF16)
    out_ref[LABEL_ROWS:, :] = normed
    out_ref[:LABEL_ROWS, :] = jnp.zeros((LABEL_ROWS, bands), BF16)
    out_ref[: label_ref.shape[0], :] = label_ref[...].astype(F32).astype(BF16)


def rows_of(value):
    return value.reshape(-1, value.shape[-1]).astype(BF16)


def halves(conv_ref, gate):
    half = conv_ref.shape[1] // 2
    return rows_of(conv_ref[gate, :half]), rows_of(conv_ref[gate, half:])


def place(core, pair, puts):
    for ref, own in zip(pair, (True, False)):
        s = core if own else 1 - core
        rest = ref.shape[0] // 8
        bits = rest.bit_length() - 1
        for steps in itertools.product((0, 1), repeat=3):
            base = (4 * steps[0] + 2 * steps[1] + steps[2]) * rest

            def put(p, _):
                high = sum(((p >> (bits - 1 - b)) & 1) << b for b in range(bits))
                puts(s, steps, high, ref, base + p)
                return 0

            if rest <= 2:
                for p in range(rest):
                    put(p, 0)
            else:
                lax.fori_loop(0, rest, put, 0)


def place_main(conv_ref, row):
    def put(s, steps, high, ref, k):
        third, second, first = steps
        across = by_core(s, third, second)
        tm = 4 * high + 2 * by_core(s, second, first) + by_core(s, first, third)
        conv_ref[across, 2 * tm + s, row : row + ref.shape[1], :] = ref[k].astype(conv_ref.dtype)

    return put


def place_side(layer, conv_ref, res_ref, *extra):
    def put(s, steps, high, ref, k):
        far, near, across = steps
        device = 2 * (4 * high + 2 * far + near) + s
        half = res_ref.shape[1] // 2
        res_ref[device, across * half : (across + 1) * half, :] = ref[k, :half, :].astype(res_ref.dtype)
        value = ref[k, half:, :]
        if layer == 1:
            conv_ref[across, device, conv_ref.shape[2] - value.shape[0] :, :] = value.astype(conv_ref.dtype)
            return
        in_ref, out_ref = extra
        value = value.astype(F32)
        if across == 0:
            in_ref[device] = value
            return
        count, classes = value.shape[0], out_ref.shape[2]
        for q in range(value.shape[1] // classes):
            out_ref[device, q * count : (q + 1) * count, :] = value[:, q * classes : (q + 1) * classes]

    return put


def activate(past, now, conv_ref):
    joined = jnp.concatenate([past, now], axis=1)
    t = jnp.tanh(dot(joined, rows_of(conv_ref[0])))
    s = 0.5 + 0.5 * jnp.tanh(0.5 * dot(joined, rows_of(conv_ref[1])))
    return t, s


def slopes(t, s):
    return s * (1.0 - t * t), t * s * (1.0 - s)


def tile_of(i, offset=0):
    return slice(i * TILE + offset, (i + 1) * TILE + offset)


def forward_first(before, steps, scalar_ref, norm_ref, a_ref, a2_ref, b_ref, b2_ref,
                  h1_ref, w_out_ref, kept_ref, gated_ref, slope_ref, conv_ref, res_ref,
                  h0_ref, in_ref, out_ref):
    rows = h0_ref.shape[0]
    kept = slope_ref.shape[1]
    d = rows - h1_ref.shape[0]
    core = scalar_ref[0]
    place(core, (a_ref, a2_ref), place_main(conv_ref, 0))
    place(core, (b_ref, b2_ref), place_side(0, conv_ref, res_ref, in_ref, out_ref))
    w_out_ref[...] = rows_of(out_ref[...])
    w_in = rows_of(in_ref[...])
    for i in range(rows // TILE):
        h0_ref[tile_of(i), :] = dot(norm_ref[tile_of(i), :], w_in).astype(BF16)
    kept_ref[...] = h0_ref[before : before + kept, :]
    for i in range(h1_ref.shape[0] // TILE):
        now = h0_ref[tile_of(i, d), :]
        t, s = activate(h0_ref[tile_of(i), :], now, conv_ref)
        gated = (t * s).astype(BF16)
        h1_ref[tile_of(i), :] = (now.astype(F32) + dot(gated, rows_of(res_ref[...]))).astype(BF16)
        first = i * TILE - before
        if 0 <= first < kept:
            own = slice(first, first + TILE)
            slope_ref[0, own, :], slope_ref[1, own, :] = (v.astype(BF16) for v in slopes(t, s))
            if first < steps:
                gated_ref[own, :] = gated


def store_terms(core, keep_ref, send_ref, row, value, first, size, start, count, lane=0):
    at = (slice(row, row + count), slice(lane, lane + value.shape[1]))
    for k in range(value.shape[0] // (2 * size)):
        low = value[2 * k * size + start : 2 * k * size + start + count]
        high = value[(2 * k + 1) * size + start : (2 * k + 1) * size + start + count]
        one, two = spots(first + k, keep_ref.shape[0])
        keep_ref[(by_core(core, one, two),) + at] = jnp.where(core == 0, low, high).astype(keep_ref.dtype)
        send_ref[(by_core(core, two, one),) + at] = jnp.where(core == 0, high, low).astype(send_ref.dtype)


def conv_terms(targets, first, size, value):
    c = value.shape[1] // 2
    store_terms(*targets, 0, value[:, :c], first, size, 0, size)
    store_terms(*targets, size, value[:, c:], first, size, 0, size)


def second_kernel(steps, scale, sizes, scalar_ref, h1_ref, w_out_ref, label_ref, a_ref, a2_ref, b_ref, b2_ref,
                  slope0_ref, res0_ref,
                  loss_ref, keep_ref, send_ref, grad0_ref, round0_ref, back0_ref,
                  back_ref, grad_ref, conv_ref, res_ref, gated_ref, h2_ref, lgrad_ref, round_ref):
    rows, c = back_ref.shape[0], grad_ref.shape[1]
    d = h1_ref.shape[0] - rows
    classes = w_out_ref.shape[1]
    conv, res, _, out = sizes
    core = scalar_ref[0]
    place(core, (a_ref, a2_ref), place_main(conv_ref, 0))
    place(core, (b_ref, b2_ref), place_side(1, conv_ref, res_ref))

    lanes = label_ref.shape[1]
    class_row = lax.broadcasted_iota(jnp.int32, (classes, lanes), 0).astype(F32)
    unit = class_row == lax.broadcasted_iota(jnp.int32, (lanes, lanes), 1).astype(F32)
    row = lax.broadcasted_iota(jnp.int32, (TILE, 1), 0)
    left = scalar_ref[3] - scalar_ref[2] * steps

    for i in range(rows // TILE):
        at = tile_of(i)
        now = h1_ref[tile_of(i, d), :]
        t, s = activate(h1_ref[at, :], now, conv_ref)
        gated = (t * s).astype(BF16)
        h2 = (now.astype(F32) + dot(gated, rows_of(res_ref[...]))).astype(BF16)
        logits = dot(h2, w_out_ref[...])
        total = jnp.log(jnp.sum(jnp.exp(logits), axis=1, keepdims=True))
        groups = range(i * TILE // lanes, (i + 1) * TILE // lanes)
        hot = jnp.concatenate(
            [(class_row == label_ref[k : k + 1, :].astype(F32)).astype(F32).T for k in groups])
        valid = (row + i * TILE < left).astype(F32)
        lgrad = ((jnp.exp(logits - total) - hot) * (valid * scale)).astype(BF16)
        grad = dot_t(lgrad, w_out_ref[...])
        rounded = grad.astype(BF16)
        back = dot_t(rounded, rows_of(res_ref[...]))
        filter_slope, gate_slope = slopes(t, s)
        back_ref[at, :c] = (back * filter_slope).astype(BF16)
        back_ref[at, c:] = (back * gate_slope).astype(BF16)
        if i * TILE < grad_ref.shape[0]:
            grad_ref[at, :] = grad
        if i * TILE < steps:
            loss = (total - jnp.sum(logits * hot, axis=1, keepdims=True)) * valid
            for j, k in enumerate(groups):
                part = jnp.where(unit, loss[j * lanes : (j + 1) * lanes], 0.0)
                loss_ref[k : k + 1, :] = jnp.sum(part, axis=0, keepdims=True)
            gated_ref[at, :] = gated
            h2_ref[at, :] = h2
            lgrad_ref[at, :] = lgrad
            round_ref[at, :] = rounded

    own = slice(0, steps)
    targets = (core, keep_ref, send_ref)
    for i in range(c // TILE):
        at = tile_of(i)
        first, per = i * (TILE // (2 * conv)), c // (2 * conv)
        conv_terms(targets, first, conv, t_dot(h1_ref[0:steps, at], back_ref[own, :]))
        conv_terms(targets, first + per, conv, t_dot(h1_ref[d : d + steps, at], back_ref[own, :]))
        value = t_dot(gated_ref[own, at], round_ref[own, :])
        store_terms(*targets, 2 * conv, value, i * (TILE // (2 * res)), res, 0, res)
        value = t_dot(h2_ref[own, at], lgrad_ref[own, :])
        count = out * classes // c
        for q in range(c // classes):
            store_terms(*targets, 2 * conv + res, value, i * (TILE // (2 * out)), out, q * count, count, q * classes)

    rows0 = back0_ref.shape[0]
    weights = halves(conv_ref, 0), halves(conv_ref, 1)
    for i in range(rows0 // TILE):
        at = tile_of(i)
        grad = grad_below(grad_ref[at, :], back_ref, i, rows - rows0, weights)
        rounded = grad.astype(BF16)
        back = dot_t(rounded, rows_of(res0_ref[...]))
        back0_ref[at, :c] = (back * slope0_ref[0, at, :].astype(F32)).astype(BF16)
        back0_ref[at, c:] = (back * slope0_ref[1, at, :].astype(F32)).astype(BF16)
        if i * TILE < steps:
            grad0_ref[at, :] = grad
            round0_ref[at, :] = rounded


def grad_below(grad, back_ref, i, d, weights):
    c = back_ref.shape[1] // 2
    (filt_past, filt_now), (gate_past, gate_now) = weights
    grad = grad + dot_t(back_ref[tile_of(i), :c], filt_now) + dot_t(back_ref[tile_of(i), c:], gate_now)
    return grad + dot_t(back_ref[tile_of(i, d), :c], filt_past) + dot_t(back_ref[tile_of(i, d), c:], gate_past)


def terms_first(sizes, scalar_ref, back_ref, grad_ref, round_ref, norm_ref, h0_ref, gated_ref, conv_ref,
                keep_ref, send_ref, last_ref):
    steps, c = grad_ref.shape
    d0 = back_ref.shape[0] - steps
    conv, res, enter, _ = sizes
    own = slice(0, steps)
    targets = (scalar_ref[0], keep_ref, send_ref)
    for i in range(c // TILE):
        at = tile_of(i)
        first, per = i * (TILE // (2 * conv)), c // (2 * conv)
        conv_terms(targets, first, conv, t_dot(h0_ref[0:steps, at], back_ref[own, :]))
        conv_terms(targets, first + per, conv, t_dot(h0_ref[d0 : d0 + steps, at], back_ref[own, :]))
        value = t_dot(gated_ref[:, at], round_ref[...])
        store_terms(*targets, 2 * conv, value, i * (TILE // (2 * res)), res, 0, res)
    weights = halves(conv_ref, 0), halves(conv_ref, 1)
    for i in range(steps // TILE):
        last_ref[tile_of(i), :] = grad_below(grad_ref[tile_of(i), :], back_ref, i, d0, weights).astype(BF16)
    value = t_dot(norm_ref[...], last_ref[...])
    store_terms(*targets, 2 * conv + res, value, 0, enter, 0, enter)


NEAR, FAR, ACROSS = ("tm", 0), ("tm", 1), ("groups", 0)
CORE = ("site", 0)


def swap(value, links):
    names = ("groups", "tm", "site")
    sizes = [lax.axis_size(name) for name in names]
    pairs = []
    for at in itertools.product(*(range(size) for size in sizes)):
        axis, bit = links[at[2]]
        to = tuple(i ^ (1 << bit) if name == axis else i for name, i in zip(names, at))
        pairs.append(tuple((p[0] * sizes[1] + p[1]) * sizes[2] + p[2] for p in (at, to)))
    return lax.ppermute(value, names, pairs)


def my_bit(links):
    first, second = ((lax.axis_index(axis) >> bit) & 1 for axis, bit in links)
    return jnp.where(lax.axis_index("site") == 0, first, second)


def time_bits():
    return lax.axis_size("tm").bit_length() - 1


def grow(held, links):
    other = swap(held, links)
    return jnp.where(
        my_bit(links) == 0, jnp.concatenate([held, other]), jnp.concatenate([other, held]))


def together(*values):
    return lax.optimization_barrier(values)


def sum_step(held, links, dim=0):
    mine = my_bit(links)
    other = swap(lax.dynamic_index_in_dim(held, 1 - mine, dim), links)
    return lax.dynamic_index_in_dim(held, mine, dim).astype(F32) + other.astype(F32)


def sum_steps():
    bits = time_bits()

    def first(held):
        return sum_step(held.reshape((2,) * bits + held.shape[1:]), (NEAR, FAR)).astype(BF16)

    def later(links, dim, last):
        def step(held):
            total = sum_step(held, links, dim)
            return total if last else total.astype(BF16)

        return step

    rest = [later((("tm", bit),) * 2, 1 + bits - bit, bit == bits - 1) for bit in range(2, bits)]
    return [first, later((FAR, NEAR), 1, not rest)] + rest


def hop(value, by):
    size = lax.axis_size("tm")
    return lax.ppermute(value, "tm", [(i, i + by) for i in range(size) if 0 <= i + by < size])


def rows_before(value, count):
    steps, parts, by = value.shape[0] - LABEL_ROWS, [], 1
    while count > 0:
        take = min(count, steps)
        parts.insert(0, hop(value[LABEL_ROWS + steps - take :], by))
        count, by = count - take, by + 1
    return parts


def rows_after(value, count):
    steps, parts, by = value.shape[0] - LABEL_ROWS, [], 1
    while count > 0:
        take = min(count, steps)
        parts.append(hop(value[: LABEL_ROWS + take], -by))
        count, by = count - take, by + 1
    return parts


def on_device(features, forget, labels, lengths, w_conv, w_res, w_in, w_out):
    _, steps, bands = features.shape
    time_devices, site_devices = lax.axis_size("tm"), lax.axis_size("site")
    devices = time_devices * site_devices
    c = w_res.shape[2]
    classes = w_out.shape[1]
    conv, res, enter, out = sizes = (w_conv.shape[1], w_res.shape[1], w_in.shape[0], w_out.shape[0])
    half, cut = res // 2, conv * 3 // 4
    aligned = conv % 64 == 0 and res % 32 == 0
    kind = BF16 if aligned else F32
    d0, d1 = BASE_DILATION, 2 * BASE_DILATION
    reach = d0 + d1
    across = my_bit((ACROSS, ACROSS))
    scalars = jnp.stack(
        [lax.axis_index("site"), across, lax.axis_index("tm"), lengths[0]]).astype(jnp.int32)

    block = ((steps, bands), F32)
    feat = features[0]
    if aligned:
        packed = 2 * (conv + half) + enter + CARRY_ROWS
        keep, mass, weight, held, _ = call(
            pack_kernel, [block] * 3 + [((packed, c), BF16), ((CARRY_ROWS, c), F32)], [], 40 * steps * bands,
            scalars, feat, forget[0], w_conv, w_res, w_in, w_out, limit=FIRST_LIMIT)
    else:
        keep, mass, weight, carry = call(
            scan_kernel, [block] * 3 + [((CARRY_ROWS, c), F32)], [], 40 * steps * bands, feat, forget[0])
        conv_own = jnp.where(across == 0, w_conv[:, :, :c], w_conv[:, :, c:])
        res_own = jnp.where(across == 0, w_res[:, :half], w_res[:, half:])
        out_own = jnp.concatenate([w_out[k * enter : (k + 1) * enter] for k in range(c // classes)], axis=1)
        held = jnp.concatenate([
            conv_own[0], carry.astype(BF16), conv_own[1, :cut], res_own[0],
            jnp.where(across == 0, w_in, out_own), res_own[1], conv_own[1, cut:]])
    held = held[None]
    for bit in reversed(range(2, time_bits())):
        held = grow(held, (("tm", bit),) * 2)

    main_links = [(NEAR, FAR), (FAR, ACROSS), (ACROSS, NEAR)]
    side_links = [(ACROSS, ACROSS), (NEAR, NEAR), (FAR, FAR)]
    ends = conv + CARRY_ROWS + cut
    main, side = held[:, :ends], held[:, ends:]
    main, side = grow(main, main_links[0]), grow(side, side_links[0])
    carry = main[:, conv : conv + CARRY_ROWS]
    main = jnp.concatenate([main[:, :conv], main[:, conv + CARRY_ROWS :]], axis=1)
    main, side, carry = together(main, side, carry)
    carry = grow(carry, (FAR, NEAR))
    main, side = grow(main, main_links[1]), grow(side, side_links[1])
    main, side, carry = together(main, side, carry)
    label_rows = steps // bands
    bits = time_bits()
    carry = carry.reshape((2,) * bits + (CARRY_ROWS, c))
    carry = carry.transpose((1, 0) + tuple(range(bits - 1, 1, -1)) + (bits, bits + 1))
    (normed,) = call(norm_kernel, [((LABEL_ROWS + steps, bands), BF16)], [], 10 * steps * bands,
                     scalars, feat, keep, mass, weight, carry.reshape(time_devices, CARRY_ROWS, c),
                     labels[0].reshape(label_rows, bands))
    main, side, normed = together(main, side, normed)
    first = [main[:, :conv], side[:, : half + enter]]
    second = [main[:, conv:], side[:, half + enter :]]

    def last_step(parts):
        return [grow(p, links[2]) for p, links in zip(parts, (main_links, side_links))]

    def both_cores(parts):
        return [v.astype(kind) for p in parts for v in (p, swap(p, (CORE, CORE)))]

    first = last_step(first)
    past, future = rows_before(normed, reach), rows_after(normed, reach)
    *first, second[0], second[1], past, future = together(*first, *second, past, future)
    own_normed = normed[LABEL_ROWS:]
    window = jnp.concatenate(past + [own_normed] + [v[LABEL_ROWS:] for v in future])
    label_window = jnp.concatenate(
        [v[: (v.shape[0] - LABEL_ROWS) // bands] for v in [normed] + future])
    first, second = both_cores(first), last_step(second)

    total_rows, rows0, rows1 = steps + 2 * reach, steps + d0, steps + reach
    conv_all, res_all = ((2, devices, conv, c), kind), ((devices, res, c), kind)
    V = pltpu.VMEM
    h1, out_all, h0, gated0, slope0, conv0, res0 = call(
        functools.partial(forward_first, d1, steps),
        [((total_rows - d0, c), BF16), ((c, classes), BF16), ((rows0, c), BF16), ((steps, c), BF16),
         ((2, rows0, c), BF16), conv_all, res_all],
        [V((total_rows, c), BF16), V((devices, enter, c), F32), V((devices, out, classes), F32)],
        2 * total_rows * c * (bands + 5 * c), scalars, window, *first)

    *second, h1 = together(*second, h1)
    second = both_cores(second)
    scale = 1.0 / math.sqrt(site_devices * steps * time_devices)
    package = [((time_devices, 2 * conv + res + enter, c), kind)] * 2
    loss, keep1, send1, grad1, round0, back0 = call(
        functools.partial(second_kernel, steps, scale, sizes),
        [((label_rows, bands), F32)] + package + [((steps, c), F32), ((steps, c), BF16), ((rows0, 2 * c), BF16)],
        [V((rows1, 2 * c), BF16), V((rows0, c), F32), V(*conv_all), V(*res_all),
         V((steps, c), BF16), V((steps, c), BF16), V((steps, classes), BF16), V((steps, c), BF16)],
        2 * rows1 * c * 6 * c + 2 * steps * 5 * c * c + 2 * rows0 * c * 5 * c,
        scalars, h1, out_all, label_window, *second, slope0, res0)

    def core_sum(keep, send):
        other = swap(send.astype(BF16), (CORE, CORE))
        return (keep.astype(F32) + other.astype(F32)).astype(BF16)

    sum1 = core_sum(keep1, send1)
    keep0, send0 = call(
        functools.partial(terms_first, sizes), package, [V((steps, c), BF16)],
        2 * steps * 9 * c * c, scalars, back0, grad1, round0, own_normed, h0, gated0, conv0)
    sum1, keep0, send0 = together(sum1, keep0, send0)

    chain1, chain0 = sum_steps(), [core_sum] + sum_steps()
    sum1, sum0 = chain1[0](sum1), chain0[0](keep0, send0)
    for step in range(1, len(chain0)):
        sum1, sum0 = together(sum1, sum0)
        if step < len(chain1):
            sum1 = chain1[step](sum1)
        sum0 = chain0[step](sum0)

    convs, ress, extras = [], [], []
    for held in (sum0, sum1):
        total = held.reshape(held.shape[-2:])
        convs.append(jnp.concatenate([total[:conv], total[conv : 2 * conv]], axis=1))
        ress.append(total[2 * conv : 2 * conv + res])
        extras.append(total[2 * conv + res :])
    grad_in, grad_out = extras
    return (
        loss.reshape(1, steps),
        jnp.stack(convs),
        jnp.stack(ress),
        grad_in,
        jnp.concatenate([grad_out[:, k * classes : (k + 1) * classes] for k in range(c // classes)]),
    )


def solution(mesh):
    return jax.shard_map(
        on_device,
        mesh=mesh,
        in_specs=(
            P(("groups", "site"), "tm", None),
            P(("groups", "site"), "tm", None),
            P(("groups", "site"), "tm"),
            P(("groups", "site")),
            P(None, ("tm", "site"), None),
            P(None, ("tm", "site"), None),
            P(("tm", "site"), None),
            P(("tm", "site"), None),
        ),
        out_specs=(
            P(("groups", "site"), "tm"),
            P("groups", ("tm", "site"), None),
            P("groups", ("tm", "site"), None),
            P(("tm", "site"), "groups"),
            P(("tm", "site"), "groups"),
        ),
        check_vma=False,
    )
```

```python
import functools
import itertools
import math

import jax
import jax.numpy as jnp
from jax import lax
from jax.experimental import pallas as pl
from jax.experimental.pallas import tpu as pltpu
from jax.sharding import PartitionSpec as P

BASE_DILATION = 256
LEVEL_FLOOR = 0.1
F32 = jnp.float32
BF16 = jnp.bfloat16
TILE = 256
VMEM_LIMIT = 24 * 1024 * 1024
FIRST_LIMIT = 56 * 1024 * 1024
WHOLE = pl.BlockSpec(memory_space=pltpu.VMEM)
SCALAR = pl.BlockSpec(memory_space=pltpu.SMEM)


def dot(a, b):
    return lax.dot_general(a, b, (((1,), (0,)), ((), ())), preferred_element_type=F32)


def dot_t(a, b):
    return lax.dot_general(a, b, (((1,), (1,)), ((), ())), preferred_element_type=F32)


def t_dot(a, b):
    return lax.dot_general(a, b, (((0,), (0,)), ((), ())), preferred_element_type=F32)


def call(kernel, outs, scratch, flops, *args, limit=VMEM_LIMIT):
    moved = sum(a.size * a.dtype.itemsize for a in args)
    moved += sum(math.prod(s) * jnp.dtype(d).itemsize for s, d in outs)
    return pl.pallas_call(
        kernel,
        out_shape=[jax.ShapeDtypeStruct(s, d) for s, d in outs],
        in_specs=[SCALAR if a.dtype == jnp.int32 and a.ndim == 1 else WHOLE for a in args],
        out_specs=[WHOLE] * len(outs),
        scratch_shapes=scratch,
        compiler_params=pltpu.CompilerParams(vmem_limit_bytes=limit),
        cost_estimate=pl.CostEstimate(flops=flops, bytes_accessed=moved, transcendentals=0),
    )(*args)


def by_core(core, first, second):
    return first + core * (second - first)


def spots(tm, count):
    near, far, rest, step = tm & 1, (tm >> 1) & 1, tm >> 2, count // 4
    return (2 * near + far) * step + rest, (2 * far + near) * step + rest


LABEL_ROWS = 16


def scan(feat, forget):
    rows = feat.shape[0]
    keep, mass, weight = 1.0 - forget, forget * (feat * feat), forget
    row = lax.broadcasted_iota(jnp.int32, feat.shape, 0)
    step = 1
    while step < rows:
        inside = row >= step
        before = jnp.where(inside, pltpu.roll(mass, step, 0), 0.0)
        mass = keep * before + mass
        before = jnp.where(inside, pltpu.roll(weight, step, 0), 0.0)
        weight = keep * before + weight
        keep = keep * jnp.where(inside, pltpu.roll(keep, step, 0), 1.0)
        step *= 2
    return keep, mass, weight


def scan_kernel(feat_ref, forget_ref, keep_ref, mass_ref, weight_ref, carry_ref):
    rows = feat_ref.shape[0]
    values = scan(feat_ref[...], forget_ref[...])
    for k, (ref, value) in enumerate(zip((keep_ref, mass_ref, weight_ref), values)):
        ref[...] = value
        carry_ref[k : k + 1, :] = value[rows - 1 :]


def pack_kernel(scalar_ref, conv_ref, res_ref, in_ref, out_ref, pack_ref):
    c = pack_ref.shape[1]
    cut, half, more = conv_ref.shape[1] * 3 // 4, res_ref.shape[1] // 2, in_ref.shape[0]

    def fill(across):
        cols = slice(across * c, (across + 1) * c)
        part = slice(across * half, (across + 1) * half)
        at = 0

        def put(value):
            nonlocal at
            pack_ref[at : at + value.shape[0], :] = value
            at += value.shape[0]

        put(conv_ref[0, :, cols])
        put(conv_ref[1, :cut, cols])
        put(res_ref[0, part, :])
        if across:
            put(jnp.concatenate([out_ref[k * more : (k + 1) * more, :] for k in range(c // out_ref.shape[1])], axis=1))
        else:
            put(in_ref[...])
        put(res_ref[1, part, :])
        put(conv_ref[1, cut:, cols])

    pl.when(scalar_ref[1] == 0)(lambda: fill(0))
    pl.when(scalar_ref[1] == 1)(lambda: fill(1))


def norm_kernel(scalar_ref, feat_ref, keep_ref, mass_ref, weight_ref, carry_ref, label_ref, out_ref):
    bands = feat_ref.shape[1]
    mass0 = jnp.zeros((1, bands), F32)
    weight0 = jnp.zeros((1, bands), F32)
    for tm in range(carry_ref.shape[0]):
        before = tm < scalar_ref[2]
        keep, mass, weight = (carry_ref[tm, k : k + 1, :] for k in range(3))
        mass0 = jnp.where(before, keep * mass0 + mass, mass0)
        weight0 = jnp.where(before, keep * weight0 + weight, weight0)
    keep = keep_ref[...]
    mass = keep * mass0 + mass_ref[...]
    weight = keep * weight0 + weight_ref[...]
    normed = (feat_ref[...] / jnp.sqrt(mass / weight + LEVEL_FLOOR)).astype(BF16)
    out_ref[LABEL_ROWS:, :] = normed
    out_ref[:LABEL_ROWS, :] = jnp.zeros((LABEL_ROWS, bands), BF16)
    out_ref[: label_ref.shape[0], :] = label_ref[...].astype(F32).astype(BF16)


def rows_of(value):
    return value.reshape(-1, value.shape[-1]).astype(BF16)


def halves(conv_ref, gate):
    half = conv_ref.shape[1] // 2
    return rows_of(conv_ref[gate, :half]), rows_of(conv_ref[gate, half:])


def place(core, pair, puts):
    for ref, own in zip(pair, (True, False)):
        s = core if own else 1 - core
        rest = ref.shape[0] // 8
        bits = rest.bit_length() - 1
        for steps in itertools.product((0, 1), repeat=3):
            base = (4 * steps[0] + 2 * steps[1] + steps[2]) * rest

            def put(p, _):
                high = sum(((p >> (bits - 1 - b)) & 1) << b for b in range(bits))
                puts(s, steps, high, ref, base + p)
                return 0

            if rest <= 2:
                for p in range(rest):
                    put(p, 0)
            else:
                lax.fori_loop(0, rest, put, 0)


def place_main(conv_ref, row):
    def put(s, steps, high, ref, k):
        third, second, first = steps
        across = by_core(s, third, second)
        tm = 4 * high + 2 * by_core(s, second, first) + by_core(s, first, third)
        conv_ref[across, 2 * tm + s, row : row + ref.shape[1], :] = ref[k].astype(conv_ref.dtype)

    return put


def place_side(layer, conv_ref, res_ref, *extra):
    def put(s, steps, high, ref, k):
        far, near, across = steps
        device = 2 * (4 * high + 2 * far + near) + s
        half = res_ref.shape[1] // 2
        res_ref[device, across * half : (across + 1) * half, :] = ref[k, :half, :].astype(res_ref.dtype)
        value = ref[k, half:, :]
        if layer == 1:
            conv_ref[across, device, conv_ref.shape[2] - value.shape[0] :, :] = value.astype(conv_ref.dtype)
            return
        in_ref, out_ref = extra
        value = value.astype(F32)
        if across == 0:
            in_ref[device] = value
            return
        count, classes = value.shape[0], out_ref.shape[2]
        for q in range(value.shape[1] // classes):
            out_ref[device, q * count : (q + 1) * count, :] = value[:, q * classes : (q + 1) * classes]

    return put


def activate(past, now, conv_ref):
    joined = jnp.concatenate([past, now], axis=1)
    t = jnp.tanh(dot(joined, rows_of(conv_ref[0])))
    s = 0.5 + 0.5 * jnp.tanh(0.5 * dot(joined, rows_of(conv_ref[1])))
    return t, s


def slopes(t, s):
    return s * (1.0 - t * t), t * s * (1.0 - s)


def tile_of(i, offset=0):
    return slice(i * TILE + offset, (i + 1) * TILE + offset)


def forward_first(before, steps, scalar_ref, norm_ref, a_ref, a2_ref, b_ref, b2_ref,
                  h1_ref, w_out_ref, kept_ref, gated_ref, slope_ref, conv_ref, res_ref,
                  h0_ref, in_ref, out_ref):
    rows = h0_ref.shape[0]
    kept = slope_ref.shape[1]
    d = rows - h1_ref.shape[0]
    core = scalar_ref[0]
    place(core, (a_ref, a2_ref), place_main(conv_ref, 0))
    place(core, (b_ref, b2_ref), place_side(0, conv_ref, res_ref, in_ref, out_ref))
    w_out_ref[...] = rows_of(out_ref[...])
    w_in = rows_of(in_ref[...])
    for i in range(rows // TILE):
        h0_ref[tile_of(i), :] = dot(norm_ref[tile_of(i), :], w_in).astype(BF16)
    kept_ref[...] = h0_ref[before : before + kept, :]
    for i in range(h1_ref.shape[0] // TILE):
        now = h0_ref[tile_of(i, d), :]
        t, s = activate(h0_ref[tile_of(i), :], now, conv_ref)
        gated = (t * s).astype(BF16)
        h1_ref[tile_of(i), :] = (now.astype(F32) + dot(gated, rows_of(res_ref[...]))).astype(BF16)
        first = i * TILE - before
        if 0 <= first < kept:
            own = slice(first, first + TILE)
            slope_ref[0, own, :], slope_ref[1, own, :] = (v.astype(BF16) for v in slopes(t, s))
            if first < steps:
                gated_ref[own, :] = gated


def store_terms(core, keep_ref, send_ref, row, value, first, size, start, count, lane=0):
    at = (slice(row, row + count), slice(lane, lane + value.shape[1]))
    for k in range(value.shape[0] // (2 * size)):
        low = value[2 * k * size + start : 2 * k * size + start + count]
        high = value[(2 * k + 1) * size + start : (2 * k + 1) * size + start + count]
        one, two = spots(first + k, keep_ref.shape[0])
        keep_ref[(by_core(core, one, two),) + at] = jnp.where(core == 0, low, high).astype(keep_ref.dtype)
        send_ref[(by_core(core, two, one),) + at] = jnp.where(core == 0, high, low).astype(send_ref.dtype)


def conv_terms(targets, first, size, value):
    c = value.shape[1] // 2
    store_terms(*targets, 0, value[:, :c], first, size, 0, size)
    store_terms(*targets, size, value[:, c:], first, size, 0, size)


def second_kernel(steps, scale, sizes, scalar_ref, h1_ref, w_out_ref, label_ref, a_ref, a2_ref, b_ref, b2_ref,
                  slope0_ref, res0_ref,
                  loss_ref, keep_ref, send_ref, grad0_ref, round0_ref, back0_ref,
                  back_ref, grad_ref, conv_ref, res_ref, gated_ref, h2_ref, lgrad_ref, round_ref):
    rows, c = back_ref.shape[0], grad_ref.shape[1]
    d = h1_ref.shape[0] - rows
    classes = w_out_ref.shape[1]
    conv, res, _, out = sizes
    core = scalar_ref[0]
    place(core, (a_ref, a2_ref), place_main(conv_ref, 0))
    place(core, (b_ref, b2_ref), place_side(1, conv_ref, res_ref))

    lanes = label_ref.shape[1]
    class_row = lax.broadcasted_iota(jnp.int32, (classes, lanes), 0).astype(F32)
    unit = class_row == lax.broadcasted_iota(jnp.int32, (lanes, lanes), 1).astype(F32)
    row = lax.broadcasted_iota(jnp.int32, (TILE, 1), 0)
    left = scalar_ref[3] - scalar_ref[2] * steps

    for i in range(rows // TILE):
        at = tile_of(i)
        now = h1_ref[tile_of(i, d), :]
        t, s = activate(h1_ref[at, :], now, conv_ref)
        gated = (t * s).astype(BF16)
        h2 = (now.astype(F32) + dot(gated, rows_of(res_ref[...]))).astype(BF16)
        logits = dot(h2, w_out_ref[...])
        total = jnp.log(jnp.sum(jnp.exp(logits), axis=1, keepdims=True))
        groups = range(i * TILE // lanes, (i + 1) * TILE // lanes)
        hot = jnp.concatenate(
            [(class_row == label_ref[k : k + 1, :].astype(F32)).astype(F32).T for k in groups])
        valid = (row + i * TILE < left).astype(F32)
        lgrad = ((jnp.exp(logits - total) - hot) * (valid * scale)).astype(BF16)
        grad = dot_t(lgrad, w_out_ref[...])
        rounded = grad.astype(BF16)
        back = dot_t(rounded, rows_of(res_ref[...]))
        filter_slope, gate_slope = slopes(t, s)
        back_ref[at, :c] = (back * filter_slope).astype(BF16)
        back_ref[at, c:] = (back * gate_slope).astype(BF16)
        if i * TILE < grad_ref.shape[0]:
            grad_ref[at, :] = grad
        if i * TILE < steps:
            loss = (total - jnp.sum(logits * hot, axis=1, keepdims=True)) * valid
            for j, k in enumerate(groups):
                part = jnp.where(unit, loss[j * lanes : (j + 1) * lanes], 0.0)
                loss_ref[k : k + 1, :] = jnp.sum(part, axis=0, keepdims=True)
            gated_ref[at, :] = gated
            h2_ref[at, :] = h2
            lgrad_ref[at, :] = lgrad
            round_ref[at, :] = rounded

    own = slice(0, steps)
    targets = (core, keep_ref, send_ref)
    for i in range(c // TILE):
        at = tile_of(i)
        first, per = i * (TILE // (2 * conv)), c // (2 * conv)
        conv_terms(targets, first, conv, t_dot(h1_ref[0:steps, at], back_ref[own, :]))
        conv_terms(targets, first + per, conv, t_dot(h1_ref[d : d + steps, at], back_ref[own, :]))
        value = t_dot(gated_ref[own, at], round_ref[own, :])
        store_terms(*targets, 2 * conv, value, i * (TILE // (2 * res)), res, 0, res)
        value = t_dot(h2_ref[own, at], lgrad_ref[own, :])
        count = out * classes // c
        for q in range(c // classes):
            store_terms(*targets, 2 * conv + res, value, i * (TILE // (2 * out)), out, q * count, count, q * classes)

    rows0 = back0_ref.shape[0]
    weights = halves(conv_ref, 0), halves(conv_ref, 1)
    for i in range(rows0 // TILE):
        at = tile_of(i)
        grad = grad_below(grad_ref[at, :], back_ref, i, rows - rows0, weights)
        rounded = grad.astype(BF16)
        back = dot_t(rounded, rows_of(res0_ref[...]))
        back0_ref[at, :c] = (back * slope0_ref[0, at, :].astype(F32)).astype(BF16)
        back0_ref[at, c:] = (back * slope0_ref[1, at, :].astype(F32)).astype(BF16)
        if i * TILE < steps:
            grad0_ref[at, :] = grad
            round0_ref[at, :] = rounded


def grad_below(grad, back_ref, i, d, weights):
    c = back_ref.shape[1] // 2
    (filt_past, filt_now), (gate_past, gate_now) = weights
    grad = grad + dot_t(back_ref[tile_of(i), :c], filt_now) + dot_t(back_ref[tile_of(i), c:], gate_now)
    return grad + dot_t(back_ref[tile_of(i, d), :c], filt_past) + dot_t(back_ref[tile_of(i, d), c:], gate_past)


def terms_first(sizes, scalar_ref, back_ref, grad_ref, round_ref, norm_ref, h0_ref, gated_ref, conv_ref,
                keep_ref, send_ref, last_ref):
    steps, c = grad_ref.shape
    d0 = back_ref.shape[0] - steps
    conv, res, enter, _ = sizes
    own = slice(0, steps)
    targets = (scalar_ref[0], keep_ref, send_ref)
    for i in range(c // TILE):
        at = tile_of(i)
        first, per = i * (TILE // (2 * conv)), c // (2 * conv)
        conv_terms(targets, first, conv, t_dot(h0_ref[0:steps, at], back_ref[own, :]))
        conv_terms(targets, first + per, conv, t_dot(h0_ref[d0 : d0 + steps, at], back_ref[own, :]))
        value = t_dot(gated_ref[:, at], round_ref[...])
        store_terms(*targets, 2 * conv, value, i * (TILE // (2 * res)), res, 0, res)
    weights = halves(conv_ref, 0), halves(conv_ref, 1)
    for i in range(steps // TILE):
        last_ref[tile_of(i), :] = grad_below(grad_ref[tile_of(i), :], back_ref, i, d0, weights).astype(BF16)
    value = t_dot(norm_ref[...], last_ref[...])
    store_terms(*targets, 2 * conv + res, value, 0, enter, 0, enter)


def finish_kernel(sizes, one0_ref, two0_ref, one1_ref, two1_ref, conv_ref, res_ref, in_ref, out_ref):
    conv, res, _, _ = sizes
    for layer, (one, two) in enumerate(((one0_ref, two0_ref), (one1_ref, two1_ref))):
        total = one[...].astype(F32) + two[...].astype(F32)
        c = total.shape[1]
        conv_ref[layer, :, :c] = total[:conv]
        conv_ref[layer, :, c:] = total[conv : 2 * conv]
        res_ref[layer] = total[2 * conv : 2 * conv + res]
        rest = total[2 * conv + res :]
        if layer == 0:
            in_ref[...] = rest
        else:
            count, classes = rest.shape[0], out_ref.shape[1]
            for q in range(c // classes):
                out_ref[q * count : (q + 1) * count, :] = rest[:, q * classes : (q + 1) * classes]


NEAR, FAR, ACROSS = ("tm", 0), ("tm", 1), ("groups", 0)
CORE = ("site", 0)


def swap(value, links):
    names = ("groups", "tm", "site")
    sizes = [lax.axis_size(name) for name in names]
    pairs = []
    for at in itertools.product(*(range(size) for size in sizes)):
        axis, bit = links[at[2]]
        to = tuple(i ^ (1 << bit) if name == axis else i for name, i in zip(names, at))
        pairs.append(tuple((p[0] * sizes[1] + p[1]) * sizes[2] + p[2] for p in (at, to)))
    return lax.ppermute(value, names, pairs)


def my_bit(links):
    first, second = ((lax.axis_index(axis) >> bit) & 1 for axis, bit in links)
    return jnp.where(lax.axis_index("site") == 0, first, second)


def time_bits():
    return lax.axis_size("tm").bit_length() - 1


def arranged(held, other, links):
    return jnp.where(
        my_bit(links) == 0, jnp.concatenate([held, other]), jnp.concatenate([other, held]))


def grow(held, links):
    return arranged(held, swap(held, links), links)


def together(*values):
    return lax.optimization_barrier(values)


def sum_step(addends, links, dim):
    mine = my_bit(links)

    def half(index):
        one, two = (lax.dynamic_index_in_dim(v, index, dim).astype(F32) for v in addends)
        return (one + two).astype(BF16)

    return half(mine), swap(half(1 - mine), links)


def sum_steps():
    bits = time_bits()
    rest = [((("tm", bit),) * 2, 1 + bits - bit) for bit in range(2, bits)]
    return [((NEAR, FAR), 0), ((FAR, NEAR), 1)] + rest


def hop(value, by):
    size = lax.axis_size("tm")
    return lax.ppermute(value, "tm", [(i, i + by) for i in range(size) if 0 <= i + by < size])


def rows_before(value, count):
    steps, parts, by = value.shape[0] - LABEL_ROWS, [], 1
    while count > 0:
        take = min(count, steps)
        parts.insert(0, hop(value[LABEL_ROWS + steps - take :], by))
        count, by = count - take, by + 1
    return parts


def rows_after(value, count):
    steps, parts, by = value.shape[0] - LABEL_ROWS, [], 1
    while count > 0:
        take = min(count, steps)
        parts.append(hop(value[: LABEL_ROWS + take], -by))
        count, by = count - take, by + 1
    return parts


def on_device(features, forget, labels, lengths, w_conv, w_res, w_in, w_out):
    _, steps, bands = features.shape
    time_devices, site_devices = lax.axis_size("tm"), lax.axis_size("site")
    devices = time_devices * site_devices
    c = w_res.shape[2]
    classes = w_out.shape[1]
    conv, res, enter, out = sizes = (w_conv.shape[1], w_res.shape[1], w_in.shape[0], w_out.shape[0])
    half, cut = res // 2, conv * 3 // 4
    aligned = conv % 64 == 0 and res % 32 == 0
    kind = BF16 if aligned else F32
    d0, d1 = BASE_DILATION, 2 * BASE_DILATION
    reach = d0 + d1
    across = my_bit((ACROSS, ACROSS))
    scalars = jnp.stack(
        [lax.axis_index("site"), across, lax.axis_index("tm"), lengths[0]]).astype(jnp.int32)

    if aligned:
        (held,) = call(pack_kernel, [((2 * (conv + half) + enter, c), BF16)], [], 1,
                       scalars, w_conv, w_res, w_in, w_out, limit=FIRST_LIMIT)
    else:
        conv_own = jnp.where(across == 0, w_conv[:, :, :c], w_conv[:, :, c:])
        res_own = jnp.where(across == 0, w_res[:, :half], w_res[:, half:])
        out_own = jnp.concatenate([w_out[k * enter : (k + 1) * enter] for k in range(c // classes)], axis=1)
        held = jnp.concatenate([
            conv_own[0], conv_own[1, :cut], res_own[0],
            jnp.where(across == 0, w_in, out_own), res_own[1], conv_own[1, cut:]])
    held, feat, forget = together(held[None], features[0], forget[0])
    block = ((steps, bands), F32)
    keep, mass, weight, carry = call(
        scan_kernel, [block] * 3 + [((3, bands), F32)], [], 40 * steps * bands, feat, forget, limit=FIRST_LIMIT)
    carry = carry[None]
    for bit in reversed(range(2, time_bits())):
        held = grow(held, (("tm", bit),) * 2)
    for bit in range(2):
        carry = grow(carry, (("tm", bit),) * 2)
    held, carry = together(held, carry)

    main_links = [(NEAR, FAR), (FAR, ACROSS), (ACROSS, NEAR)]
    side_links = [(ACROSS, ACROSS), (NEAR, NEAR), (FAR, FAR)]
    main, side = held[:, : conv + cut], held[:, conv + cut :]
    main, side = grow(main, main_links[0]), grow(side, side_links[0])
    for bit in range(2, time_bits()):
        carry = grow(carry, (("tm", bit),) * 2)
    label_rows = steps // bands
    (normed,) = call(norm_kernel, [((LABEL_ROWS + steps, bands), BF16)], [], 10 * steps * bands,
                     scalars, feat, keep, mass, weight, carry, labels[0].reshape(label_rows, bands))
    main, side, normed = together(main, side, normed)
    main, side = grow(main, main_links[1]), grow(side, side_links[1])
    past, future = rows_before(normed, reach), rows_after(normed, reach)
    main, side, past, future = together(main, side, past, future)
    first = [main[:, :conv], side[:, : half + enter]]
    second = [main[:, conv:], side[:, half + enter :]]

    last_links = (main_links[2], side_links[2])

    def both_cores(parts):
        return [v.astype(kind) for p in parts for v in (p, swap(p, (CORE, CORE)))]

    first = [grow(p, links) for p, links in zip(first, last_links)]
    *first, second[0], second[1] = together(*first, *second)
    own_normed = normed[LABEL_ROWS:]
    window = jnp.concatenate(past + [own_normed] + [v[LABEL_ROWS:] for v in future])
    label_window = jnp.concatenate(
        [v[: (v.shape[0] - LABEL_ROWS) // bands] for v in [normed] + future])
    first, others = both_cores(first), [swap(p, links) for p, links in zip(second, last_links)]

    total_rows, rows0, rows1 = steps + 2 * reach, steps + d0, steps + reach
    conv_all, res_all = ((2, devices, conv, c), kind), ((devices, res, c), kind)
    V = pltpu.VMEM
    h1, out_all, h0, gated0, slope0, conv0, res0 = call(
        functools.partial(forward_first, d1, steps),
        [((total_rows - d0, c), BF16), ((c, classes), BF16), ((rows0, c), BF16), ((steps, c), BF16),
         ((2, rows0, c), BF16), conv_all, res_all],
        [V((total_rows, c), BF16), V((devices, enter, c), F32), V((devices, out, classes), F32)],
        2 * total_rows * c * (bands + 5 * c), scalars, window, *first)

    others[0], others[1], h1 = together(*others, h1)
    second = both_cores([arranged(*v) for v in zip(second, others, last_links)])
    scale = 1.0 / math.sqrt(site_devices * steps * time_devices)
    package = [((time_devices, 2 * conv + res + enter, c), kind)] * 2
    loss, keep1, send1, grad1, round0, back0 = call(
        functools.partial(second_kernel, steps, scale, sizes),
        [((label_rows, bands), F32)] + package + [((steps, c), F32), ((steps, c), BF16), ((rows0, 2 * c), BF16)],
        [V((rows1, 2 * c), BF16), V((rows0, c), F32), V(*conv_all), V(*res_all),
         V((steps, c), BF16), V((steps, c), BF16), V((steps, classes), BF16), V((steps, c), BF16)],
        2 * rows1 * c * 6 * c + 2 * steps * 5 * c * c + 2 * rows0 * c * 5 * c,
        scalars, h1, out_all, label_window, *second, slope0, res0)

    def core_step(keep, send):
        other = swap(send.astype(BF16), (CORE, CORE))
        shape = (2,) * time_bits() + keep.shape[1:]
        return keep.reshape(shape), other.reshape(shape)

    sums1 = core_step(keep1, send1)
    keep0, send0 = call(
        functools.partial(terms_first, sizes), package, [V((steps, c), BF16)],
        2 * steps * 9 * c * c, scalars, back0, grad1, round0, own_normed, h0, gated0, conv0)
    sums1, keep0, send0 = together(sums1, keep0, send0)

    order = sum_steps()
    sums1, sums0 = sum_step(sums1, *order[0]), core_step(keep0, send0)
    for step in range(len(order)):
        sums1, sums0 = together(sums1, sums0)
        if step + 1 < len(order):
            sums1 = sum_step(sums1, *order[step + 1])
        sums0 = sum_step(sums0, *order[step])
    rows = 2 * conv + res + enter
    grad_conv, grad_res, grad_in, grad_out = call(
        functools.partial(finish_kernel, sizes),
        [((2, conv, 2 * c), F32), ((2, res, c), F32), ((enter, c), F32), ((out, classes), F32)], [], 1,
        *(v.reshape(rows, c) for v in sums0 + sums1))
    return loss.reshape(1, steps), grad_conv, grad_res, grad_in, grad_out


def solution(mesh):
    return jax.shard_map(
        on_device,
        mesh=mesh,
        in_specs=(
            P(("groups", "site"), "tm", None),
            P(("groups", "site"), "tm", None),
            P(("groups", "site"), "tm"),
            P(("groups", "site")),
            P(None, ("tm", "site"), None),
            P(None, ("tm", "site"), None),
            P(("tm", "site"), None),
            P(("tm", "site"), None),
        ),
        out_specs=(
            P(("groups", "site"), "tm"),
            P("groups", ("tm", "site"), None),
            P("groups", ("tm", "site"), None),
            P(("tm", "site"), "groups"),
            P(("tm", "site"), "groups"),
        ),
        check_vma=False,
    )
```

```python
import functools
import itertools
import math

import jax
import jax.numpy as jnp
from jax import lax
from jax.experimental import pallas as pl
from jax.experimental.pallas import tpu as pltpu
from jax.sharding import PartitionSpec as P

BASE_DILATION = 256
LEVEL_FLOOR = 0.1
F32 = jnp.float32
BF16 = jnp.bfloat16
TILE = 256
VMEM_LIMIT = 24 * 1024 * 1024
FIRST_LIMIT = 56 * 1024 * 1024
WHOLE = pl.BlockSpec(memory_space=pltpu.VMEM)
SCALAR = pl.BlockSpec(memory_space=pltpu.SMEM)


def dot(a, b):
    return lax.dot_general(a, b, (((1,), (0,)), ((), ())), preferred_element_type=F32)


def dot_t(a, b):
    return lax.dot_general(a, b, (((1,), (1,)), ((), ())), preferred_element_type=F32)


def t_dot(a, b):
    return lax.dot_general(a, b, (((0,), (0,)), ((), ())), preferred_element_type=F32)


def call(kernel, outs, scratch, flops, *args, limit=VMEM_LIMIT):
    moved = sum(a.size * a.dtype.itemsize for a in args)
    moved += sum(math.prod(s) * jnp.dtype(d).itemsize for s, d in outs)
    return pl.pallas_call(
        kernel,
        out_shape=[jax.ShapeDtypeStruct(s, d) for s, d in outs],
        in_specs=[SCALAR if a.dtype == jnp.int32 and a.ndim == 1 else WHOLE for a in args],
        out_specs=[WHOLE] * len(outs),
        scratch_shapes=scratch,
        compiler_params=pltpu.CompilerParams(vmem_limit_bytes=limit),
        cost_estimate=pl.CostEstimate(flops=flops, bytes_accessed=moved, transcendentals=0),
    )(*args)


def by_core(core, first, second):
    return first + core * (second - first)


def spots(tm, count):
    near, far, rest, step = tm & 1, (tm >> 1) & 1, tm >> 2, count // 4
    return (2 * near + far) * step + rest, (2 * far + near) * step + rest


LABEL_ROWS = 16


def scan(feat, forget):
    rows = feat.shape[0]
    keep, mass, weight = 1.0 - forget, forget * (feat * feat), forget
    row = lax.broadcasted_iota(jnp.int32, feat.shape, 0)
    step = 1
    while step < rows:
        inside = row >= step
        before = jnp.where(inside, pltpu.roll(mass, step, 0), 0.0)
        mass = keep * before + mass
        before = jnp.where(inside, pltpu.roll(weight, step, 0), 0.0)
        weight = keep * before + weight
        keep = keep * jnp.where(inside, pltpu.roll(keep, step, 0), 1.0)
        step *= 2
    return keep, mass, weight


def scan_kernel(feat_ref, forget_ref, keep_ref, mass_ref, weight_ref, carry_ref):
    rows = feat_ref.shape[0]
    values = scan(feat_ref[...], forget_ref[...])
    for k, (ref, value) in enumerate(zip((keep_ref, mass_ref, weight_ref), values)):
        ref[...] = value
        carry_ref[k : k + 1, :] = value[rows - 1 :]


def pack_kernel(scalar_ref, conv_ref, res_ref, in_ref, out_ref, pack_ref):
    c = pack_ref.shape[1]
    cut, half, more = conv_ref.shape[1] * 3 // 4, res_ref.shape[1] // 2, in_ref.shape[0]

    def fill(across):
        cols = slice(across * c, (across + 1) * c)
        part = slice(across * half, (across + 1) * half)
        at = 0

        def put(value):
            nonlocal at
            pack_ref[at : at + value.shape[0], :] = value
            at += value.shape[0]

        put(conv_ref[0, :, cols])
        put(conv_ref[1, :cut, cols])
        put(res_ref[0, part, :])
        if across:
            put(jnp.concatenate([out_ref[k * more : (k + 1) * more, :] for k in range(c // out_ref.shape[1])], axis=1))
        else:
            put(in_ref[...])
        put(res_ref[1, part, :])
        put(conv_ref[1, cut:, cols])

    pl.when(scalar_ref[1] == 0)(lambda: fill(0))
    pl.when(scalar_ref[1] == 1)(lambda: fill(1))


def norm_kernel(scalar_ref, feat_ref, keep_ref, mass_ref, weight_ref, carry_ref, label_ref, out_ref, low_ref, high_ref):
    bands = feat_ref.shape[1]
    mass0 = jnp.zeros((1, bands), F32)
    weight0 = jnp.zeros((1, bands), F32)
    for tm in range(carry_ref.shape[0]):
        before = tm < scalar_ref[2]
        keep, mass, weight = (carry_ref[tm, k : k + 1, :] for k in range(3))
        mass0 = jnp.where(before, keep * mass0 + mass, mass0)
        weight0 = jnp.where(before, keep * weight0 + weight, weight0)
    keep = keep_ref[...]
    mass = keep * mass0 + mass_ref[...]
    weight = keep * weight0 + weight_ref[...]
    normed = (feat_ref[...] / jnp.sqrt(mass / weight + LEVEL_FLOOR)).astype(BF16)
    label = jnp.concatenate(
        [label_ref[...].astype(F32), jnp.zeros((LABEL_ROWS - label_ref.shape[0], bands), F32)]).astype(BF16)
    part = low_ref.shape[0] - LABEL_ROWS
    first, last = normed[:part], normed[normed.shape[0] - part :]
    upper = (scalar_ref[2] >> 1) & 1 == 1
    for ref, value in (
        (out_ref, normed), (low_ref, jnp.where(upper, first, last)), (high_ref, jnp.where(upper, last, first))):
        ref[:LABEL_ROWS, :] = label
        ref[LABEL_ROWS:, :] = value


def rows_of(value):
    return value.reshape(-1, value.shape[-1]).astype(BF16)


def halves(conv_ref, gate):
    half = conv_ref.shape[1] // 2
    return rows_of(conv_ref[gate, :half]), rows_of(conv_ref[gate, half:])


def place(core, pair, puts):
    for ref, own in zip(pair, (True, False)):
        s = core if own else 1 - core
        rest = ref.shape[0] // 8
        bits = rest.bit_length() - 1
        for steps in itertools.product((0, 1), repeat=3):
            base = (4 * steps[0] + 2 * steps[1] + steps[2]) * rest

            def put(p, _):
                high = sum(((p >> (bits - 1 - b)) & 1) << b for b in range(bits))
                puts(s, steps, high, ref, base + p)
                return 0

            if rest <= 2:
                for p in range(rest):
                    put(p, 0)
            else:
                lax.fori_loop(0, rest, put, 0)


def place_main(conv_ref, row):
    def put(s, steps, high, ref, k):
        third, second, first = steps
        across = by_core(s, third, second)
        tm = 4 * high + 2 * by_core(s, second, first) + by_core(s, first, third)
        conv_ref[across, 2 * tm + s, row : row + ref.shape[1], :] = ref[k].astype(conv_ref.dtype)

    return put


def place_side(layer, conv_ref, res_ref, *extra):
    def put(s, steps, high, ref, k):
        far, near, across = steps
        device = 2 * (4 * high + 2 * far + near) + s
        half = res_ref.shape[1] // 2
        res_ref[device, across * half : (across + 1) * half, :] = ref[k, :half, :].astype(res_ref.dtype)
        value = ref[k, half:, :]
        if layer == 1:
            conv_ref[across, device, conv_ref.shape[2] - value.shape[0] :, :] = value.astype(conv_ref.dtype)
            return
        in_ref, out_ref = extra
        value = value.astype(F32)
        if across == 0:
            in_ref[device] = value
            return
        count, classes = value.shape[0], out_ref.shape[2]
        for q in range(value.shape[1] // classes):
            out_ref[device, q * count : (q + 1) * count, :] = value[:, q * classes : (q + 1) * classes]

    return put


def activate(past, now, conv_ref):
    joined = jnp.concatenate([past, now], axis=1)
    t = jnp.tanh(dot(joined, rows_of(conv_ref[0])))
    s = 0.5 + 0.5 * jnp.tanh(0.5 * dot(joined, rows_of(conv_ref[1])))
    return t, s


def slopes(t, s):
    return s * (1.0 - t * t), t * s * (1.0 - s)


def tile_of(i, offset=0):
    return slice(i * TILE + offset, (i + 1) * TILE + offset)


def halo(scalar_ref, own_ref, even_ref, odd_ref, low_ref, high_ref, window_ref, label_ref):
    steps, part = own_ref.shape[0] - LABEL_ROWS, low_ref.shape[0] - LABEL_ROWS
    lane = own_ref.shape[1]
    odd, upper = scalar_ref[2] & 1 == 1, (scalar_ref[2] >> 1) & 1 == 1
    even, uneven, low, high = even_ref[...], odd_ref[...], low_ref[...], high_ref[...]
    at, row = 0, 0
    for value, ahead in ((jnp.where(upper, low, high), False), (jnp.where(odd, even, uneven), False),
                         (own_ref[...], True), (jnp.where(odd, uneven, even), True),
                         (jnp.where(upper, high, low), True)):
        count = value.shape[0] - LABEL_ROWS
        window_ref[at : at + count, :] = value[LABEL_ROWS:]
        at += count
        if ahead:
            label_ref[row : row + count // lane, :] = value[:LABEL_ROWS].astype(F32)[: count // lane]
            row += count // lane


def forward_first(before, steps, scalar_ref, own_ref, even_ref, odd_ref, low_ref, high_ref,
                  a_ref, a2_ref, b_ref, b2_ref, h1_ref, w_out_ref, label_ref, kept_ref, gated_ref, slope_ref, conv_ref, res_ref,
                  norm_ref, h0_ref, in_ref, out_ref):
    rows = h0_ref.shape[0]
    kept = slope_ref.shape[1]
    d = rows - h1_ref.shape[0]
    core = scalar_ref[0]
    place(core, (a_ref, a2_ref), place_main(conv_ref, 0))
    place(core, (b_ref, b2_ref), place_side(0, conv_ref, res_ref, in_ref, out_ref))
    halo(scalar_ref, own_ref, even_ref, odd_ref, low_ref, high_ref, norm_ref, label_ref)
    w_out_ref[...] = rows_of(out_ref[...])
    w_in = rows_of(in_ref[...])
    for i in range(rows // TILE):
        h0_ref[tile_of(i), :] = dot(norm_ref[tile_of(i), :], w_in).astype(BF16)
    kept_ref[...] = h0_ref[before : before + kept, :]
    for i in range(h1_ref.shape[0] // TILE):
        now = h0_ref[tile_of(i, d), :]
        t, s = activate(h0_ref[tile_of(i), :], now, conv_ref)
        gated = (t * s).astype(BF16)
        h1_ref[tile_of(i), :] = (now.astype(F32) + dot(gated, rows_of(res_ref[...]))).astype(BF16)
        first = i * TILE - before
        if 0 <= first < kept:
            own = slice(first, first + TILE)
            slope_ref[0, own, :], slope_ref[1, own, :] = (v.astype(BF16) for v in slopes(t, s))
            if first < steps:
                gated_ref[own, :] = gated


def store_terms(core, keep_ref, send_ref, row, value, first, size, start, count, lane=0):
    at = (slice(row, row + count), slice(lane, lane + value.shape[1]))
    for k in range(value.shape[0] // (2 * size)):
        low = value[2 * k * size + start : 2 * k * size + start + count]
        high = value[(2 * k + 1) * size + start : (2 * k + 1) * size + start + count]
        one, two = spots(first + k, keep_ref.shape[0])
        keep_ref[(by_core(core, one, two),) + at] = jnp.where(core == 0, low, high).astype(keep_ref.dtype)
        send_ref[(by_core(core, two, one),) + at] = jnp.where(core == 0, high, low).astype(send_ref.dtype)


def conv_terms(targets, first, size, value):
    c = value.shape[1] // 2
    store_terms(*targets, 0, value[:, :c], first, size, 0, size)
    store_terms(*targets, size, value[:, c:], first, size, 0, size)


def second_kernel(steps, scale, sizes, scalar_ref, h1_ref, w_out_ref, label_ref, a_ref, a2_ref, b_ref, b2_ref,
                  slope0_ref, res0_ref,
                  loss_ref, keep_ref, send_ref, grad0_ref, round0_ref, back0_ref,
                  back_ref, grad_ref, conv_ref, res_ref, gated_ref, h2_ref, lgrad_ref, round_ref):
    rows, c = back_ref.shape[0], grad_ref.shape[1]
    d = h1_ref.shape[0] - rows
    classes = w_out_ref.shape[1]
    conv, res, _, out = sizes
    core = scalar_ref[0]
    place(core, (a_ref, a2_ref), place_main(conv_ref, 0))
    place(core, (b_ref, b2_ref), place_side(1, conv_ref, res_ref))

    lanes = label_ref.shape[1]
    class_row = lax.broadcasted_iota(jnp.int32, (classes, lanes), 0).astype(F32)
    unit = class_row == lax.broadcasted_iota(jnp.int32, (lanes, lanes), 1).astype(F32)
    row = lax.broadcasted_iota(jnp.int32, (TILE, 1), 0)
    left = scalar_ref[3] - scalar_ref[2] * steps

    for i in range(rows // TILE):
        at = tile_of(i)
        now = h1_ref[tile_of(i, d), :]
        t, s = activate(h1_ref[at, :], now, conv_ref)
        gated = (t * s).astype(BF16)
        h2 = (now.astype(F32) + dot(gated, rows_of(res_ref[...]))).astype(BF16)
        logits = dot(h2, w_out_ref[...])
        total = jnp.log(jnp.sum(jnp.exp(logits), axis=1, keepdims=True))
        groups = range(i * TILE // lanes, (i + 1) * TILE // lanes)
        hot = jnp.concatenate(
            [(class_row == label_ref[k : k + 1, :]).astype(F32).T for k in groups])
        valid = (row + i * TILE < left).astype(F32)
        lgrad = ((jnp.exp(logits - total) - hot) * (valid * scale)).astype(BF16)
        grad = dot_t(lgrad, w_out_ref[...])
        rounded = grad.astype(BF16)
        back = dot_t(rounded, rows_of(res_ref[...]))
        filter_slope, gate_slope = slopes(t, s)
        back_ref[at, :c] = (back * filter_slope).astype(BF16)
        back_ref[at, c:] = (back * gate_slope).astype(BF16)
        if i * TILE < grad_ref.shape[0]:
            grad_ref[at, :] = grad
        if i * TILE < steps:
            loss = (total - jnp.sum(logits * hot, axis=1, keepdims=True)) * valid
            for j, k in enumerate(groups):
                part = jnp.where(unit, loss[j * lanes : (j + 1) * lanes], 0.0)
                loss_ref[k : k + 1, :] = jnp.sum(part, axis=0, keepdims=True)
            gated_ref[at, :] = gated
            h2_ref[at, :] = h2
            lgrad_ref[at, :] = lgrad
            round_ref[at, :] = rounded

    own = slice(0, steps)
    targets = (core, keep_ref, send_ref)
    for i in range(c // TILE):
        at = tile_of(i)
        first, per = i * (TILE // (2 * conv)), c // (2 * conv)
        conv_terms(targets, first, conv, t_dot(h1_ref[0:steps, at], back_ref[own, :]))
        conv_terms(targets, first + per, conv, t_dot(h1_ref[d : d + steps, at], back_ref[own, :]))
        value = t_dot(gated_ref[own, at], round_ref[own, :])
        store_terms(*targets, 2 * conv, value, i * (TILE // (2 * res)), res, 0, res)
        value = t_dot(h2_ref[own, at], lgrad_ref[own, :])
        count = out * classes // c
        for q in range(c // classes):
            store_terms(*targets, 2 * conv + res, value, i * (TILE // (2 * out)), out, q * count, count, q * classes)

    rows0 = back0_ref.shape[0]
    weights = halves(conv_ref, 0), halves(conv_ref, 1)
    for i in range(rows0 // TILE):
        at = tile_of(i)
        grad = grad_below(grad_ref[at, :], back_ref, i, rows - rows0, weights)
        rounded = grad.astype(BF16)
        back = dot_t(rounded, rows_of(res0_ref[...]))
        back0_ref[at, :c] = (back * slope0_ref[0, at, :].astype(F32)).astype(BF16)
        back0_ref[at, c:] = (back * slope0_ref[1, at, :].astype(F32)).astype(BF16)
        if i * TILE < steps:
            grad0_ref[at, :] = grad
            round0_ref[at, :] = rounded


def grad_below(grad, back_ref, i, d, weights):
    c = back_ref.shape[1] // 2
    (filt_past, filt_now), (gate_past, gate_now) = weights
    grad = grad + dot_t(back_ref[tile_of(i), :c], filt_now) + dot_t(back_ref[tile_of(i), c:], gate_now)
    return grad + dot_t(back_ref[tile_of(i, d), :c], filt_past) + dot_t(back_ref[tile_of(i, d), c:], gate_past)


def terms_first(sizes, scalar_ref, back_ref, grad_ref, round_ref, norm_ref, h0_ref, gated_ref, conv_ref,
                keep_ref, send_ref, last_ref):
    steps, c = grad_ref.shape
    d0 = back_ref.shape[0] - steps
    conv, res, enter, _ = sizes
    own = slice(0, steps)
    targets = (scalar_ref[0], keep_ref, send_ref)
    for i in range(c // TILE):
        at = tile_of(i)
        first, per = i * (TILE // (2 * conv)), c // (2 * conv)
        conv_terms(targets, first, conv, t_dot(h0_ref[0:steps, at], back_ref[own, :]))
        conv_terms(targets, first + per, conv, t_dot(h0_ref[d0 : d0 + steps, at], back_ref[own, :]))
        value = t_dot(gated_ref[:, at], round_ref[...])
        store_terms(*targets, 2 * conv, value, i * (TILE // (2 * res)), res, 0, res)
    weights = halves(conv_ref, 0), halves(conv_ref, 1)
    for i in range(steps // TILE):
        last_ref[tile_of(i), :] = grad_below(grad_ref[tile_of(i), :], back_ref, i, d0, weights).astype(BF16)
    value = t_dot(norm_ref[LABEL_ROWS:, :], last_ref[...])
    store_terms(*targets, 2 * conv + res, value, 0, enter, 0, enter)


def finish_kernel(sizes, one0_ref, two0_ref, one1_ref, two1_ref, conv_ref, res_ref, in_ref, out_ref):
    conv, res, _, _ = sizes
    for layer, (one, two) in enumerate(((one0_ref, two0_ref), (one1_ref, two1_ref))):
        total = one[...].astype(F32) + two[...].astype(F32)
        c = total.shape[1]
        conv_ref[layer, :, :c] = total[:conv]
        conv_ref[layer, :, c:] = total[conv : 2 * conv]
        res_ref[layer] = total[2 * conv : 2 * conv + res]
        rest = total[2 * conv + res :]
        if layer == 0:
            in_ref[...] = rest
        else:
            count, classes = rest.shape[0], out_ref.shape[1]
            for q in range(c // classes):
                out_ref[q * count : (q + 1) * count, :] = rest[:, q * classes : (q + 1) * classes]


NEAR, FAR, ACROSS = ("tm", 0), ("tm", 1), ("groups", 0)
CORE = ("site", 0)


def swap(value, links):
    names = ("groups", "tm", "site")
    sizes = [lax.axis_size(name) for name in names]
    pairs = []
    for at in itertools.product(*(range(size) for size in sizes)):
        axis, bit = links[at[2]]
        to = tuple(i ^ (1 << bit) if name == axis else i for name, i in zip(names, at))
        pairs.append(tuple((p[0] * sizes[1] + p[1]) * sizes[2] + p[2] for p in (at, to)))
    return lax.ppermute(value, names, pairs)


def my_bit(links):
    first, second = ((lax.axis_index(axis) >> bit) & 1 for axis, bit in links)
    return jnp.where(lax.axis_index("site") == 0, first, second)


def time_bits():
    return lax.axis_size("tm").bit_length() - 1


def arranged(held, other, links):
    return jnp.where(
        my_bit(links) == 0, jnp.concatenate([held, other]), jnp.concatenate([other, held]))


def grow(held, links):
    return arranged(held, swap(held, links), links)


def together(*values):
    return lax.optimization_barrier(values)


def add(addends, taken):
    total = 0.0
    for v in addends:
        starts = [taken[d] if d in taken and v.shape[d] == 2 else 0 for d in range(time_bits())]
        sizes = [1 if d in taken else v.shape[d] for d in range(time_bits())]
        total = total + lax.dynamic_slice(v, starts + [0, 0], sizes + list(v.shape[-2:])).astype(F32)
    return total


def sum_step(addends, taken, links, dim):
    mine = my_bit(links)
    other = swap(add(addends, taken | {dim: 1 - mine}).astype(BF16), links)
    return addends + [other], taken | {dim: mine}


def sum_steps():
    bits = time_bits()
    rest = [((("tm", bit),) * 2, 1 + bits - bit) for bit in range(2, bits)]
    return [((NEAR, FAR), 0), ((FAR, NEAR), 1)] + rest


def exchange(value, reach):
    size, pairs = lax.axis_size("tm"), []
    for i in range(size - reach):
        if (i // reach) % 2 == 1:
            pairs += [(i, i + reach), (i + reach, i)]
    return lax.ppermute(value, "tm", pairs)


def on_device(features, forget, labels, lengths, w_conv, w_res, w_in, w_out):
    _, steps, bands = features.shape
    time_devices, site_devices = lax.axis_size("tm"), lax.axis_size("site")
    devices = time_devices * site_devices
    c = w_res.shape[2]
    classes = w_out.shape[1]
    conv, res, enter, out = sizes = (w_conv.shape[1], w_res.shape[1], w_in.shape[0], w_out.shape[0])
    half, cut = res // 2, conv * 3 // 4
    aligned = conv % 64 == 0 and res % 32 == 0
    kind = BF16 if aligned else F32
    d0, d1 = BASE_DILATION, 2 * BASE_DILATION
    reach = d0 + d1
    across = my_bit((ACROSS, ACROSS))
    scalars = jnp.stack(
        [lax.axis_index("site"), across, lax.axis_index("tm"), lengths[0]]).astype(jnp.int32)

    if aligned:
        (held,) = call(pack_kernel, [((2 * (conv + half) + enter, c), BF16)], [], 1,
                       scalars, w_conv, w_res, w_in, w_out, limit=FIRST_LIMIT)
    else:
        conv_own = jnp.where(across == 0, w_conv[:, :, :c], w_conv[:, :, c:])
        res_own = jnp.where(across == 0, w_res[:, :half], w_res[:, half:])
        out_own = jnp.concatenate([w_out[k * enter : (k + 1) * enter] for k in range(c // classes)], axis=1)
        held = jnp.concatenate([
            conv_own[0], conv_own[1, :cut], res_own[0],
            jnp.where(across == 0, w_in, out_own), res_own[1], conv_own[1, cut:]])
    held, feat, forget = together(held[None], features[0], forget[0])
    block = ((steps, bands), F32)
    keep, mass, weight, carry = call(
        scan_kernel, [block] * 3 + [((3, bands), F32)], [], 2 * 10**9, feat, forget, limit=FIRST_LIMIT)
    carry = carry[None]
    for bit in reversed(range(2, time_bits())):
        held = grow(held, (("tm", bit),) * 2)
    carry = grow(carry, (NEAR, NEAR))
    held, carry = together(held, carry)

    main_links = [(NEAR, FAR), (FAR, ACROSS), (ACROSS, NEAR)]
    side_links = [(ACROSS, ACROSS), (NEAR, NEAR), (FAR, FAR)]
    main, side = held[:, : conv + cut], held[:, conv + cut :]
    main, side = grow(main, main_links[0]), grow(side, side_links[0])
    for bit in range(1, time_bits()):
        carry = grow(carry, (("tm", bit),) * 2)
    label_rows = steps // bands
    normed, low, high = call(norm_kernel, [((LABEL_ROWS + r, bands), BF16) for r in (steps, reach - steps, reach - steps)],
                             [], 10**8,
                     scalars, feat, keep, mass, weight, carry, labels[0].reshape(label_rows, bands))
    main, side, normed, low, high = together(main, side, normed, low, high)
    main, side = grow(main, main_links[1]), grow(side, side_links[1])
    around = [swap(normed, (NEAR, NEAR)), exchange(normed, 1), swap(low, (FAR, FAR)), exchange(high, 2)]
    main, side, around = together(main, side, around)
    first = [main[:, :conv], side[:, : half + enter]]
    second = [main[:, conv:], side[:, half + enter :]]

    last_links = (main_links[2], side_links[2])

    def both_cores(parts):
        return [v.astype(kind) for p in parts for v in (p, swap(p, (CORE, CORE)))]

    first = [grow(p, links) for p, links in zip(first, last_links)]
    *first, second[0], second[1] = together(*first, *second)
    first, others = both_cores(first), [swap(p, links) for p, links in zip(second, last_links)]

    total_rows, rows0, rows1 = steps + 2 * reach, steps + d0, steps + reach
    conv_all, res_all = ((2, devices, conv, c), kind), ((devices, res, c), kind)
    V = pltpu.VMEM
    h1, out_all, label_window, h0, gated0, slope0, conv0, res0 = call(
        functools.partial(forward_first, d1, steps),
        [((total_rows - d0, c), BF16), ((c, classes), BF16), ((rows1 // bands, bands), F32), ((rows0, c), BF16), ((steps, c), BF16),
         ((2, rows0, c), BF16), conv_all, res_all],
        [V((total_rows, bands), BF16), V((total_rows, c), BF16), V((devices, enter, c), F32), V((devices, out, classes), F32)],
        2 * total_rows * c * (bands + 5 * c), scalars, normed, *around, *first)

    others[0], others[1], h1 = together(*others, h1)
    second = both_cores([arranged(*v) for v in zip(second, others, last_links)])
    scale = 1.0 / math.sqrt(site_devices * steps * time_devices)
    package = [((time_devices, 2 * conv + res + enter, c), kind)] * 2
    loss, keep1, send1, grad1, round0, back0 = call(
        functools.partial(second_kernel, steps, scale, sizes),
        [((label_rows, bands), F32)] + package + [((steps, c), F32), ((steps, c), BF16), ((rows0, 2 * c), BF16)],
        [V((rows1, 2 * c), BF16), V((rows0, c), F32), V(*conv_all), V(*res_all),
         V((steps, c), BF16), V((steps, c), BF16), V((steps, classes), BF16), V((steps, c), BF16)],
        2 * rows1 * c * 6 * c + 2 * steps * 5 * c * c + 2 * rows0 * c * 5 * c,
        scalars, h1, out_all, label_window, *second, slope0, res0)

    def core_step(keep, send):
        other = swap(send.astype(BF16), (CORE, CORE))
        shape = (2,) * time_bits() + keep.shape[1:]
        return [keep.reshape(shape), other.reshape(shape)]

    sums1 = core_step(keep1, send1)
    sums1, back0 = together(sums1, back0)
    keep0, send0 = call(
        functools.partial(terms_first, sizes), package, [V((steps, c), BF16)],
        2 * steps * 9 * c * c, scalars, back0, grad1, round0, normed, h0, gated0, conv0)

    order = sum_steps()
    taken0, taken1 = {}, {}
    sums1, taken1 = sum_step(sums1, taken1, *order[0])
    sums0 = core_step(keep0, send0)
    for step in range(len(order)):
        sums1, sums0 = together(sums1, sums0)
        if step + 1 < len(order):
            sums1, taken1 = sum_step(sums1, taken1, *order[step + 1])
        sums0, taken0 = sum_step(sums0, taken0, *order[step])
    rows = 2 * conv + res + enter
    parts = [v.reshape(rows, c) for sums, taken in ((sums0, taken0), (sums1, taken1))
             for v in (add(sums[:-1], taken), sums[-1])]
    grad_conv, grad_res, grad_in, grad_out = call(
        functools.partial(finish_kernel, sizes),
        [((2, conv, 2 * c), F32), ((2, res, c), F32), ((enter, c), F32), ((out, classes), F32)], [], 1,
        *parts)
    return loss.reshape(1, steps), grad_conv, grad_res, grad_in, grad_out


def solution(mesh):
    return jax.shard_map(
        on_device,
        mesh=mesh,
        in_specs=(
            P(("groups", "site"), "tm", None),
            P(("groups", "site"), "tm", None),
            P(("groups", "site"), "tm"),
            P(("groups", "site")),
            P(None, ("tm", "site"), None),
            P(None, ("tm", "site"), None),
            P(("tm", "site"), None),
            P(("tm", "site"), None),
        ),
        out_specs=(
            P(("groups", "site"), "tm"),
            P("groups", ("tm", "site"), None),
            P("groups", ("tm", "site"), None),
            P(("tm", "site"), "groups"),
            P(("tm", "site"), "groups"),
        ),
        check_vma=False,
    )
```

```python
import functools
import itertools
import math

import jax
import jax.numpy as jnp
from jax import lax
from jax.experimental import pallas as pl
from jax.experimental.pallas import tpu as pltpu
from jax.sharding import PartitionSpec as P

BASE_DILATION = 256
LEVEL_FLOOR = 0.1
F32 = jnp.float32
BF16 = jnp.bfloat16
TILE = 256
VMEM_LIMIT = 24 * 1024 * 1024
FIRST_LIMIT = 56 * 1024 * 1024
WHOLE = pl.BlockSpec(memory_space=pltpu.VMEM)
SCALAR = pl.BlockSpec(memory_space=pltpu.SMEM)


def dot(a, b):
    return lax.dot_general(a, b, (((1,), (0,)), ((), ())), preferred_element_type=F32)


def dot_t(a, b):
    return lax.dot_general(a, b, (((1,), (1,)), ((), ())), preferred_element_type=F32)


def t_dot(a, b):
    return lax.dot_general(a, b, (((0,), (0,)), ((), ())), preferred_element_type=F32)


def call(kernel, outs, scratch, flops, *args, limit=VMEM_LIMIT):
    moved = sum(a.size * a.dtype.itemsize for a in args)
    moved += sum(math.prod(s) * jnp.dtype(d).itemsize for s, d in outs)
    return pl.pallas_call(
        kernel,
        out_shape=[jax.ShapeDtypeStruct(s, d) for s, d in outs],
        in_specs=[SCALAR if a.dtype == jnp.int32 and a.ndim == 1 else WHOLE for a in args],
        out_specs=[WHOLE] * len(outs),
        scratch_shapes=scratch,
        compiler_params=pltpu.CompilerParams(vmem_limit_bytes=limit),
        cost_estimate=pl.CostEstimate(flops=flops, bytes_accessed=moved, transcendentals=0),
    )(*args)


def by_core(core, first, second):
    return first + core * (second - first)


def spots(tm, count):
    near, far, rest, step = tm & 1, (tm >> 1) & 1, tm >> 2, count // 4
    return (2 * near + far) * step + rest, (2 * far + near) * step + rest


LABEL_ROWS = 16


def scan(feat, forget):
    rows = feat.shape[0]
    keep, mass, weight = 1.0 - forget, forget * (feat * feat), forget
    row = lax.broadcasted_iota(jnp.int32, feat.shape, 0)
    step = 1
    while step < rows:
        inside = row >= step
        before = jnp.where(inside, pltpu.roll(mass, step, 0), 0.0)
        mass = keep * before + mass
        before = jnp.where(inside, pltpu.roll(weight, step, 0), 0.0)
        weight = keep * before + weight
        keep = keep * jnp.where(inside, pltpu.roll(keep, step, 0), 1.0)
        step *= 2
    return keep, mass, weight


def scan_kernel(feat_ref, forget_ref, keep_ref, mass_ref, weight_ref, carry_ref):
    rows = feat_ref.shape[0]
    values = scan(feat_ref[...], forget_ref[...])
    for k, (ref, value) in enumerate(zip((keep_ref, mass_ref, weight_ref), values)):
        ref[...] = value
        carry_ref[k : k + 1, :] = value[rows - 1 :]


def pack_kernel(conv_ref, res_ref, in_ref, out_ref, first_ref, second_ref):
    conv, res, more, c = conv_ref.shape[1], res_ref.shape[1], in_ref.shape[0], first_ref.shape[1]
    for layer, ref in enumerate((first_ref, second_ref)):
        ref[:conv, :] = conv_ref[layer, :, :c]
        ref[conv : 2 * conv, :] = conv_ref[layer, :, c:]
        ref[2 * conv : 2 * conv + res, :] = res_ref[layer]
    at = 2 * conv + res
    first_ref[at : at + more, :] = in_ref[...]
    first_ref[at + more : at + 2 * more, :] = jnp.concatenate(
        [out_ref[k * more : (k + 1) * more, :] for k in range(c // out_ref.shape[1])], axis=1)


def norm_kernel(scalar_ref, feat_ref, keep_ref, mass_ref, weight_ref, carry_ref, label_ref, out_ref, low_ref, high_ref):
    bands = feat_ref.shape[1]
    mass0 = jnp.zeros((1, bands), F32)
    weight0 = jnp.zeros((1, bands), F32)
    for tm in range(carry_ref.shape[0]):
        before = tm < scalar_ref[1]
        keep, mass, weight = (carry_ref[tm, k : k + 1, :] for k in range(3))
        mass0 = jnp.where(before, keep * mass0 + mass, mass0)
        weight0 = jnp.where(before, keep * weight0 + weight, weight0)
    keep = keep_ref[...]
    mass = keep * mass0 + mass_ref[...]
    weight = keep * weight0 + weight_ref[...]
    normed = (feat_ref[...] / jnp.sqrt(mass / weight + LEVEL_FLOOR)).astype(BF16)
    label = jnp.concatenate(
        [label_ref[...].astype(F32), jnp.zeros((LABEL_ROWS - label_ref.shape[0], bands), F32)]).astype(BF16)
    part = low_ref.shape[0] - LABEL_ROWS
    first, last = normed[:part], normed[normed.shape[0] - part :]
    upper = (scalar_ref[1] >> 1) & 1 == 1
    for ref, value in (
        (out_ref, normed), (low_ref, jnp.where(upper, first, last)), (high_ref, jnp.where(upper, last, first))):
        ref[:LABEL_ROWS, :] = label
        ref[LABEL_ROWS:, :] = value


def rows_of(value):
    return value.reshape(-1, value.shape[-1]).astype(BF16)


def halves(conv_ref, gate):
    half = conv_ref.shape[1] // 2
    return rows_of(conv_ref[gate, :half]), rows_of(conv_ref[gate, half:])


def place(core, pair, conv_ref, res_ref, in_ref=None, out_ref=None):
    conv, res = conv_ref.shape[2], res_ref.shape[1]
    for ref, own in zip(pair, (True, False)):
        s = core if own else 1 - core
        rest = ref.shape[0] // 4
        bits = rest.bit_length() - 1
        for second, first in itertools.product((0, 1), repeat=2):

            def put(p, _, second=second, first=first, ref=ref, s=s):
                high = sum(((p >> (bits - 1 - b)) & 1) << b for b in range(bits))
                device = 2 * (4 * high + 2 * by_core(s, second, first) + by_core(s, first, second)) + s
                k = (2 * second + first) * rest + p
                conv_ref[0, device] = ref[k, :conv, :].astype(conv_ref.dtype)
                conv_ref[1, device] = ref[k, conv : 2 * conv, :].astype(conv_ref.dtype)
                res_ref[device] = ref[k, 2 * conv : 2 * conv + res, :].astype(res_ref.dtype)
                if in_ref is not None:
                    value = ref[k, 2 * conv + res :, :].astype(F32)
                    count, classes = value.shape[0] // 2, out_ref.shape[2]
                    in_ref[device] = value[:count]
                    for q in range(value.shape[1] // classes):
                        out_ref[device, q * count : (q + 1) * count, :] = (
                            value[count:, q * classes : (q + 1) * classes])
                return 0

            if rest <= 2:
                for p in range(rest):
                    put(p, 0)
            else:
                lax.fori_loop(0, rest, put, 0)


def activate(past, now, conv_ref):
    joined = jnp.concatenate([past, now], axis=1)
    t = jnp.tanh(dot(joined, rows_of(conv_ref[0])))
    s = 0.5 + 0.5 * jnp.tanh(0.5 * dot(joined, rows_of(conv_ref[1])))
    return t, s


def slopes(t, s):
    return s * (1.0 - t * t), t * s * (1.0 - s)


def tile_of(i, offset=0):
    return slice(i * TILE + offset, (i + 1) * TILE + offset)


def halo(scalar_ref, own_ref, even_ref, odd_ref, low_ref, high_ref, window_ref, label_ref):
    steps, part = own_ref.shape[0] - LABEL_ROWS, low_ref.shape[0] - LABEL_ROWS
    lane = own_ref.shape[1]
    odd, upper = scalar_ref[1] & 1 == 1, (scalar_ref[1] >> 1) & 1 == 1
    even, uneven, low, high = even_ref[...], odd_ref[...], low_ref[...], high_ref[...]
    at, row = 0, 0
    for value, ahead in ((jnp.where(upper, low, high), False), (jnp.where(odd, even, uneven), False),
                         (own_ref[...], True), (jnp.where(odd, uneven, even), True),
                         (jnp.where(upper, high, low), True)):
        count = value.shape[0] - LABEL_ROWS
        window_ref[at : at + count, :] = value[LABEL_ROWS:]
        at += count
        if ahead:
            label_ref[row : row + count // lane, :] = value[:LABEL_ROWS].astype(F32)[: count // lane]
            row += count // lane


def forward_first(before, steps, scalar_ref, own_ref, even_ref, odd_ref, low_ref, high_ref,
                  here_ref, there_ref, h1_ref, w_out_ref, label_ref, kept_ref, gated_ref, slope_ref, conv_ref, res_ref,
                  norm_ref, h0_ref, in_ref, out_ref):
    rows = h0_ref.shape[0]
    kept = slope_ref.shape[1]
    d = rows - h1_ref.shape[0]
    core = scalar_ref[0]
    place(core, (here_ref, there_ref), conv_ref, res_ref, in_ref, out_ref)
    halo(scalar_ref, own_ref, even_ref, odd_ref, low_ref, high_ref, norm_ref, label_ref)
    w_out_ref[...] = rows_of(out_ref[...])
    w_in = rows_of(in_ref[...])
    for i in range(rows // TILE):
        h0_ref[tile_of(i), :] = dot(norm_ref[tile_of(i), :], w_in).astype(BF16)
    kept_ref[...] = h0_ref[before : before + kept, :]
    for i in range(h1_ref.shape[0] // TILE):
        now = h0_ref[tile_of(i, d), :]
        t, s = activate(h0_ref[tile_of(i), :], now, conv_ref)
        gated = (t * s).astype(BF16)
        h1_ref[tile_of(i), :] = (now.astype(F32) + dot(gated, rows_of(res_ref[...]))).astype(BF16)
        first = i * TILE - before
        if 0 <= first < kept:
            own = slice(first, first + TILE)
            slope_ref[0, own, :], slope_ref[1, own, :] = (v.astype(BF16) for v in slopes(t, s))
            if first < steps:
                gated_ref[own, :] = gated


def store_terms(core, keep_ref, send_ref, row, value, first, size, start, count, lane=0):
    at = (slice(row, row + count), slice(lane, lane + value.shape[1]))
    for k in range(value.shape[0] // (2 * size)):
        low = value[2 * k * size + start : 2 * k * size + start + count]
        high = value[(2 * k + 1) * size + start : (2 * k + 1) * size + start + count]
        one, two = spots(first + k, keep_ref.shape[0])
        keep_ref[(by_core(core, one, two),) + at] = jnp.where(core == 0, low, high).astype(keep_ref.dtype)
        send_ref[(by_core(core, two, one),) + at] = jnp.where(core == 0, high, low).astype(send_ref.dtype)


def conv_terms(targets, first, size, value):
    c = value.shape[1] // 2
    store_terms(*targets, 0, value[:, :c], first, size, 0, size)
    store_terms(*targets, size, value[:, c:], first, size, 0, size)


def second_kernel(steps, scale, sizes, scalar_ref, h1_ref, w_out_ref, label_ref, here_ref, there_ref,
                  slope0_ref, res0_ref,
                  loss_ref, keep_ref, send_ref, grad0_ref, round0_ref, back0_ref,
                  back_ref, grad_ref, conv_ref, res_ref, gated_ref, h2_ref, lgrad_ref, round_ref):
    rows, c = back_ref.shape[0], grad_ref.shape[1]
    d = h1_ref.shape[0] - rows
    classes = w_out_ref.shape[1]
    conv, res, _, out = sizes
    core = scalar_ref[0]
    place(core, (here_ref, there_ref), conv_ref, res_ref)

    lanes = label_ref.shape[1]
    class_row = lax.broadcasted_iota(jnp.int32, (classes, lanes), 0).astype(F32)
    unit = class_row == lax.broadcasted_iota(jnp.int32, (lanes, lanes), 1).astype(F32)
    row = lax.broadcasted_iota(jnp.int32, (TILE, 1), 0)
    left = scalar_ref[2] - scalar_ref[1] * steps

    for i in range(rows // TILE):
        at = tile_of(i)
        now = h1_ref[tile_of(i, d), :]
        t, s = activate(h1_ref[at, :], now, conv_ref)
        gated = (t * s).astype(BF16)
        h2 = (now.astype(F32) + dot(gated, rows_of(res_ref[...]))).astype(BF16)
        logits = dot(h2, w_out_ref[...])
        total = jnp.log(jnp.sum(jnp.exp(logits), axis=1, keepdims=True))
        groups = range(i * TILE // lanes, (i + 1) * TILE // lanes)
        hot = jnp.concatenate(
            [(class_row == label_ref[k : k + 1, :]).astype(F32).T for k in groups])
        valid = (row + i * TILE < left).astype(F32)
        lgrad = ((jnp.exp(logits - total) - hot) * (valid * scale)).astype(BF16)
        grad = dot_t(lgrad, w_out_ref[...])
        rounded = grad.astype(BF16)
        back = dot_t(rounded, rows_of(res_ref[...]))
        filter_slope, gate_slope = slopes(t, s)
        back_ref[at, :c] = (back * filter_slope).astype(BF16)
        back_ref[at, c:] = (back * gate_slope).astype(BF16)
        if i * TILE < grad_ref.shape[0]:
            grad_ref[at, :] = grad
        if i * TILE < steps:
            loss = (total - jnp.sum(logits * hot, axis=1, keepdims=True)) * valid
            for j, k in enumerate(groups):
                part = jnp.where(unit, loss[j * lanes : (j + 1) * lanes], 0.0)
                loss_ref[k : k + 1, :] = jnp.sum(part, axis=0, keepdims=True)
            gated_ref[at, :] = gated
            h2_ref[at, :] = h2
            lgrad_ref[at, :] = lgrad
            round_ref[at, :] = rounded

    own = slice(0, steps)
    targets = (core, keep_ref, send_ref)
    for i in range(c // TILE):
        at = tile_of(i)
        first, per = i * (TILE // (2 * conv)), c // (2 * conv)
        conv_terms(targets, first, conv, t_dot(h1_ref[0:steps, at], back_ref[own, :]))
        conv_terms(targets, first + per, conv, t_dot(h1_ref[d : d + steps, at], back_ref[own, :]))
        value = t_dot(gated_ref[own, at], round_ref[own, :])
        store_terms(*targets, 2 * conv, value, i * (TILE // (2 * res)), res, 0, res)
        value = t_dot(h2_ref[own, at], lgrad_ref[own, :])
        count = out * classes // c
        for q in range(c // classes):
            store_terms(*targets, 2 * conv + res, value, i * (TILE // (2 * out)), out, q * count, count, q * classes)

    rows0 = back0_ref.shape[0]
    weights = halves(conv_ref, 0), halves(conv_ref, 1)
    for i in range(rows0 // TILE):
        at = tile_of(i)
        grad = grad_below(grad_ref[at, :], back_ref, i, rows - rows0, weights)
        rounded = grad.astype(BF16)
        back = dot_t(rounded, rows_of(res0_ref[...]))
        back0_ref[at, :c] = (back * slope0_ref[0, at, :].astype(F32)).astype(BF16)
        back0_ref[at, c:] = (back * slope0_ref[1, at, :].astype(F32)).astype(BF16)
        if i * TILE < steps:
            grad0_ref[at, :] = grad
            round0_ref[at, :] = rounded


def grad_below(grad, back_ref, i, d, weights):
    c = back_ref.shape[1] // 2
    (filt_past, filt_now), (gate_past, gate_now) = weights
    grad = grad + dot_t(back_ref[tile_of(i), :c], filt_now) + dot_t(back_ref[tile_of(i), c:], gate_now)
    return grad + dot_t(back_ref[tile_of(i, d), :c], filt_past) + dot_t(back_ref[tile_of(i, d), c:], gate_past)


def terms_first(sizes, scalar_ref, back_ref, grad_ref, round_ref, norm_ref, h0_ref, gated_ref, conv_ref,
                keep_ref, send_ref, last_ref):
    steps, c = grad_ref.shape
    d0 = back_ref.shape[0] - steps
    conv, res, enter, _ = sizes
    own = slice(0, steps)
    targets = (scalar_ref[0], keep_ref, send_ref)
    for i in range(c // TILE):
        at = tile_of(i)
        first, per = i * (TILE // (2 * conv)), c // (2 * conv)
        conv_terms(targets, first, conv, t_dot(h0_ref[0:steps, at], back_ref[own, :]))
        conv_terms(targets, first + per, conv, t_dot(h0_ref[d0 : d0 + steps, at], back_ref[own, :]))
        value = t_dot(gated_ref[:, at], round_ref[...])
        store_terms(*targets, 2 * conv, value, i * (TILE // (2 * res)), res, 0, res)
    weights = halves(conv_ref, 0), halves(conv_ref, 1)
    for i in range(steps // TILE):
        last_ref[tile_of(i), :] = grad_below(grad_ref[tile_of(i), :], back_ref, i, d0, weights).astype(BF16)
    value = t_dot(norm_ref[LABEL_ROWS:, :], last_ref[...])
    store_terms(*targets, 2 * conv + res, value, 0, enter, 0, enter)


def finish_kernel(sizes, one0_ref, two0_ref, one1_ref, two1_ref, conv_ref, res_ref, in_ref, out_ref):
    conv, res, _, _ = sizes
    for layer, (one, two) in enumerate(((one0_ref, two0_ref), (one1_ref, two1_ref))):
        total = one[...].astype(F32) + two[...].astype(F32)
        c = total.shape[1]
        conv_ref[layer, :, :c] = total[:conv]
        conv_ref[layer, :, c:] = total[conv : 2 * conv]
        res_ref[layer] = total[2 * conv : 2 * conv + res]
        rest = total[2 * conv + res :]
        if layer == 0:
            in_ref[...] = rest
        else:
            count, classes = rest.shape[0], out_ref.shape[1]
            for q in range(c // classes):
                out_ref[q * count : (q + 1) * count, :] = rest[:, q * classes : (q + 1) * classes]


NEAR, FAR = ("tm", 0), ("tm", 1)
CORE = ("site", 0)


def swap(value, links):
    count, pairs = lax.axis_size("site"), []
    for tm, site in itertools.product(range(lax.axis_size("tm")), range(count)):
        axis, bit = links[site]
        to = (tm ^ (1 << bit), site) if axis == "tm" else (tm, site ^ (1 << bit))
        pairs.append((tm * count + site, to[0] * count + to[1]))
    return lax.ppermute(value, ("tm", "site"), pairs)


def my_bit(links):
    first, second = ((lax.axis_index(axis) >> bit) & 1 for axis, bit in links)
    return jnp.where(lax.axis_index("site") == 0, first, second)


def time_bits():
    return lax.axis_size("tm").bit_length() - 1


def arranged(held, other, links):
    return jnp.where(
        my_bit(links) == 0, jnp.concatenate([held, other]), jnp.concatenate([other, held]))


def grow(held, links):
    return arranged(held, swap(held, links), links)


def together(*values):
    return lax.optimization_barrier(values)


def half_kernel(bits, sent, scalar_ref, one_ref, two_ref, out_ref):
    position = scalar_ref[1]
    mine = by_core(scalar_ref[0], (position >> bits[0]) & 1, (position >> bits[1]) & 1)
    index = 1 - mine if sent else mine
    for p in range(out_ref.shape[0]):
        out_ref[p] = (one_ref[p, index].astype(F32) + two_ref[p, index].astype(F32)).astype(BF16)


def sum_step(addends, scalars, links, dim):
    shape = addends[0].shape
    outer, rows = math.prod(shape[:dim]), math.prod(shape[dim + 1 : -1])
    flat = [v.reshape(outer, 2, rows, shape[-1]) for v in addends]

    def half(sent):
        bits = tuple(bit for _, bit in links)
        (value,) = call(functools.partial(half_kernel, bits, sent), [((outer, rows, shape[-1]), BF16)], [],
                        2 * 10**8, scalars, *flat)
        return value.reshape(shape[:dim] + (1,) + shape[dim + 1 :])

    return [half(False), swap(half(True), links)]


def sum_steps():
    bits = time_bits()
    rest = [((("tm", bit),) * 2, 1 + bits - bit) for bit in range(2, bits)]
    return [((NEAR, FAR), 0), ((FAR, NEAR), 1)] + rest


def exchange(value, reach):
    size, pairs = lax.axis_size("tm"), []
    for i in range(size - reach):
        if (i // reach) % 2 == 1:
            pairs += [(i, i + reach), (i + reach, i)]
    return lax.ppermute(value, "tm", pairs)


def on_device(features, forget, labels, lengths, w_conv, w_res, w_in, w_out):
    _, steps, bands = features.shape
    time_devices, site_devices = lax.axis_size("tm"), lax.axis_size("site")
    devices = time_devices * site_devices
    c = w_res.shape[2]
    classes = w_out.shape[1]
    conv, res, enter, out = sizes = (w_conv.shape[1], w_res.shape[1], w_in.shape[0], w_out.shape[0])
    aligned = conv % 64 == 0 and res % 32 == 0
    kind = BF16 if aligned else F32
    d0, d1 = BASE_DILATION, 2 * BASE_DILATION
    reach = d0 + d1
    scalars = jnp.stack([lax.axis_index("site"), lax.axis_index("tm"), lengths[0]]).astype(jnp.int32)

    if aligned:
        held0, held1 = call(pack_kernel, [((2 * conv + res + 2 * enter, c), BF16), ((2 * conv + res, c), BF16)], [], 1,
                            w_conv, w_res, w_in, w_out, limit=FIRST_LIMIT)
    else:
        out_own = jnp.concatenate([w_out[k * enter : (k + 1) * enter] for k in range(c // classes)], axis=1)
        held0, held1 = (jnp.concatenate([w_conv[k, :, :c], w_conv[k, :, c:], w_res[k]] + more)
                        for k, more in ((0, [w_in, out_own]), (1, [])))
    held0, held1, feat, forget = together(held0[None], held1[None], features[0], forget[0])
    block = ((steps, bands), F32)
    keep, mass, weight, carry = call(
        scan_kernel, [block] * 3 + [((3, bands), F32)], [], 2 * 10**9, feat, forget, limit=FIRST_LIMIT)
    carry = carry[None]
    far = [(("tm", bit),) * 2 for bit in reversed(range(2, time_bits()))]
    turns = [(NEAR, FAR), (FAR, NEAR)]
    for links in far:
        held0 = grow(held0, links)
    for link in (NEAR, FAR):
        carry = grow(carry, (link, link))
    held0, carry, held1 = together(held0, carry, held1)
    held0 = grow(held0, turns[0])
    for links in reversed(far):
        carry = grow(carry, links)
    for links in far:
        held1 = grow(held1, links)
    label_rows = steps // bands
    normed, low, high = call(norm_kernel, [((LABEL_ROWS + r, bands), BF16) for r in (steps, reach - steps, reach - steps)],
                             [], 10**8,
                     scalars, feat, keep, mass, weight, carry, labels[0].reshape(label_rows, bands))
    held0, normed, low, high, held1 = together(held0, normed, low, high, held1)
    held0, held1 = grow(held0, turns[1]), grow(held1, turns[0])
    around = [swap(normed, (NEAR, NEAR)), exchange(normed, 1), swap(low, (FAR, FAR)), exchange(high, 2)]
    held0, held1, around = together(held0, held1, around)
    other1 = swap(held1, turns[1])

    def both_cores(held):
        return held.astype(kind), swap(held, (CORE, CORE)).astype(kind)

    total_rows, rows0, rows1 = steps + 2 * reach, steps + d0, steps + reach
    conv_all, res_all = ((2, devices, conv, c), kind), ((devices, res, c), kind)
    V = pltpu.VMEM
    h1, out_all, label_window, h0, gated0, slope0, conv0, res0 = call(
        functools.partial(forward_first, d1, steps),
        [((total_rows - d0, c), BF16), ((c, classes), BF16), ((rows1 // bands, bands), F32), ((rows0, c), BF16), ((steps, c), BF16),
         ((2, rows0, c), BF16), conv_all, res_all],
        [V((total_rows, bands), BF16), V((total_rows, c), BF16), V((devices, enter, c), F32), V((devices, out, classes), F32)],
        2 * total_rows * c * (bands + 5 * c), scalars, normed, *around, *both_cores(held0))

    other1, h1 = together(other1, h1)
    second = both_cores(arranged(held1, other1, turns[1]))
    scale = 1.0 / math.sqrt(site_devices * steps * time_devices)
    package = [((time_devices, 2 * conv + res + enter, c), kind)] * 2
    loss, keep1, send1, grad1, round0, back0 = call(
        functools.partial(second_kernel, steps, scale, sizes),
        [((label_rows, bands), F32)] + package + [((steps, c), F32), ((steps, c), BF16), ((rows0, 2 * c), BF16)],
        [V((rows1, 2 * c), BF16), V((rows0, c), F32), V(*conv_all), V(*res_all),
         V((steps, c), BF16), V((steps, c), BF16), V((steps, classes), BF16), V((steps, c), BF16)],
        2 * rows1 * c * 6 * c + 2 * steps * 5 * c * c + 2 * rows0 * c * 5 * c,
        scalars, h1, out_all, label_window, *second, slope0, res0)

    def core_step(keep, send):
        other = swap(send.astype(BF16), (CORE, CORE))
        shape = (2,) * time_bits() + keep.shape[1:]
        return [keep.reshape(shape), other.reshape(shape)]

    sums1 = core_step(keep1, send1)
    keep0, send0 = call(
        functools.partial(terms_first, sizes), package, [V((steps, c), BF16)],
        2 * steps * 9 * c * c, scalars, back0, grad1, round0, normed, h0, gated0, conv0)
    sums1, keep0, send0 = together(sums1, keep0, send0)

    order = sum_steps()
    sums1, sums0 = sum_step(sums1, scalars, *order[0]), core_step(keep0, send0)
    for step in range(len(order)):
        sums1, sums0 = together(sums1, sums0)
        if step + 1 < len(order):
            sums1 = sum_step(sums1, scalars, *order[step + 1])
        sums0 = sum_step(sums0, scalars, *order[step])
    rows = 2 * conv + res + enter
    parts = [v.reshape(rows, c) for v in sums0 + sums1]
    grad_conv, grad_res, grad_in, grad_out = call(
        functools.partial(finish_kernel, sizes),
        [((2, conv, 2 * c), F32), ((2, res, c), F32), ((enter, c), F32), ((out, classes), F32)], [], 1,
        *parts)
    return loss.reshape(1, steps), grad_conv, grad_res, grad_in, grad_out


def solution(mesh):
    return jax.shard_map(
        on_device,
        mesh=mesh,
        in_specs=(
            P(("groups", "site"), "tm", None),
            P(("groups", "site"), "tm", None),
            P(("groups", "site"), "tm"),
            P(("groups", "site")),
            P(None, ("tm", "site"), None),
            P(None, ("tm", "site"), None),
            P(("tm", "site"), None),
            P(("tm", "site"), None),
        ),
        out_specs=(
            P(("groups", "site"), "tm"),
            P("groups", ("tm", "site"), None),
            P("groups", ("tm", "site"), None),
            P(("tm", "site"), "groups"),
            P(("tm", "site"), "groups"),
        ),
        check_vma=False,
    )
```

```python
import functools
import itertools
import math

import jax
import jax.numpy as jnp
from jax import lax
from jax.experimental import pallas as pl
from jax.experimental.pallas import tpu as pltpu
from jax.sharding import PartitionSpec as P

BASE_DILATION = 256
LEVEL_FLOOR = 0.1
F32 = jnp.float32
BF16 = jnp.bfloat16
TILE = 256
VMEM_LIMIT = 24 * 1024 * 1024
FIRST_LIMIT = 56 * 1024 * 1024
WHOLE = pl.BlockSpec(memory_space=pltpu.VMEM)
SCALAR = pl.BlockSpec(memory_space=pltpu.SMEM)


def dot(a, b):
    return lax.dot_general(a, b, (((1,), (0,)), ((), ())), preferred_element_type=F32)


def dot_t(a, b):
    return lax.dot_general(a, b, (((1,), (1,)), ((), ())), preferred_element_type=F32)


def t_dot(a, b):
    return lax.dot_general(a, b, (((0,), (0,)), ((), ())), preferred_element_type=F32)


def call(kernel, outs, scratch, flops, *args, limit=VMEM_LIMIT):
    moved = sum(a.size * a.dtype.itemsize for a in args)
    moved += sum(math.prod(s) * jnp.dtype(d).itemsize for s, d in outs)
    return pl.pallas_call(
        kernel,
        out_shape=[jax.ShapeDtypeStruct(s, d) for s, d in outs],
        in_specs=[SCALAR if a.dtype == jnp.int32 and a.ndim == 1 else WHOLE for a in args],
        out_specs=[WHOLE] * len(outs),
        scratch_shapes=scratch,
        compiler_params=pltpu.CompilerParams(vmem_limit_bytes=limit),
        cost_estimate=pl.CostEstimate(flops=flops, bytes_accessed=moved, transcendentals=0),
    )(*args)


def by_core(core, first, second):
    return first + core * (second - first)


def spots(tm, count):
    near, far, rest, step = tm & 1, (tm >> 1) & 1, tm >> 2, count // 4
    return (2 * near + far) * step + rest, (2 * far + near) * step + rest


LABEL_ROWS = 16


def scan(feat, forget):
    rows = feat.shape[0]
    keep, mass, weight = 1.0 - forget, forget * (feat * feat), forget
    row = lax.broadcasted_iota(jnp.int32, feat.shape, 0)
    step = 1
    while step < rows:
        inside = row >= step
        before = jnp.where(inside, pltpu.roll(mass, step, 0), 0.0)
        mass = keep * before + mass
        before = jnp.where(inside, pltpu.roll(weight, step, 0), 0.0)
        weight = keep * before + weight
        keep = keep * jnp.where(inside, pltpu.roll(keep, step, 0), 1.0)
        step *= 2
    return keep, mass, weight


def scan_kernel(feat_ref, forget_ref, keep_ref, mass_ref, weight_ref, carry_ref):
    rows = feat_ref.shape[0]
    values = scan(feat_ref[...], forget_ref[...])
    for k, (ref, value) in enumerate(zip((keep_ref, mass_ref, weight_ref), values)):
        ref[...] = value
        carry_ref[k : k + 1, :] = value[rows - 1 :]


def pack_kernel(feat_ref, forget_ref, conv_ref, res_ref, in_ref, out_ref,
                keep_ref, mass_ref, weight_ref, carry_ref, first_ref, second_ref):
    scan_kernel(feat_ref, forget_ref, keep_ref, mass_ref, weight_ref, carry_ref)
    conv, res, more, c = conv_ref.shape[1], res_ref.shape[1], in_ref.shape[0], first_ref.shape[1]
    for layer, ref in enumerate((first_ref, second_ref)):
        ref[:conv, :] = conv_ref[layer, :, :c]
        ref[conv : 2 * conv, :] = conv_ref[layer, :, c:]
        ref[2 * conv : 2 * conv + res, :] = res_ref[layer]
    at = 2 * conv + res
    first_ref[at : at + more, :] = in_ref[...]
    first_ref[at + more : at + 2 * more, :] = jnp.concatenate(
        [out_ref[k * more : (k + 1) * more, :] for k in range(c // out_ref.shape[1])], axis=1)


def norm_kernel(scalar_ref, feat_ref, keep_ref, mass_ref, weight_ref, carry_ref, label_ref, out_ref, low_ref, high_ref):
    bands = feat_ref.shape[1]
    mass0 = jnp.zeros((1, bands), F32)
    weight0 = jnp.zeros((1, bands), F32)
    for tm in range(carry_ref.shape[0]):
        before = tm < scalar_ref[1]
        keep, mass, weight = (carry_ref[tm, k : k + 1, :] for k in range(3))
        mass0 = jnp.where(before, keep * mass0 + mass, mass0)
        weight0 = jnp.where(before, keep * weight0 + weight, weight0)
    keep = keep_ref[...]
    mass = keep * mass0 + mass_ref[...]
    weight = keep * weight0 + weight_ref[...]
    normed = (feat_ref[...] / jnp.sqrt(mass / weight + LEVEL_FLOOR)).astype(BF16)
    label = jnp.concatenate(
        [label_ref[...].astype(F32), jnp.zeros((LABEL_ROWS - label_ref.shape[0], bands), F32)]).astype(BF16)
    part = low_ref.shape[0] - LABEL_ROWS
    first, last = normed[:part], normed[normed.shape[0] - part :]
    upper = (scalar_ref[1] >> 1) & 1 == 1
    for ref, value in (
        (out_ref, normed), (low_ref, jnp.where(upper, first, last)), (high_ref, jnp.where(upper, last, first))):
        ref[:LABEL_ROWS, :] = label
        ref[LABEL_ROWS:, :] = value


def rows_of(value):
    return value.reshape(-1, value.shape[-1]).astype(BF16)


def halves(conv_ref, gate):
    half = conv_ref.shape[1] // 2
    return rows_of(conv_ref[gate, :half]), rows_of(conv_ref[gate, half:])


def place(core, pair, conv_ref, res_ref, in_ref=None, out_ref=None):
    conv, res = conv_ref.shape[2], res_ref.shape[1]
    for ref, own in zip(pair, (True, False)):
        s = core if own else 1 - core
        rest = ref.shape[0] // 4
        bits = rest.bit_length() - 1
        for second, first in itertools.product((0, 1), repeat=2):

            def put(p, _, second=second, first=first, ref=ref, s=s):
                high = sum(((p >> (bits - 1 - b)) & 1) << b for b in range(bits))
                device = 2 * (4 * high + 2 * by_core(s, second, first) + by_core(s, first, second)) + s
                k = (2 * second + first) * rest + p
                conv_ref[0, device] = ref[k, :conv, :].astype(conv_ref.dtype)
                conv_ref[1, device] = ref[k, conv : 2 * conv, :].astype(conv_ref.dtype)
                res_ref[device] = ref[k, 2 * conv : 2 * conv + res, :].astype(res_ref.dtype)
                if in_ref is not None:
                    value = ref[k, 2 * conv + res :, :].astype(F32)
                    count, classes = value.shape[0] // 2, out_ref.shape[2]
                    in_ref[device] = value[:count]
                    for q in range(value.shape[1] // classes):
                        out_ref[device, q * count : (q + 1) * count, :] = (
                            value[count:, q * classes : (q + 1) * classes])
                return 0

            if rest <= 2:
                for p in range(rest):
                    put(p, 0)
            else:
                lax.fori_loop(0, rest, put, 0)


def activate(past, now, conv_ref):
    joined = jnp.concatenate([past, now], axis=1)
    t = jnp.tanh(dot(joined, rows_of(conv_ref[0])))
    s = 0.5 + 0.5 * jnp.tanh(0.5 * dot(joined, rows_of(conv_ref[1])))
    return t, s


def slopes(t, s):
    return s * (1.0 - t * t), t * s * (1.0 - s)


def tile_of(i, offset=0):
    return slice(i * TILE + offset, (i + 1) * TILE + offset)


def halo(scalar_ref, own_ref, even_ref, odd_ref, low_ref, high_ref, window_ref, label_ref):
    steps, part = own_ref.shape[0] - LABEL_ROWS, low_ref.shape[0] - LABEL_ROWS
    lane = own_ref.shape[1]
    odd, upper = scalar_ref[1] & 1 == 1, (scalar_ref[1] >> 1) & 1 == 1
    even, uneven, low, high = even_ref[...], odd_ref[...], low_ref[...], high_ref[...]
    at, row = 0, 0
    for value, ahead in ((jnp.where(upper, low, high), False), (jnp.where(odd, even, uneven), False),
                         (own_ref[...], True), (jnp.where(odd, uneven, even), True),
                         (jnp.where(upper, high, low), True)):
        count = value.shape[0] - LABEL_ROWS
        window_ref[at : at + count, :] = value[LABEL_ROWS:]
        at += count
        if ahead:
            label_ref[row : row + count // lane, :] = value[:LABEL_ROWS].astype(F32)[: count // lane]
            row += count // lane


def forward_first(before, steps, scalar_ref, own_ref, even_ref, odd_ref, low_ref, high_ref,
                  here_ref, there_ref, h1_ref, w_out_ref, label_ref, kept_ref, gated_ref, slope_ref, conv_ref, res_ref,
                  norm_ref, h0_ref, in_ref, out_ref):
    rows = h0_ref.shape[0]
    kept = slope_ref.shape[1]
    d = rows - h1_ref.shape[0]
    core = scalar_ref[0]
    place(core, (here_ref, there_ref), conv_ref, res_ref, in_ref, out_ref)
    halo(scalar_ref, own_ref, even_ref, odd_ref, low_ref, high_ref, norm_ref, label_ref)
    w_out_ref[...] = rows_of(out_ref[...])
    w_in = rows_of(in_ref[...])
    for i in range(rows // TILE):
        h0_ref[tile_of(i), :] = dot(norm_ref[tile_of(i), :], w_in).astype(BF16)
    kept_ref[...] = h0_ref[before : before + kept, :]
    for i in range(h1_ref.shape[0] // TILE):
        now = h0_ref[tile_of(i, d), :]
        t, s = activate(h0_ref[tile_of(i), :], now, conv_ref)
        gated = (t * s).astype(BF16)
        h1_ref[tile_of(i), :] = (now.astype(F32) + dot(gated, rows_of(res_ref[...]))).astype(BF16)
        first = i * TILE - before
        if 0 <= first < kept:
            own = slice(first, first + TILE)
            slope_ref[0, own, :], slope_ref[1, own, :] = (v.astype(BF16) for v in slopes(t, s))
            if first < steps:
                gated_ref[own, :] = gated


def store_terms(core, keep_ref, send_ref, row, value, first, size, start, count, lane=0):
    at = (slice(row, row + count), slice(lane, lane + value.shape[1]))
    for k in range(value.shape[0] // (2 * size)):
        low = value[2 * k * size + start : 2 * k * size + start + count]
        high = value[(2 * k + 1) * size + start : (2 * k + 1) * size + start + count]
        one, two = spots(first + k, keep_ref.shape[0])
        keep_ref[(by_core(core, one, two),) + at] = jnp.where(core == 0, low, high).astype(keep_ref.dtype)
        send_ref[(by_core(core, two, one),) + at] = jnp.where(core == 0, high, low).astype(send_ref.dtype)


def conv_terms(targets, first, size, value):
    c = value.shape[1] // 2
    store_terms(*targets, 0, value[:, :c], first, size, 0, size)
    store_terms(*targets, size, value[:, c:], first, size, 0, size)


def second_kernel(steps, scale, sizes, scalar_ref, h1_ref, w_out_ref, label_ref, here_ref, there_ref,
                  slope0_ref, res0_ref,
                  loss_ref, keep_ref, send_ref, grad0_ref, round0_ref, back0_ref,
                  back_ref, grad_ref, conv_ref, res_ref, gated_ref, h2_ref, lgrad_ref, round_ref):
    rows, c = back_ref.shape[0], grad_ref.shape[1]
    d = h1_ref.shape[0] - rows
    classes = w_out_ref.shape[1]
    conv, res, _, out = sizes
    core = scalar_ref[0]
    place(core, (here_ref, there_ref), conv_ref, res_ref)

    lanes = label_ref.shape[1]
    class_row = lax.broadcasted_iota(jnp.int32, (classes, lanes), 0).astype(F32)
    unit = class_row == lax.broadcasted_iota(jnp.int32, (lanes, lanes), 1).astype(F32)
    row = lax.broadcasted_iota(jnp.int32, (TILE, 1), 0)
    left = scalar_ref[2] - scalar_ref[1] * steps

    for i in range(rows // TILE):
        at = tile_of(i)
        now = h1_ref[tile_of(i, d), :]
        t, s = activate(h1_ref[at, :], now, conv_ref)
        gated = (t * s).astype(BF16)
        h2 = (now.astype(F32) + dot(gated, rows_of(res_ref[...]))).astype(BF16)
        logits = dot(h2, w_out_ref[...])
        total = jnp.log(jnp.sum(jnp.exp(logits), axis=1, keepdims=True))
        groups = range(i * TILE // lanes, (i + 1) * TILE // lanes)
        hot = jnp.concatenate(
            [(class_row == label_ref[k : k + 1, :]).astype(F32).T for k in groups])
        valid = (row + i * TILE < left).astype(F32)
        lgrad = ((jnp.exp(logits - total) - hot) * (valid * scale)).astype(BF16)
        grad = dot_t(lgrad, w_out_ref[...])
        rounded = grad.astype(BF16)
        back = dot_t(rounded, rows_of(res_ref[...]))
        filter_slope, gate_slope = slopes(t, s)
        back_ref[at, :c] = (back * filter_slope).astype(BF16)
        back_ref[at, c:] = (back * gate_slope).astype(BF16)
        if i * TILE < grad_ref.shape[0]:
            grad_ref[at, :] = grad
        if i * TILE < steps:
            loss = (total - jnp.sum(logits * hot, axis=1, keepdims=True)) * valid
            for j, k in enumerate(groups):
                part = jnp.where(unit, loss[j * lanes : (j + 1) * lanes], 0.0)
                loss_ref[k : k + 1, :] = jnp.sum(part, axis=0, keepdims=True)
            gated_ref[at, :] = gated
            h2_ref[at, :] = h2
            lgrad_ref[at, :] = lgrad
            round_ref[at, :] = rounded

    own = slice(0, steps)
    targets = (core, keep_ref, send_ref)
    for i in range(c // TILE):
        at = tile_of(i)
        first, per = i * (TILE // (2 * conv)), c // (2 * conv)
        conv_terms(targets, first, conv, t_dot(h1_ref[0:steps, at], back_ref[own, :]))
        conv_terms(targets, first + per, conv, t_dot(h1_ref[d : d + steps, at], back_ref[own, :]))
        value = t_dot(gated_ref[own, at], round_ref[own, :])
        store_terms(*targets, 2 * conv, value, i * (TILE // (2 * res)), res, 0, res)
        value = t_dot(h2_ref[own, at], lgrad_ref[own, :])
        count = out * classes // c
        for q in range(c // classes):
            store_terms(*targets, 2 * conv + res, value, i * (TILE // (2 * out)), out, q * count, count, q * classes)

    rows0 = back0_ref.shape[0]
    weights = halves(conv_ref, 0), halves(conv_ref, 1)
    for i in range(rows0 // TILE):
        at = tile_of(i)
        grad = grad_below(grad_ref[at, :], back_ref, i, rows - rows0, weights)
        rounded = grad.astype(BF16)
        back = dot_t(rounded, rows_of(res0_ref[...]))
        back0_ref[at, :c] = (back * slope0_ref[0, at, :].astype(F32)).astype(BF16)
        back0_ref[at, c:] = (back * slope0_ref[1, at, :].astype(F32)).astype(BF16)
        if i * TILE < steps:
            grad0_ref[at, :] = grad
            round0_ref[at, :] = rounded


def grad_below(grad, back_ref, i, d, weights):
    c = back_ref.shape[1] // 2
    (filt_past, filt_now), (gate_past, gate_now) = weights
    grad = grad + dot_t(back_ref[tile_of(i), :c], filt_now) + dot_t(back_ref[tile_of(i), c:], gate_now)
    return grad + dot_t(back_ref[tile_of(i, d), :c], filt_past) + dot_t(back_ref[tile_of(i, d), c:], gate_past)


def terms_first(sizes, scalar_ref, back_ref, grad_ref, round_ref, norm_ref, h0_ref, gated_ref, conv_ref,
                keep_ref, send_ref, last_ref):
    steps, c = grad_ref.shape
    d0 = back_ref.shape[0] - steps
    conv, res, enter, _ = sizes
    own = slice(0, steps)
    targets = (scalar_ref[0], keep_ref, send_ref)
    for i in range(c // TILE):
        at = tile_of(i)
        first, per = i * (TILE // (2 * conv)), c // (2 * conv)
        conv_terms(targets, first, conv, t_dot(h0_ref[0:steps, at], back_ref[own, :]))
        conv_terms(targets, first + per, conv, t_dot(h0_ref[d0 : d0 + steps, at], back_ref[own, :]))
        value = t_dot(gated_ref[:, at], round_ref[...])
        store_terms(*targets, 2 * conv, value, i * (TILE // (2 * res)), res, 0, res)
    weights = halves(conv_ref, 0), halves(conv_ref, 1)
    for i in range(steps // TILE):
        last_ref[tile_of(i), :] = grad_below(grad_ref[tile_of(i), :], back_ref, i, d0, weights).astype(BF16)
    value = t_dot(norm_ref[LABEL_ROWS:, :], last_ref[...])
    store_terms(*targets, 2 * conv + res, value, 0, enter, 0, enter)


def finish_kernel(sizes, one0_ref, two0_ref, one1_ref, two1_ref, conv_ref, res_ref, in_ref, out_ref):
    conv, res, _, _ = sizes
    for layer, (one, two) in enumerate(((one0_ref, two0_ref), (one1_ref, two1_ref))):
        total = one[...].astype(F32) + two[...].astype(F32)
        c = total.shape[1]
        conv_ref[layer, :, :c] = total[:conv]
        conv_ref[layer, :, c:] = total[conv : 2 * conv]
        res_ref[layer] = total[2 * conv : 2 * conv + res]
        rest = total[2 * conv + res :]
        if layer == 0:
            in_ref[...] = rest
        else:
            count, classes = rest.shape[0], out_ref.shape[1]
            for q in range(c // classes):
                out_ref[q * count : (q + 1) * count, :] = rest[:, q * classes : (q + 1) * classes]


NEAR, FAR = ("tm", 0), ("tm", 1)
CORE = ("site", 0)


def swap(value, links):
    count, pairs = lax.axis_size("site"), []
    for tm, site in itertools.product(range(lax.axis_size("tm")), range(count)):
        axis, bit = links[site]
        to = (tm ^ (1 << bit), site) if axis == "tm" else (tm, site ^ (1 << bit))
        pairs.append((tm * count + site, to[0] * count + to[1]))
    return lax.ppermute(value, ("tm", "site"), pairs)


def my_bit(links):
    first, second = ((lax.axis_index(axis) >> bit) & 1 for axis, bit in links)
    return jnp.where(lax.axis_index("site") == 0, first, second)


def time_bits():
    return lax.axis_size("tm").bit_length() - 1


def arranged(held, other, links):
    return jnp.where(
        my_bit(links) == 0, jnp.concatenate([held, other]), jnp.concatenate([other, held]))


def grow(held, links):
    return arranged(held, swap(held, links), links)


def together(*values):
    return lax.optimization_barrier(values)


def half_kernel(bits, sent, scalar_ref, one_ref, two_ref, out_ref):
    position = scalar_ref[1]
    mine = by_core(scalar_ref[0], (position >> bits[0]) & 1, (position >> bits[1]) & 1)
    index = 1 - mine if sent else mine
    for p in range(out_ref.shape[0]):
        out_ref[p] = (one_ref[p, index].astype(F32) + two_ref[p, index].astype(F32)).astype(BF16)


def halves_of(addends, scalars, links, dim):
    shape = addends[0].shape
    outer, rows = math.prod(shape[:dim]), math.prod(shape[dim + 1 : -1])
    flat = [v.reshape(outer, 2, rows, shape[-1]) for v in addends]

    def half(sent):
        bits = tuple(bit for _, bit in links)
        (value,) = call(functools.partial(half_kernel, bits, sent), [((outer, rows, shape[-1]), BF16)], [],
                        2 * 10**8, scalars, *flat)
        return value.reshape(shape[:dim] + (1,) + shape[dim + 1 :])

    return half(False), half(True)


def sum_step(addends, scalars, links, dim):
    kept, sent = halves_of(addends, scalars, links, dim)
    return [kept, swap(sent, links)]


def sum_steps():
    bits = time_bits()
    rest = [((("tm", bit),) * 2, 1 + bits - bit) for bit in range(2, bits)]
    return [((NEAR, FAR), 0), ((FAR, NEAR), 1)] + rest


def exchange(value, reach):
    size, pairs = lax.axis_size("tm"), []
    for i in range(size - reach):
        if (i // reach) % 2 == 1:
            pairs += [(i, i + reach), (i + reach, i)]
    return lax.ppermute(value, "tm", pairs)


def on_device(features, forget, labels, lengths, w_conv, w_res, w_in, w_out):
    _, steps, bands = features.shape
    time_devices, site_devices = lax.axis_size("tm"), lax.axis_size("site")
    devices = time_devices * site_devices
    c = w_res.shape[2]
    classes = w_out.shape[1]
    conv, res, enter, out = sizes = (w_conv.shape[1], w_res.shape[1], w_in.shape[0], w_out.shape[0])
    aligned = conv % 64 == 0 and res % 32 == 0
    kind = BF16 if aligned else F32
    d0, d1 = BASE_DILATION, 2 * BASE_DILATION
    reach = d0 + d1
    scalars = jnp.stack([lax.axis_index("site"), lax.axis_index("tm"), lengths[0]]).astype(jnp.int32)

    feat = features[0]
    scanned = [((steps, bands), F32)] * 3 + [((3, bands), F32)]
    if aligned:
        keep, mass, weight, carry, held0, held1 = call(
            pack_kernel, scanned + [((2 * conv + res + 2 * enter, c), BF16), ((2 * conv + res, c), BF16)], [],
            2 * 10**9, feat, forget[0], w_conv, w_res, w_in, w_out, limit=FIRST_LIMIT)
    else:
        keep, mass, weight, carry = call(scan_kernel, scanned, [], 2 * 10**9, feat, forget[0], limit=FIRST_LIMIT)
        out_own = jnp.concatenate([w_out[k * enter : (k + 1) * enter] for k in range(c // classes)], axis=1)
        held0, held1 = (jnp.concatenate([w_conv[k, :, :c], w_conv[k, :, c:], w_res[k]] + more)
                        for k, more in ((0, [w_in, out_own]), (1, [])))
    held0, held1 = held0[None], held1[None]
    carry = carry[None]
    far = [(("tm", bit),) * 2 for bit in reversed(range(2, time_bits()))]
    turns = [(NEAR, FAR), (FAR, NEAR)]
    for links in far:
        held0 = grow(held0, links)
    for link in (NEAR, FAR):
        carry = grow(carry, (link, link))
    held0, carry, held1 = together(held0, carry, held1)
    held0 = grow(held0, turns[0])
    for links in reversed(far):
        carry = grow(carry, links)
    for links in far:
        held1 = grow(held1, links)
    label_rows = steps // bands
    normed, low, high = call(norm_kernel, [((LABEL_ROWS + r, bands), BF16) for r in (steps, reach - steps, reach - steps)],
                             [], 10**8,
                     scalars, feat, keep, mass, weight, carry, labels[0].reshape(label_rows, bands), limit=FIRST_LIMIT)
    held0, normed, low, high, held1 = together(held0, normed, low, high, held1)
    held0 = grow(held0, turns[1])
    around = [swap(normed, (NEAR, NEAR)), exchange(normed, 1), swap(low, (FAR, FAR)), exchange(high, 2)]
    held0, held1, around = together(held0, held1, around)

    def both_cores(held):
        return held.astype(kind), swap(held, (CORE, CORE)).astype(kind)

    first, held1 = both_cores(held0), grow(held1, turns[0])
    first, held1 = together(first, held1)
    other1 = swap(held1, turns[1])

    total_rows, rows0, rows1 = steps + 2 * reach, steps + d0, steps + reach
    conv_all, res_all = ((2, devices, conv, c), kind), ((devices, res, c), kind)
    V = pltpu.VMEM
    h1, out_all, label_window, h0, gated0, slope0, conv0, res0 = call(
        functools.partial(forward_first, d1, steps),
        [((total_rows - d0, c), BF16), ((c, classes), BF16), ((rows1 // bands, bands), F32), ((rows0, c), BF16), ((steps, c), BF16),
         ((2, rows0, c), BF16), conv_all, res_all],
        [V((total_rows, bands), BF16), V((total_rows, c), BF16), V((devices, enter, c), F32), V((devices, out, classes), F32)],
        2 * total_rows * c * (bands + 5 * c), scalars, normed, *around, *first)

    other1, h1 = together(other1, h1)
    second = both_cores(arranged(held1, other1, turns[1]))
    scale = 1.0 / math.sqrt(site_devices * steps * time_devices)
    package = [((time_devices, 2 * conv + res + enter, c), kind)] * 2
    loss, keep1, send1, grad1, round0, back0 = call(
        functools.partial(second_kernel, steps, scale, sizes),
        [((label_rows, bands), F32)] + package + [((steps, c), F32), ((steps, c), BF16), ((rows0, 2 * c), BF16)],
        [V((rows1, 2 * c), BF16), V((rows0, c), F32), V(*conv_all), V(*res_all),
         V((steps, c), BF16), V((steps, c), BF16), V((steps, classes), BF16), V((steps, c), BF16)],
        2 * rows1 * c * 6 * c + 2 * steps * 5 * c * c + 2 * rows0 * c * 5 * c,
        scalars, h1, out_all, label_window, *second, slope0, res0)

    def core_step(keep, send):
        other = swap(send.astype(BF16), (CORE, CORE))
        shape = (2,) * time_bits() + keep.shape[1:]
        return [keep.reshape(shape), other.reshape(shape)]

    order = sum_steps()
    kept1, sent1 = halves_of(core_step(keep1, send1), scalars, *order[0])
    sent1, back0 = together(sent1, back0)
    sums1 = [kept1, swap(sent1, order[0][0])]
    keep0, send0 = call(
        functools.partial(terms_first, sizes), package, [V((steps, c), BF16)],
        2 * steps * 9 * c * c, scalars, back0, grad1, round0, normed, h0, gated0, conv0)

    sums0 = core_step(keep0, send0)
    for step in range(len(order)):
        sums1, sums0 = together(sums1, sums0)
        if step + 1 < len(order):
            sums1 = sum_step(sums1, scalars, *order[step + 1])
        sums0 = sum_step(sums0, scalars, *order[step])
    rows = 2 * conv + res + enter
    parts = [v.reshape(rows, c) for v in sums0 + sums1]
    grad_conv, grad_res, grad_in, grad_out = call(
        functools.partial(finish_kernel, sizes),
        [((2, conv, 2 * c), F32), ((2, res, c), F32), ((enter, c), F32), ((out, classes), F32)], [], 1,
        *parts)
    return loss.reshape(1, steps), grad_conv, grad_res, grad_in, grad_out


def solution(mesh):
    return jax.shard_map(
        on_device,
        mesh=mesh,
        in_specs=(
            P(("groups", "site"), "tm", None),
            P(("groups", "site"), "tm", None),
            P(("groups", "site"), "tm"),
            P(("groups", "site")),
            P(None, ("tm", "site"), None),
            P(None, ("tm", "site"), None),
            P(("tm", "site"), None),
            P(("tm", "site"), None),
        ),
        out_specs=(
            P(("groups", "site"), "tm"),
            P("groups", ("tm", "site"), None),
            P("groups", ("tm", "site"), None),
            P(("tm", "site"), "groups"),
            P(("tm", "site"), "groups"),
        ),
        check_vma=False,
    )
```

```python
import functools
import itertools
import math

import jax
import jax.numpy as jnp
from jax import lax
from jax.experimental import pallas as pl
from jax.experimental.pallas import tpu as pltpu
from jax.sharding import PartitionSpec as P

BASE_DILATION = 256
LEVEL_FLOOR = 0.1
F32 = jnp.float32
BF16 = jnp.bfloat16
TILE = 256
VMEM_LIMIT = 24 * 1024 * 1024
FIRST_LIMIT = 56 * 1024 * 1024
WHOLE = pl.BlockSpec(memory_space=pltpu.VMEM)
SCALAR = pl.BlockSpec(memory_space=pltpu.SMEM)


def dot(a, b):
    return lax.dot_general(a, b, (((1,), (0,)), ((), ())), preferred_element_type=F32)


def dot_t(a, b):
    return lax.dot_general(a, b, (((1,), (1,)), ((), ())), preferred_element_type=F32)


def t_dot(a, b):
    return lax.dot_general(a, b, (((0,), (0,)), ((), ())), preferred_element_type=F32)


def call(kernel, outs, scratch, flops, *args, limit=VMEM_LIMIT):
    moved = sum(a.size * a.dtype.itemsize for a in args)
    moved += sum(math.prod(s) * jnp.dtype(d).itemsize for s, d in outs)
    return pl.pallas_call(
        kernel,
        out_shape=[jax.ShapeDtypeStruct(s, d) for s, d in outs],
        in_specs=[SCALAR if a.dtype == jnp.int32 and a.ndim == 1 else WHOLE for a in args],
        out_specs=[WHOLE] * len(outs),
        scratch_shapes=scratch,
        compiler_params=pltpu.CompilerParams(vmem_limit_bytes=limit),
        cost_estimate=pl.CostEstimate(flops=flops, bytes_accessed=moved, transcendentals=0),
    )(*args)


def by_core(core, first, second):
    return first + core * (second - first)


def spots(tm, count):
    near, far, rest, step = tm & 1, (tm >> 1) & 1, tm >> 2, count // 4
    return (2 * near + far) * step + rest, (2 * far + near) * step + rest


LABEL_ROWS = 16


def scan(feat, forget):
    rows = feat.shape[0]
    keep, mass, weight = 1.0 - forget, forget * (feat * feat), forget
    row = lax.broadcasted_iota(jnp.int32, feat.shape, 0)
    step = 1
    while step < rows:
        inside = row >= step
        before = jnp.where(inside, pltpu.roll(mass, step, 0), 0.0)
        mass = keep * before + mass
        before = jnp.where(inside, pltpu.roll(weight, step, 0), 0.0)
        weight = keep * before + weight
        keep = keep * jnp.where(inside, pltpu.roll(keep, step, 0), 1.0)
        step *= 2
    return keep, mass, weight


def scan_kernel(feat_ref, forget_ref, keep_ref, mass_ref, weight_ref, carry_ref):
    rows = feat_ref.shape[0]
    values = scan(feat_ref[...], forget_ref[...])
    for k, (ref, value) in enumerate(zip((keep_ref, mass_ref, weight_ref), values)):
        ref[...] = value
        carry_ref[k : k + 1, :] = value[rows - 1 :]


def pack_kernel(feat_ref, forget_ref, conv_ref, res_ref, in_ref, out_ref,
                keep_ref, mass_ref, weight_ref, carry_ref, first_ref, second_ref):
    scan_kernel(feat_ref, forget_ref, keep_ref, mass_ref, weight_ref, carry_ref)
    conv, res, more, c = conv_ref.shape[1], res_ref.shape[1], in_ref.shape[0], first_ref.shape[1]
    for layer, ref in enumerate((first_ref, second_ref)):
        ref[:conv, :] = conv_ref[layer, :, :c]
        ref[conv : 2 * conv, :] = conv_ref[layer, :, c:]
        ref[2 * conv : 2 * conv + res, :] = res_ref[layer]
    at = 2 * conv + res
    first_ref[at : at + more, :] = in_ref[...]
    first_ref[at + more : at + 2 * more, :] = jnp.concatenate(
        [out_ref[k * more : (k + 1) * more, :] for k in range(c // out_ref.shape[1])], axis=1)


def norm_kernel(scalar_ref, feat_ref, keep_ref, mass_ref, weight_ref, carry_ref, label_ref, out_ref, low_ref, high_ref):
    bands = feat_ref.shape[1]
    mass0 = jnp.zeros((1, bands), F32)
    weight0 = jnp.zeros((1, bands), F32)
    for tm in range(carry_ref.shape[0]):
        before = tm < scalar_ref[1]
        keep, mass, weight = (carry_ref[tm, k : k + 1, :] for k in range(3))
        mass0 = jnp.where(before, keep * mass0 + mass, mass0)
        weight0 = jnp.where(before, keep * weight0 + weight, weight0)
    keep = keep_ref[...]
    mass = keep * mass0 + mass_ref[...]
    weight = keep * weight0 + weight_ref[...]
    normed = (feat_ref[...] / jnp.sqrt(mass / weight + LEVEL_FLOOR)).astype(BF16)
    label = jnp.concatenate(
        [label_ref[...].astype(F32), jnp.zeros((LABEL_ROWS - label_ref.shape[0], bands), F32)]).astype(BF16)
    part = low_ref.shape[0] - LABEL_ROWS
    first, last = normed[:part], normed[normed.shape[0] - part :]
    upper = (scalar_ref[1] >> 1) & 1 == 1
    for ref, value in (
        (out_ref, normed), (low_ref, jnp.where(upper, first, last)), (high_ref, jnp.where(upper, last, first))):
        ref[:LABEL_ROWS, :] = label
        ref[LABEL_ROWS:, :] = value


def rows_of(value):
    return value.reshape(-1, value.shape[-1]).astype(BF16)


def halves(conv_ref, gate):
    half = conv_ref.shape[1] // 2
    return rows_of(conv_ref[gate, :half]), rows_of(conv_ref[gate, half:])


def place(core, pair, conv_ref, res_ref, in_ref=None, out_ref=None):
    conv, res = conv_ref.shape[2], res_ref.shape[1]
    for ref, own in zip(pair, (True, False)):
        s = core if own else 1 - core
        rest = ref.shape[0] // 4
        bits = rest.bit_length() - 1
        for second, first in itertools.product((0, 1), repeat=2):

            def put(p, _, second=second, first=first, ref=ref, s=s):
                high = sum(((p >> (bits - 1 - b)) & 1) << b for b in range(bits))
                device = 2 * (4 * high + 2 * by_core(s, second, first) + by_core(s, first, second)) + s
                k = (2 * second + first) * rest + p
                conv_ref[0, device] = ref[k, :conv, :].astype(conv_ref.dtype)
                conv_ref[1, device] = ref[k, conv : 2 * conv, :].astype(conv_ref.dtype)
                res_ref[device] = ref[k, 2 * conv : 2 * conv + res, :].astype(res_ref.dtype)
                if in_ref is not None:
                    value = ref[k, 2 * conv + res :, :].astype(F32)
                    count, classes = value.shape[0] // 2, out_ref.shape[2]
                    in_ref[device] = value[:count]
                    for q in range(value.shape[1] // classes):
                        out_ref[device, q * count : (q + 1) * count, :] = (
                            value[count:, q * classes : (q + 1) * classes])
                return 0

            if rest <= 2:
                for p in range(rest):
                    put(p, 0)
            else:
                lax.fori_loop(0, rest, put, 0)


def activate(past, now, conv_ref):
    joined = jnp.concatenate([past, now], axis=1)
    t = jnp.tanh(dot(joined, rows_of(conv_ref[0])))
    s = 0.5 + 0.5 * jnp.tanh(0.5 * dot(joined, rows_of(conv_ref[1])))
    return t, s


def slopes(t, s):
    return s * (1.0 - t * t), t * s * (1.0 - s)


def tile_of(i, offset=0):
    return slice(i * TILE + offset, (i + 1) * TILE + offset)


def halo(scalar_ref, own_ref, even_ref, odd_ref, low_ref, high_ref, window_ref, label_ref):
    steps, part = own_ref.shape[0] - LABEL_ROWS, low_ref.shape[0] - LABEL_ROWS
    lane = own_ref.shape[1]
    odd, upper = scalar_ref[1] & 1 == 1, (scalar_ref[1] >> 1) & 1 == 1
    even, uneven, low, high = even_ref[...], odd_ref[...], low_ref[...], high_ref[...]
    at, row = 0, 0
    for value, ahead in ((jnp.where(upper, low, high), False), (jnp.where(odd, even, uneven), False),
                         (own_ref[...], True), (jnp.where(odd, uneven, even), True),
                         (jnp.where(upper, high, low), True)):
        count = value.shape[0] - LABEL_ROWS
        window_ref[at : at + count, :] = value[LABEL_ROWS:]
        at += count
        if ahead:
            label_ref[row : row + count // lane, :] = value[:LABEL_ROWS].astype(F32)[: count // lane]
            row += count // lane


def forward_first(before, steps, scalar_ref, own_ref, even_ref, odd_ref, low_ref, high_ref,
                  here_ref, there_ref, h1_ref, w_out_ref, label_ref, kept_ref, gated_ref, slope_ref, conv_ref, res_ref,
                  norm_ref, h0_ref, in_ref, out_ref):
    rows = h0_ref.shape[0]
    kept = slope_ref.shape[1]
    d = rows - h1_ref.shape[0]
    core = scalar_ref[0]
    place(core, (here_ref, there_ref), conv_ref, res_ref, in_ref, out_ref)
    halo(scalar_ref, own_ref, even_ref, odd_ref, low_ref, high_ref, norm_ref, label_ref)
    w_out_ref[...] = rows_of(out_ref[...])
    w_in = rows_of(in_ref[...])
    for i in range(rows // steps):
        at = slice(i * steps, (i + 1) * steps)
        h0_ref[at, :] = dot(norm_ref[at, :], w_in).astype(BF16)
    kept_ref[...] = h0_ref[before : before + kept, :]
    cuts = [0, before, before + steps, before + kept, h1_ref.shape[0]]
    for start, end in zip(cuts, cuts[1:]):
        at = slice(start, end)
        now = h0_ref[start + d : end + d, :]
        t, s = activate(h0_ref[at, :], now, conv_ref)
        gated = (t * s).astype(BF16)
        h1_ref[at, :] = (now.astype(F32) + dot(gated, rows_of(res_ref[...]))).astype(BF16)
        if before <= start < before + kept:
            own = slice(start - before, end - before)
            slope_ref[0, own, :], slope_ref[1, own, :] = (v.astype(BF16) for v in slopes(t, s))
            if start == before:
                gated_ref[...] = gated


def store_terms(core, keep_ref, send_ref, row, value, first, size, start, count, lane=0):
    at = (slice(row, row + count), slice(lane, lane + value.shape[1]))
    for k in range(value.shape[0] // (2 * size)):
        low = value[2 * k * size + start : 2 * k * size + start + count]
        high = value[(2 * k + 1) * size + start : (2 * k + 1) * size + start + count]
        one, two = spots(first + k, keep_ref.shape[0])
        keep_ref[(by_core(core, one, two),) + at] = jnp.where(core == 0, low, high).astype(keep_ref.dtype)
        send_ref[(by_core(core, two, one),) + at] = jnp.where(core == 0, high, low).astype(send_ref.dtype)


def conv_terms(targets, first, size, value):
    c = value.shape[1] // 2
    store_terms(*targets, 0, value[:, :c], first, size, 0, size)
    store_terms(*targets, size, value[:, c:], first, size, 0, size)


def second_kernel(steps, scale, sizes, scalar_ref, h1_ref, w_out_ref, label_ref, here_ref, there_ref,
                  slope0_ref, res0_ref,
                  loss_ref, keep_ref, send_ref, grad0_ref, round0_ref, back0_ref,
                  back_ref, grad_ref, conv_ref, res_ref, gated_ref, h2_ref, lgrad_ref, round_ref):
    rows, c = back_ref.shape[0], grad_ref.shape[1]
    d = h1_ref.shape[0] - rows
    classes = w_out_ref.shape[1]
    conv, res, _, out = sizes
    core = scalar_ref[0]
    place(core, (here_ref, there_ref), conv_ref, res_ref)

    lanes = label_ref.shape[1]
    class_row = lax.broadcasted_iota(jnp.int32, (classes, lanes), 0).astype(F32)
    unit = class_row == lax.broadcasted_iota(jnp.int32, (lanes, lanes), 1).astype(F32)
    row = lax.broadcasted_iota(jnp.int32, (TILE, 1), 0)
    left = scalar_ref[2] - scalar_ref[1] * steps

    for i in range(rows // TILE):
        at = tile_of(i)
        now = h1_ref[tile_of(i, d), :]
        t, s = activate(h1_ref[at, :], now, conv_ref)
        gated = (t * s).astype(BF16)
        h2 = (now.astype(F32) + dot(gated, rows_of(res_ref[...]))).astype(BF16)
        logits = dot(h2, w_out_ref[...])
        total = jnp.log(jnp.sum(jnp.exp(logits), axis=1, keepdims=True))
        groups = range(i * TILE // lanes, (i + 1) * TILE // lanes)
        hot = jnp.concatenate(
            [(class_row == label_ref[k : k + 1, :]).astype(F32).T for k in groups])
        valid = (row + i * TILE < left).astype(F32)
        lgrad = ((jnp.exp(logits - total) - hot) * (valid * scale)).astype(BF16)
        grad = dot_t(lgrad, w_out_ref[...])
        rounded = grad.astype(BF16)
        back = dot_t(rounded, rows_of(res_ref[...]))
        filter_slope, gate_slope = slopes(t, s)
        back_ref[at, :c] = (back * filter_slope).astype(BF16)
        back_ref[at, c:] = (back * gate_slope).astype(BF16)
        if i * TILE < grad_ref.shape[0]:
            grad_ref[at, :] = grad
        if i * TILE < steps:
            loss = (total - jnp.sum(logits * hot, axis=1, keepdims=True)) * valid
            for j, k in enumerate(groups):
                part = jnp.where(unit, loss[j * lanes : (j + 1) * lanes], 0.0)
                loss_ref[k : k + 1, :] = jnp.sum(part, axis=0, keepdims=True)
            gated_ref[at, :] = gated
            h2_ref[at, :] = h2
            lgrad_ref[at, :] = lgrad
            round_ref[at, :] = rounded

    own = slice(0, steps)
    targets = (core, keep_ref, send_ref)
    for i in range(c // TILE):
        at = tile_of(i)
        first, per = i * (TILE // (2 * conv)), c // (2 * conv)
        conv_terms(targets, first, conv, t_dot(h1_ref[0:steps, at], back_ref[own, :]))
        conv_terms(targets, first + per, conv, t_dot(h1_ref[d : d + steps, at], back_ref[own, :]))
        value = t_dot(gated_ref[own, at], round_ref[own, :])
        store_terms(*targets, 2 * conv, value, i * (TILE // (2 * res)), res, 0, res)
        value = t_dot(h2_ref[own, at], lgrad_ref[own, :])
        count = out * classes // c
        for q in range(c // classes):
            store_terms(*targets, 2 * conv + res, value, i * (TILE // (2 * out)), out, q * count, count, q * classes)

    rows0 = back0_ref.shape[0]
    weights = halves(conv_ref, 0), halves(conv_ref, 1)
    for i in range(rows0 // TILE):
        at = tile_of(i)
        grad = grad_below(grad_ref[at, :], back_ref, i, rows - rows0, weights)
        rounded = grad.astype(BF16)
        back = dot_t(rounded, rows_of(res0_ref[...]))
        back0_ref[at, :c] = (back * slope0_ref[0, at, :].astype(F32)).astype(BF16)
        back0_ref[at, c:] = (back * slope0_ref[1, at, :].astype(F32)).astype(BF16)
        if i * TILE < steps:
            grad0_ref[at, :] = grad
            round0_ref[at, :] = rounded


def grad_below(grad, back_ref, i, d, weights):
    c = back_ref.shape[1] // 2
    (filt_past, filt_now), (gate_past, gate_now) = weights
    grad = grad + dot_t(back_ref[tile_of(i), :c], filt_now) + dot_t(back_ref[tile_of(i), c:], gate_now)
    return grad + dot_t(back_ref[tile_of(i, d), :c], filt_past) + dot_t(back_ref[tile_of(i, d), c:], gate_past)


def terms_first(sizes, scalar_ref, back_ref, grad_ref, round_ref, norm_ref, h0_ref, gated_ref, conv_ref,
                keep_ref, send_ref, last_ref):
    steps, c = grad_ref.shape
    d0 = back_ref.shape[0] - steps
    conv, res, enter, _ = sizes
    own = slice(0, steps)
    targets = (scalar_ref[0], keep_ref, send_ref)
    for i in range(c // TILE):
        at = tile_of(i)
        first, per = i * (TILE // (2 * conv)), c // (2 * conv)
        conv_terms(targets, first, conv, t_dot(h0_ref[0:steps, at], back_ref[own, :]))
        conv_terms(targets, first + per, conv, t_dot(h0_ref[d0 : d0 + steps, at], back_ref[own, :]))
        value = t_dot(gated_ref[:, at], round_ref[...])
        store_terms(*targets, 2 * conv, value, i * (TILE // (2 * res)), res, 0, res)
    weights = halves(conv_ref, 0), halves(conv_ref, 1)
    for i in range(steps // TILE):
        last_ref[tile_of(i), :] = grad_below(grad_ref[tile_of(i), :], back_ref, i, d0, weights).astype(BF16)
    value = t_dot(norm_ref[LABEL_ROWS:, :], last_ref[...])
    store_terms(*targets, 2 * conv + res, value, 0, enter, 0, enter)


def finish_kernel(sizes, one0_ref, two0_ref, one1_ref, two1_ref, conv_ref, res_ref, in_ref, out_ref):
    conv, res, _, _ = sizes
    for layer, (one, two) in enumerate(((one0_ref, two0_ref), (one1_ref, two1_ref))):
        total = one[...].astype(F32) + two[...].astype(F32)
        c = total.shape[1]
        conv_ref[layer, :, :c] = total[:conv]
        conv_ref[layer, :, c:] = total[conv : 2 * conv]
        res_ref[layer] = total[2 * conv : 2 * conv + res]
        rest = total[2 * conv + res :]
        if layer == 0:
            in_ref[...] = rest
        else:
            count, classes = rest.shape[0], out_ref.shape[1]
            for q in range(c // classes):
                out_ref[q * count : (q + 1) * count, :] = rest[:, q * classes : (q + 1) * classes]


NEAR, FAR = ("tm", 0), ("tm", 1)
CORE = ("site", 0)


def swap(value, links):
    count, pairs = lax.axis_size("site"), []
    for tm, site in itertools.product(range(lax.axis_size("tm")), range(count)):
        axis, bit = links[site]
        to = (tm ^ (1 << bit), site) if axis == "tm" else (tm, site ^ (1 << bit))
        pairs.append((tm * count + site, to[0] * count + to[1]))
    return lax.ppermute(value, ("tm", "site"), pairs)


def my_bit(links):
    first, second = ((lax.axis_index(axis) >> bit) & 1 for axis, bit in links)
    return jnp.where(lax.axis_index("site") == 0, first, second)


def time_bits():
    return lax.axis_size("tm").bit_length() - 1


def arranged(held, other, links):
    return jnp.where(
        my_bit(links) == 0, jnp.concatenate([held, other]), jnp.concatenate([other, held]))


def grow(held, links):
    return arranged(held, swap(held, links), links)


def together(*values):
    return lax.optimization_barrier(values)


def half_kernel(bits, sent, scalar_ref, one_ref, two_ref, out_ref):
    position = scalar_ref[1]
    mine = by_core(scalar_ref[0], (position >> bits[0]) & 1, (position >> bits[1]) & 1)
    index = 1 - mine if sent else mine
    for p in range(out_ref.shape[0]):
        out_ref[p] = (one_ref[p, index].astype(F32) + two_ref[p, index].astype(F32)).astype(BF16)


def halves_of(addends, scalars, links, dim):
    shape = addends[0].shape
    outer, rows = math.prod(shape[:dim]), math.prod(shape[dim + 1 : -1])
    flat = [v.reshape(outer, 2, rows, shape[-1]) for v in addends]

    def half(sent):
        bits = tuple(bit for _, bit in links)
        (value,) = call(functools.partial(half_kernel, bits, sent), [((outer, rows, shape[-1]), BF16)], [],
                        2 * 10**8, scalars, *flat)
        return value.reshape(shape[:dim] + (1,) + shape[dim + 1 :])

    return half(False), half(True)


def sum_steps():
    bits = time_bits()
    rest = [((("tm", bit),) * 2, 1 + bits - bit) for bit in range(2, bits)]
    return [((NEAR, FAR), 0), ((FAR, NEAR), 1)] + rest


def exchange(value, reach):
    size, pairs = lax.axis_size("tm"), []
    for i in range(size - reach):
        if (i // reach) % 2 == 1:
            pairs += [(i, i + reach), (i + reach, i)]
    return lax.ppermute(value, "tm", pairs)


def on_device(features, forget, labels, lengths, w_conv, w_res, w_in, w_out):
    _, steps, bands = features.shape
    time_devices, site_devices = lax.axis_size("tm"), lax.axis_size("site")
    devices = time_devices * site_devices
    c = w_res.shape[2]
    classes = w_out.shape[1]
    conv, res, enter, out = sizes = (w_conv.shape[1], w_res.shape[1], w_in.shape[0], w_out.shape[0])
    aligned = conv % 64 == 0 and res % 32 == 0
    kind = BF16 if aligned else F32
    d0, d1 = BASE_DILATION, 2 * BASE_DILATION
    reach = d0 + d1
    scalars = jnp.stack([lax.axis_index("site"), lax.axis_index("tm"), lengths[0]]).astype(jnp.int32)

    feat = features[0]
    scanned = [((steps, bands), F32)] * 3 + [((3, bands), F32)]
    if aligned:
        keep, mass, weight, carry, held0, held1 = call(
            pack_kernel, scanned + [((2 * conv + res + 2 * enter, c), BF16), ((2 * conv + res, c), BF16)], [],
            2 * 10**9, feat, forget[0], w_conv, w_res, w_in, w_out, limit=FIRST_LIMIT)
    else:
        keep, mass, weight, carry = call(scan_kernel, scanned, [], 2 * 10**9, feat, forget[0], limit=FIRST_LIMIT)
        out_own = jnp.concatenate([w_out[k * enter : (k + 1) * enter] for k in range(c // classes)], axis=1)
        held0, held1 = (jnp.concatenate([w_conv[k, :, :c], w_conv[k, :, c:], w_res[k]] + more)
                        for k, more in ((0, [w_in, out_own]), (1, [])))
    held0, held1 = held0[None], held1[None]
    carry = carry[None]
    far = [(("tm", bit),) * 2 for bit in reversed(range(2, time_bits()))]
    turns = [(NEAR, FAR), (FAR, NEAR)]
    for links in far:
        held0 = grow(held0, links)
    for link in (NEAR, FAR):
        carry = grow(carry, (link, link))
    held0, carry, held1 = together(held0, carry, held1)
    held0 = grow(held0, turns[0])
    for links in reversed(far):
        carry = grow(carry, links)
    for links in far:
        held1 = grow(held1, links)
    label_rows = steps // bands
    normed, low, high = call(norm_kernel, [((LABEL_ROWS + r, bands), BF16) for r in (steps, reach - steps, reach - steps)],
                             [], 10**8,
                     scalars, feat, keep, mass, weight, carry, labels[0].reshape(label_rows, bands), limit=FIRST_LIMIT)
    held0, normed, low, high, held1 = together(held0, normed, low, high, held1)
    held0, held1 = grow(held0, turns[1]), grow(held1, turns[0])
    around = [swap(normed, (NEAR, NEAR)), exchange(normed, 1), swap(low, (FAR, FAR)), exchange(high, 2)]
    held0, held1, around = together(held0, held1, around)

    def both_cores(held):
        return held.astype(kind), swap(held, (CORE, CORE)).astype(kind)

    first, other1 = both_cores(held0), swap(held1, turns[1])

    total_rows, rows0, rows1 = steps + 2 * reach, steps + d0, steps + reach
    conv_all, res_all = ((2, devices, conv, c), kind), ((devices, res, c), kind)
    V = pltpu.VMEM
    h1, out_all, label_window, h0, gated0, slope0, conv0, res0 = call(
        functools.partial(forward_first, d1, steps),
        [((total_rows - d0, c), BF16), ((c, classes), BF16), ((rows1 // bands, bands), F32), ((rows0, c), BF16), ((steps, c), BF16),
         ((2, rows0, c), BF16), conv_all, res_all],
        [V((total_rows, bands), BF16), V((total_rows, c), BF16), V((devices, enter, c), F32), V((devices, out, classes), F32)],
        2 * total_rows * c * (bands + 5 * c), scalars, normed, *around, *first)

    other1, h1 = together(other1, h1)
    second = both_cores(arranged(held1, other1, turns[1]))
    scale = 1.0 / math.sqrt(site_devices * steps * time_devices)
    package = [((time_devices, 2 * conv + res + enter, c), kind)] * 2
    loss, keep1, send1, grad1, round0, back0 = call(
        functools.partial(second_kernel, steps, scale, sizes),
        [((label_rows, bands), F32)] + package + [((steps, c), F32), ((steps, c), BF16), ((rows0, 2 * c), BF16)],
        [V((rows1, 2 * c), BF16), V((rows0, c), F32), V(*conv_all), V(*res_all),
         V((steps, c), BF16), V((steps, c), BF16), V((steps, classes), BF16), V((steps, c), BF16)],
        2 * rows1 * c * 6 * c + 2 * steps * 5 * c * c + 2 * rows0 * c * 5 * c,
        scalars, h1, out_all, label_window, *second, slope0, res0)

    def core_step(keep, send):
        other = swap(send.astype(BF16), (CORE, CORE))
        shape = (2,) * time_bits() + keep.shape[1:]
        return [keep.reshape(shape), other.reshape(shape)]

    sums1 = core_step(keep1, send1)
    keep0, send0 = call(
        functools.partial(terms_first, sizes), package, [V((steps, c), BF16)],
        2 * steps * 9 * c * c, scalars, back0, grad1, round0, normed, h0, gated0, conv0)
    sums1, keep0, send0 = together(sums1, keep0, send0)

    order = sum_steps()
    kept1, sent1 = halves_of(sums1, scalars, *order[0])
    sums1, sums0 = [kept1, swap(sent1, order[0][0])], core_step(keep0, send0)
    for step, (links, dim) in enumerate(order):
        more = step + 1 < len(order)
        kept0, sent0 = halves_of(sums0, scalars, links, dim)
        if more:
            kept1, sent1 = halves_of(sums1, scalars, *order[step + 1])
            sent1, sent0 = together(sent1, sent0)
            sums1 = [kept1, swap(sent1, order[step + 1][0])]
        sums0 = [kept0, swap(sent0, links)]
    rows = 2 * conv + res + enter
    parts = [v.reshape(rows, c) for v in sums0 + sums1]
    grad_conv, grad_res, grad_in, grad_out = call(
        functools.partial(finish_kernel, sizes),
        [((2, conv, 2 * c), F32), ((2, res, c), F32), ((enter, c), F32), ((out, classes), F32)], [], 1,
        *parts)
    return loss.reshape(1, steps), grad_conv, grad_res, grad_in, grad_out


def solution(mesh):
    return jax.shard_map(
        on_device,
        mesh=mesh,
        in_specs=(
            P(("groups", "site"), "tm", None),
            P(("groups", "site"), "tm", None),
            P(("groups", "site"), "tm"),
            P(("groups", "site")),
            P(None, ("tm", "site"), None),
            P(None, ("tm", "site"), None),
            P(("tm", "site"), None),
            P(("tm", "site"), None),
        ),
        out_specs=(
            P(("groups", "site"), "tm"),
            P("groups", ("tm", "site"), None),
            P("groups", ("tm", "site"), None),
            P(("tm", "site"), "groups"),
            P(("tm", "site"), "groups"),
        ),
        check_vma=False,
    )
```

```python
import functools
import itertools
import math

import jax
import jax.numpy as jnp
from jax import lax
from jax.experimental import pallas as pl
from jax.experimental.pallas import tpu as pltpu
from jax.sharding import PartitionSpec as P

BASE_DILATION = 256
LEVEL_FLOOR = 0.1
F32 = jnp.float32
BF16 = jnp.bfloat16
TILE = 256
VMEM_LIMIT = 24 * 1024 * 1024
FIRST_LIMIT = 56 * 1024 * 1024
WHOLE = pl.BlockSpec(memory_space=pltpu.VMEM)
SCALAR = pl.BlockSpec(memory_space=pltpu.SMEM)


def dot(a, b):
    return lax.dot_general(a, b, (((1,), (0,)), ((), ())), preferred_element_type=F32)


def dot_t(a, b):
    return lax.dot_general(a, b, (((1,), (1,)), ((), ())), preferred_element_type=F32)


def t_dot(a, b):
    return lax.dot_general(a, b, (((0,), (0,)), ((), ())), preferred_element_type=F32)


def call(kernel, outs, scratch, flops, *args, limit=VMEM_LIMIT):
    moved = sum(a.size * a.dtype.itemsize for a in args)
    moved += sum(math.prod(s) * jnp.dtype(d).itemsize for s, d in outs)
    return pl.pallas_call(
        kernel,
        out_shape=[jax.ShapeDtypeStruct(s, d) for s, d in outs],
        in_specs=[SCALAR if a.dtype == jnp.int32 and a.ndim == 1 else WHOLE for a in args],
        out_specs=[WHOLE] * len(outs),
        scratch_shapes=scratch,
        compiler_params=pltpu.CompilerParams(vmem_limit_bytes=limit),
        cost_estimate=pl.CostEstimate(flops=flops, bytes_accessed=moved, transcendentals=0),
    )(*args)


def by_core(core, first, second):
    return first + core * (second - first)


def spots(tm, count):
    near, far, rest, step = tm & 1, (tm >> 1) & 1, tm >> 2, count // 4
    return (2 * near + far) * step + rest, (2 * far + near) * step + rest


LABEL_ROWS = 16


def scan(feat, forget):
    rows = feat.shape[0]
    keep, mass, weight = 1.0 - forget, forget * (feat * feat), forget
    row = lax.broadcasted_iota(jnp.int32, feat.shape, 0)
    step = 1
    while step < rows:
        inside = row >= step
        before = jnp.where(inside, pltpu.roll(mass, step, 0), 0.0)
        mass = keep * before + mass
        before = jnp.where(inside, pltpu.roll(weight, step, 0), 0.0)
        weight = keep * before + weight
        keep = keep * jnp.where(inside, pltpu.roll(keep, step, 0), 1.0)
        step *= 2
    return keep, mass, weight


def scan_kernel(feat_ref, forget_ref, keep_ref, mass_ref, weight_ref, carry_ref):
    rows = feat_ref.shape[0]
    values = scan(feat_ref[...], forget_ref[...])
    for k, (ref, value) in enumerate(zip((keep_ref, mass_ref, weight_ref), values)):
        ref[...] = value
        carry_ref[k : k + 1, :] = value[rows - 1 :]


def pack_kernel(feat_ref, forget_ref, conv_ref, res_ref, in_ref, out_ref,
                keep_ref, mass_ref, weight_ref, carry_ref, first_ref, second_ref):
    scan_kernel(feat_ref, forget_ref, keep_ref, mass_ref, weight_ref, carry_ref)
    conv, res, more, c = conv_ref.shape[1], res_ref.shape[1], in_ref.shape[0], first_ref.shape[1]
    for layer, ref in enumerate((first_ref, second_ref)):
        ref[:conv, :] = conv_ref[layer, :, :c]
        ref[conv : 2 * conv, :] = conv_ref[layer, :, c:]
        ref[2 * conv : 2 * conv + res, :] = res_ref[layer]
    at = 2 * conv + res
    first_ref[at : at + more, :] = in_ref[...]
    first_ref[at + more : at + 2 * more, :] = jnp.concatenate(
        [out_ref[k * more : (k + 1) * more, :] for k in range(c // out_ref.shape[1])], axis=1)


def norm_kernel(scalar_ref, feat_ref, keep_ref, mass_ref, weight_ref, carry_ref, label_ref, out_ref, low_ref, high_ref):
    bands = feat_ref.shape[1]
    mass0 = jnp.zeros((1, bands), F32)
    weight0 = jnp.zeros((1, bands), F32)
    for tm in range(carry_ref.shape[0]):
        before = tm < scalar_ref[1]
        keep, mass, weight = (carry_ref[tm, k : k + 1, :] for k in range(3))
        mass0 = jnp.where(before, keep * mass0 + mass, mass0)
        weight0 = jnp.where(before, keep * weight0 + weight, weight0)
    keep = keep_ref[...]
    mass = keep * mass0 + mass_ref[...]
    weight = keep * weight0 + weight_ref[...]
    normed = (feat_ref[...] / jnp.sqrt(mass / weight + LEVEL_FLOOR)).astype(BF16)
    label = jnp.concatenate(
        [label_ref[...].astype(F32), jnp.zeros((LABEL_ROWS - label_ref.shape[0], bands), F32)]).astype(BF16)
    part = low_ref.shape[0] - LABEL_ROWS
    first, last = normed[:part], normed[normed.shape[0] - part :]
    upper = (scalar_ref[1] >> 1) & 1 == 1
    for ref, value in (
        (out_ref, normed), (low_ref, jnp.where(upper, first, last)), (high_ref, jnp.where(upper, last, first))):
        ref[:LABEL_ROWS, :] = label
        ref[LABEL_ROWS:, :] = value


def rows_of(value):
    return value.reshape(-1, value.shape[-1]).astype(BF16)


def halves(conv_ref, gate):
    half = conv_ref.shape[1] // 2
    return rows_of(conv_ref[gate, :half]), rows_of(conv_ref[gate, half:])


def place(core, pair, conv_ref, res_ref, in_ref=None, out_ref=None):
    conv, res = conv_ref.shape[2], res_ref.shape[1]
    for ref, own in zip(pair, (True, False)):
        s = core if own else 1 - core
        rest = ref.shape[0] // 4
        bits = rest.bit_length() - 1
        for second, first in itertools.product((0, 1), repeat=2):

            def put(p, _, second=second, first=first, ref=ref, s=s):
                high = sum(((p >> (bits - 1 - b)) & 1) << b for b in range(bits))
                device = 2 * (4 * high + 2 * by_core(s, second, first) + by_core(s, first, second)) + s
                k = (2 * second + first) * rest + p
                conv_ref[0, device] = ref[k, :conv, :].astype(conv_ref.dtype)
                conv_ref[1, device] = ref[k, conv : 2 * conv, :].astype(conv_ref.dtype)
                res_ref[device] = ref[k, 2 * conv : 2 * conv + res, :].astype(res_ref.dtype)
                if in_ref is not None:
                    value = ref[k, 2 * conv + res :, :].astype(F32)
                    count, classes = value.shape[0] // 2, out_ref.shape[2]
                    in_ref[device] = value[:count]
                    for q in range(value.shape[1] // classes):
                        out_ref[device, q * count : (q + 1) * count, :] = (
                            value[count:, q * classes : (q + 1) * classes])
                return 0

            if rest <= 2:
                for p in range(rest):
                    put(p, 0)
            else:
                lax.fori_loop(0, rest, put, 0)


def activate(past, now, conv_ref):
    joined = jnp.concatenate([past, now], axis=1)
    t = jnp.tanh(dot(joined, rows_of(conv_ref[0])))
    s = 0.5 + 0.5 * jnp.tanh(0.5 * dot(joined, rows_of(conv_ref[1])))
    return t, s


def slopes(t, s):
    return s * (1.0 - t * t), t * s * (1.0 - s)


def tile_of(i, offset=0):
    return slice(i * TILE + offset, (i + 1) * TILE + offset)


def halo(scalar_ref, own_ref, even_ref, odd_ref, low_ref, high_ref, window_ref, label_ref):
    steps, part = own_ref.shape[0] - LABEL_ROWS, low_ref.shape[0] - LABEL_ROWS
    lane = own_ref.shape[1]
    odd, upper = scalar_ref[1] & 1 == 1, (scalar_ref[1] >> 1) & 1 == 1
    even, uneven, low, high = even_ref[...], odd_ref[...], low_ref[...], high_ref[...]
    at, row = 0, 0
    for value, ahead in ((jnp.where(upper, low, high), False), (jnp.where(odd, even, uneven), False),
                         (own_ref[...], True), (jnp.where(odd, uneven, even), True),
                         (jnp.where(upper, high, low), True)):
        count = value.shape[0] - LABEL_ROWS
        window_ref[at : at + count, :] = value[LABEL_ROWS:]
        at += count
        if ahead:
            label_ref[row : row + count // lane, :] = value[:LABEL_ROWS].astype(F32)[: count // lane]
            row += count // lane


def forward_first(before, steps, scalar_ref, own_ref, even_ref, odd_ref, low_ref, high_ref,
                  here_ref, there_ref, h1_ref, w_out_ref, label_ref, kept_ref, gated_ref, slope_ref, conv_ref, res_ref,
                  norm_ref, h0_ref, in_ref, out_ref):
    rows = h0_ref.shape[0]
    kept = slope_ref.shape[1]
    d = rows - h1_ref.shape[0]
    core = scalar_ref[0]
    place(core, (here_ref, there_ref), conv_ref, res_ref, in_ref, out_ref)
    halo(scalar_ref, own_ref, even_ref, odd_ref, low_ref, high_ref, norm_ref, label_ref)
    w_out_ref[...] = rows_of(out_ref[...])
    w_in = rows_of(in_ref[...])
    for i in range(rows // steps):
        at = slice(i * steps, (i + 1) * steps)
        h0_ref[at, :] = dot(norm_ref[at, :], w_in).astype(BF16)
    kept_ref[...] = h0_ref[before : before + kept, :]
    cuts = [0, before, before + steps, before + kept, h1_ref.shape[0]]
    for start, end in zip(cuts, cuts[1:]):
        at = slice(start, end)
        now = h0_ref[start + d : end + d, :]
        t, s = activate(h0_ref[at, :], now, conv_ref)
        gated = (t * s).astype(BF16)
        h1_ref[at, :] = (now.astype(F32) + dot(gated, rows_of(res_ref[...]))).astype(BF16)
        if before <= start < before + kept:
            own = slice(start - before, end - before)
            slope_ref[0, own, :], slope_ref[1, own, :] = (v.astype(BF16) for v in slopes(t, s))
            if start == before:
                gated_ref[...] = gated


def store_terms(core, keep_ref, send_ref, row, value, first, size, start, count, lane=0):
    at = (slice(row, row + count), slice(lane, lane + value.shape[1]))
    for k in range(value.shape[0] // (2 * size)):
        low = value[2 * k * size + start : 2 * k * size + start + count]
        high = value[(2 * k + 1) * size + start : (2 * k + 1) * size + start + count]
        one, two = spots(first + k, keep_ref.shape[0])
        keep_ref[(by_core(core, one, two),) + at] = jnp.where(core == 0, low, high).astype(keep_ref.dtype)
        send_ref[(by_core(core, two, one),) + at] = jnp.where(core == 0, high, low).astype(send_ref.dtype)


def conv_terms(targets, first, size, value):
    c = value.shape[1] // 2
    store_terms(*targets, 0, value[:, :c], first, size, 0, size)
    store_terms(*targets, size, value[:, c:], first, size, 0, size)


def second_kernel(steps, scale, sizes, scalar_ref, h1_ref, w_out_ref, label_ref, here_ref, there_ref,
                  slope0_ref, res0_ref,
                  loss_ref, keep_ref, send_ref, grad0_ref, round0_ref, back0_ref,
                  back_ref, grad_ref, conv_ref, res_ref, gated_ref, h2_ref, lgrad_ref, round_ref):
    rows, c = back_ref.shape[0], grad_ref.shape[1]
    d = h1_ref.shape[0] - rows
    classes = w_out_ref.shape[1]
    conv, res, _, out = sizes
    core = scalar_ref[0]
    place(core, (here_ref, there_ref), conv_ref, res_ref)

    lanes = label_ref.shape[1]
    class_row = lax.broadcasted_iota(jnp.int32, (classes, lanes), 0).astype(F32)
    unit = class_row == lax.broadcasted_iota(jnp.int32, (lanes, lanes), 1).astype(F32)
    cuts = [0, steps, 2 * steps, rows]
    left = scalar_ref[2] - scalar_ref[1] * steps

    for start, end in zip(cuts, cuts[1:]):
        at = slice(start, end)
        row = lax.broadcasted_iota(jnp.int32, (end - start, 1), 0)
        now = h1_ref[start + d : end + d, :]
        t, s = activate(h1_ref[at, :], now, conv_ref)
        gated = (t * s).astype(BF16)
        h2 = (now.astype(F32) + dot(gated, rows_of(res_ref[...]))).astype(BF16)
        logits = dot(h2, w_out_ref[...])
        total = jnp.log(jnp.sum(jnp.exp(logits), axis=1, keepdims=True))
        groups = range(start // lanes, end // lanes)
        hot = jnp.concatenate(
            [(class_row == label_ref[k : k + 1, :]).astype(F32).T for k in groups])
        valid = (row + start < left).astype(F32)
        lgrad = ((jnp.exp(logits - total) - hot) * (valid * scale)).astype(BF16)
        grad = dot_t(lgrad, w_out_ref[...])
        rounded = grad.astype(BF16)
        back = dot_t(rounded, rows_of(res_ref[...]))
        filter_slope, gate_slope = slopes(t, s)
        back_ref[at, :c] = (back * filter_slope).astype(BF16)
        back_ref[at, c:] = (back * gate_slope).astype(BF16)
        kept = min(end, grad_ref.shape[0])
        if start < kept:
            grad_ref[start:kept, :] = grad[: kept - start]
        if start < steps:
            loss = (total - jnp.sum(logits * hot, axis=1, keepdims=True)) * valid
            for j, k in enumerate(groups):
                part = jnp.where(unit, loss[j * lanes : (j + 1) * lanes], 0.0)
                loss_ref[k : k + 1, :] = jnp.sum(part, axis=0, keepdims=True)
            gated_ref[at, :] = gated
            h2_ref[at, :] = h2
            lgrad_ref[at, :] = lgrad
            round_ref[at, :] = rounded

    own = slice(0, steps)
    targets = (core, keep_ref, send_ref)
    for i in range(c // TILE):
        at = tile_of(i)
        first, per = i * (TILE // (2 * conv)), c // (2 * conv)
        conv_terms(targets, first, conv, t_dot(h1_ref[0:steps, at], back_ref[own, :]))
        conv_terms(targets, first + per, conv, t_dot(h1_ref[d : d + steps, at], back_ref[own, :]))
        value = t_dot(gated_ref[own, at], round_ref[own, :])
        store_terms(*targets, 2 * conv, value, i * (TILE // (2 * res)), res, 0, res)
        value = t_dot(h2_ref[own, at], lgrad_ref[own, :])
        count = out * classes // c
        for q in range(c // classes):
            store_terms(*targets, 2 * conv + res, value, i * (TILE // (2 * out)), out, q * count, count, q * classes)

    rows0 = back0_ref.shape[0]
    weights = halves(conv_ref, 0), halves(conv_ref, 1)
    for i in range(rows0 // TILE):
        at = tile_of(i)
        grad = grad_below(grad_ref[at, :], back_ref, i, rows - rows0, weights)
        rounded = grad.astype(BF16)
        back = dot_t(rounded, rows_of(res0_ref[...]))
        back0_ref[at, :c] = (back * slope0_ref[0, at, :].astype(F32)).astype(BF16)
        back0_ref[at, c:] = (back * slope0_ref[1, at, :].astype(F32)).astype(BF16)
        if i * TILE < steps:
            grad0_ref[at, :] = grad
            round0_ref[at, :] = rounded


def grad_below(grad, back_ref, i, d, weights):
    c = back_ref.shape[1] // 2
    (filt_past, filt_now), (gate_past, gate_now) = weights
    grad = grad + dot_t(back_ref[tile_of(i), :c], filt_now) + dot_t(back_ref[tile_of(i), c:], gate_now)
    return grad + dot_t(back_ref[tile_of(i, d), :c], filt_past) + dot_t(back_ref[tile_of(i, d), c:], gate_past)


def terms_first(sizes, scalar_ref, back_ref, grad_ref, round_ref, norm_ref, h0_ref, gated_ref, conv_ref,
                keep_ref, send_ref, last_ref):
    steps, c = grad_ref.shape
    d0 = back_ref.shape[0] - steps
    conv, res, enter, _ = sizes
    own = slice(0, steps)
    targets = (scalar_ref[0], keep_ref, send_ref)
    for i in range(c // TILE):
        at = tile_of(i)
        first, per = i * (TILE // (2 * conv)), c // (2 * conv)
        conv_terms(targets, first, conv, t_dot(h0_ref[0:steps, at], back_ref[own, :]))
        conv_terms(targets, first + per, conv, t_dot(h0_ref[d0 : d0 + steps, at], back_ref[own, :]))
        value = t_dot(gated_ref[:, at], round_ref[...])
        store_terms(*targets, 2 * conv, value, i * (TILE // (2 * res)), res, 0, res)
    weights = halves(conv_ref, 0), halves(conv_ref, 1)
    for i in range(steps // TILE):
        last_ref[tile_of(i), :] = grad_below(grad_ref[tile_of(i), :], back_ref, i, d0, weights).astype(BF16)
    value = t_dot(norm_ref[LABEL_ROWS:, :], last_ref[...])
    store_terms(*targets, 2 * conv + res, value, 0, enter, 0, enter)


def finish_kernel(sizes, one0_ref, two0_ref, one1_ref, two1_ref, conv_ref, res_ref, in_ref, out_ref):
    conv, res, _, _ = sizes
    for layer, (one, two) in enumerate(((one0_ref, two0_ref), (one1_ref, two1_ref))):
        total = one[...].astype(F32) + two[...].astype(F32)
        c = total.shape[1]
        conv_ref[layer, :, :c] = total[:conv]
        conv_ref[layer, :, c:] = total[conv : 2 * conv]
        res_ref[layer] = total[2 * conv : 2 * conv + res]
        rest = total[2 * conv + res :]
        if layer == 0:
            in_ref[...] = rest
        else:
            count, classes = rest.shape[0], out_ref.shape[1]
            for q in range(c // classes):
                out_ref[q * count : (q + 1) * count, :] = rest[:, q * classes : (q + 1) * classes]


NEAR, FAR = ("tm", 0), ("tm", 1)
CORE = ("site", 0)


def swap(value, links):
    count, pairs = lax.axis_size("site"), []
    for tm, site in itertools.product(range(lax.axis_size("tm")), range(count)):
        axis, bit = links[site]
        to = (tm ^ (1 << bit), site) if axis == "tm" else (tm, site ^ (1 << bit))
        pairs.append((tm * count + site, to[0] * count + to[1]))
    return lax.ppermute(value, ("tm", "site"), pairs)


def my_bit(links):
    first, second = ((lax.axis_index(axis) >> bit) & 1 for axis, bit in links)
    return jnp.where(lax.axis_index("site") == 0, first, second)


def time_bits():
    return lax.axis_size("tm").bit_length() - 1


def arranged(held, other, links):
    return jnp.where(
        my_bit(links) == 0, jnp.concatenate([held, other]), jnp.concatenate([other, held]))


def grow(held, links):
    return arranged(held, swap(held, links), links)


def together(*values):
    return lax.optimization_barrier(values)


def half_kernel(bits, sent, scalar_ref, one_ref, two_ref, out_ref):
    position = scalar_ref[1]
    mine = by_core(scalar_ref[0], (position >> bits[0]) & 1, (position >> bits[1]) & 1)
    index = 1 - mine if sent else mine
    for p in range(out_ref.shape[0]):
        out_ref[p] = (one_ref[p, index].astype(F32) + two_ref[p, index].astype(F32)).astype(BF16)


def halves_of(addends, scalars, links, dim):
    shape = addends[0].shape
    outer, rows = math.prod(shape[:dim]), math.prod(shape[dim + 1 : -1])
    flat = [v.reshape(outer, 2, rows, shape[-1]) for v in addends]

    def half(sent):
        bits = tuple(bit for _, bit in links)
        (value,) = call(functools.partial(half_kernel, bits, sent), [((outer, rows, shape[-1]), BF16)], [],
                        2 * 10**8, scalars, *flat)
        return value.reshape(shape[:dim] + (1,) + shape[dim + 1 :])

    return half(False), half(True)


def sum_steps():
    bits = time_bits()
    rest = [((("tm", bit),) * 2, 1 + bits - bit) for bit in range(2, bits)]
    return [((NEAR, FAR), 0), ((FAR, NEAR), 1)] + rest


def exchange(value, reach):
    size, pairs = lax.axis_size("tm"), []
    for i in range(size - reach):
        if (i // reach) % 2 == 1:
            pairs += [(i, i + reach), (i + reach, i)]
    return lax.ppermute(value, "tm", pairs)


def on_device(features, forget, labels, lengths, w_conv, w_res, w_in, w_out):
    _, steps, bands = features.shape
    time_devices, site_devices = lax.axis_size("tm"), lax.axis_size("site")
    devices = time_devices * site_devices
    c = w_res.shape[2]
    classes = w_out.shape[1]
    conv, res, enter, out = sizes = (w_conv.shape[1], w_res.shape[1], w_in.shape[0], w_out.shape[0])
    aligned = conv % 64 == 0 and res % 32 == 0
    kind = BF16 if aligned else F32
    d0, d1 = BASE_DILATION, 2 * BASE_DILATION
    reach = d0 + d1
    scalars = jnp.stack([lax.axis_index("site"), lax.axis_index("tm"), lengths[0]]).astype(jnp.int32)

    feat = features[0]
    scanned = [((steps, bands), F32)] * 3 + [((3, bands), F32)]
    if aligned:
        keep, mass, weight, carry, held0, held1 = call(
            pack_kernel, scanned + [((2 * conv + res + 2 * enter, c), BF16), ((2 * conv + res, c), BF16)], [],
            2 * 10**9, feat, forget[0], w_conv, w_res, w_in, w_out, limit=FIRST_LIMIT)
    else:
        keep, mass, weight, carry = call(scan_kernel, scanned, [], 2 * 10**9, feat, forget[0], limit=FIRST_LIMIT)
        out_own = jnp.concatenate([w_out[k * enter : (k + 1) * enter] for k in range(c // classes)], axis=1)
        held0, held1 = (jnp.concatenate([w_conv[k, :, :c], w_conv[k, :, c:], w_res[k]] + more)
                        for k, more in ((0, [w_in, out_own]), (1, [])))
    held0, held1 = held0[None], held1[None]
    carry = carry[None]
    far = [(("tm", bit),) * 2 for bit in reversed(range(2, time_bits()))]
    turns = [(NEAR, FAR), (FAR, NEAR)]
    for links in far:
        held0 = grow(held0, links)
    for link in (NEAR, FAR):
        carry = grow(carry, (link, link))
    held0, carry, held1 = together(held0, carry, held1)
    held0 = grow(held0, turns[0])
    for links in reversed(far):
        carry = grow(carry, links)
    for links in far:
        held1 = grow(held1, links)
    label_rows = steps // bands
    normed, low, high = call(norm_kernel, [((LABEL_ROWS + r, bands), BF16) for r in (steps, reach - steps, reach - steps)],
                             [], 10**8,
                     scalars, feat, keep, mass, weight, carry, labels[0].reshape(label_rows, bands), limit=FIRST_LIMIT)
    held0, normed, low, high, held1 = together(held0, normed, low, high, held1)
    held0, held1 = grow(held0, turns[1]), grow(held1, turns[0])
    around = [swap(normed, (NEAR, NEAR)), exchange(normed, 1), swap(low, (FAR, FAR)), exchange(high, 2)]
    held0, held1, around = together(held0, held1, around)

    def both_cores(held):
        return held.astype(kind), swap(held, (CORE, CORE)).astype(kind)

    first, other1 = both_cores(held0), swap(held1, turns[1])

    total_rows, rows0, rows1 = steps + 2 * reach, steps + d0, steps + reach
    conv_all, res_all = ((2, devices, conv, c), kind), ((devices, res, c), kind)
    V = pltpu.VMEM
    h1, out_all, label_window, h0, gated0, slope0, conv0, res0 = call(
        functools.partial(forward_first, d1, steps),
        [((total_rows - d0, c), BF16), ((c, classes), BF16), ((rows1 // bands, bands), F32), ((rows0, c), BF16), ((steps, c), BF16),
         ((2, rows0, c), BF16), conv_all, res_all],
        [V((total_rows, bands), BF16), V((total_rows, c), BF16), V((devices, enter, c), F32), V((devices, out, classes), F32)],
        2 * total_rows * c * (bands + 5 * c), scalars, normed, *around, *first)

    other1, h1 = together(other1, h1)
    second = both_cores(arranged(held1, other1, turns[1]))
    scale = 1.0 / math.sqrt(site_devices * steps * time_devices)
    package = [((time_devices, 2 * conv + res + enter, c), kind)] * 2
    loss, keep1, send1, grad1, round0, back0 = call(
        functools.partial(second_kernel, steps, scale, sizes),
        [((label_rows, bands), F32)] + package + [((steps, c), F32), ((steps, c), BF16), ((rows0, 2 * c), BF16)],
        [V((rows1, 2 * c), BF16), V((rows0, c), F32), V(*conv_all), V(*res_all),
         V((steps, c), BF16), V((steps, c), BF16), V((steps, classes), BF16), V((steps, c), BF16)],
        2 * rows1 * c * 6 * c + 2 * steps * 5 * c * c + 2 * rows0 * c * 5 * c,
        scalars, h1, out_all, label_window, *second, slope0, res0)

    def core_step(keep, send):
        other = swap(send.astype(BF16), (CORE, CORE))
        shape = (2,) * time_bits() + keep.shape[1:]
        return [keep.reshape(shape), other.reshape(shape)]

    sums1 = core_step(keep1, send1)
    keep0, send0 = call(
        functools.partial(terms_first, sizes), package, [V((steps, c), BF16)],
        2 * steps * 9 * c * c, scalars, back0, grad1, round0, normed, h0, gated0, conv0)
    sums1, keep0, send0 = together(sums1, keep0, send0)

    order = sum_steps()
    kept1, sent1 = halves_of(sums1, scalars, *order[0])
    other1 = swap(sent1, order[0][0])
    kept0, sent0 = halves_of(core_step(keep0, send0), scalars, *order[0])
    other1, sent0 = together(other1, sent0)
    for step, (links, _) in enumerate(order):
        if step + 1 < len(order):
            kept1, sent1 = halves_of([kept1, other1], scalars, *order[step + 1])
            sent1, sent0 = together(sent1, sent0)
            other1 = swap(sent1, order[step + 1][0])
        other0 = swap(sent0, links)
        if step + 1 < len(order):
            kept0, sent0 = halves_of([kept0, other0], scalars, *order[step + 1])
    sums0, sums1 = [kept0, other0], [kept1, other1]
    rows = 2 * conv + res + enter
    parts = [v.reshape(rows, c) for v in sums0 + sums1]
    grad_conv, grad_res, grad_in, grad_out = call(
        functools.partial(finish_kernel, sizes),
        [((2, conv, 2 * c), F32), ((2, res, c), F32), ((enter, c), F32), ((out, classes), F32)], [], 1,
        *parts)
    return loss.reshape(1, steps), grad_conv, grad_res, grad_in, grad_out


def solution(mesh):
    return jax.shard_map(
        on_device,
        mesh=mesh,
        in_specs=(
            P(("groups", "site"), "tm", None),
            P(("groups", "site"), "tm", None),
            P(("groups", "site"), "tm"),
            P(("groups", "site")),
            P(None, ("tm", "site"), None),
            P(None, ("tm", "site"), None),
            P(("tm", "site"), None),
            P(("tm", "site"), None),
        ),
        out_specs=(
            P(("groups", "site"), "tm"),
            P("groups", ("tm", "site"), None),
            P("groups", ("tm", "site"), None),
            P(("tm", "site"), "groups"),
            P(("tm", "site"), "groups"),
        ),
        check_vma=False,
    )
```

```python
import functools
import itertools
import math

import jax
import jax.numpy as jnp
from jax import lax
from jax.experimental import pallas as pl
from jax.experimental.pallas import tpu as pltpu
from jax.sharding import PartitionSpec as P

BASE_DILATION = 256
LEVEL_FLOOR = 0.1
F32 = jnp.float32
BF16 = jnp.bfloat16
TILE = 256
VMEM_LIMIT = 24 * 1024 * 1024
FIRST_LIMIT = 56 * 1024 * 1024
WHOLE = pl.BlockSpec(memory_space=pltpu.VMEM)
SCALAR = pl.BlockSpec(memory_space=pltpu.SMEM)


def dot(a, b):
    return lax.dot_general(a, b, (((1,), (0,)), ((), ())), preferred_element_type=F32)


def dot_t(a, b):
    return lax.dot_general(a, b, (((1,), (1,)), ((), ())), preferred_element_type=F32)


def t_dot(a, b):
    return lax.dot_general(a, b, (((0,), (0,)), ((), ())), preferred_element_type=F32)


def call(kernel, outs, scratch, flops, *args, limit=VMEM_LIMIT):
    moved = sum(a.size * a.dtype.itemsize for a in args)
    moved += sum(math.prod(s) * jnp.dtype(d).itemsize for s, d in outs)
    return pl.pallas_call(
        kernel,
        out_shape=[jax.ShapeDtypeStruct(s, d) for s, d in outs],
        in_specs=[SCALAR if a.dtype == jnp.int32 and a.ndim == 1 else WHOLE for a in args],
        out_specs=[WHOLE] * len(outs),
        scratch_shapes=scratch,
        compiler_params=pltpu.CompilerParams(vmem_limit_bytes=limit),
        cost_estimate=pl.CostEstimate(flops=flops, bytes_accessed=moved, transcendentals=0),
    )(*args)


def by_core(core, first, second):
    return first + core * (second - first)


def spots(tm, count):
    near, far, rest, step = tm & 1, (tm >> 1) & 1, tm >> 2, count // 4
    return (2 * near + far) * step + rest, (2 * far + near) * step + rest


LABEL_ROWS = 16
WIDE_ROWS = 8


def scan(feat, forget):
    rows = feat.shape[0]
    keep, mass, weight = 1.0 - forget, forget * (feat * feat), forget
    row = lax.broadcasted_iota(jnp.int32, feat.shape, 0)
    step = 1
    while step < rows:
        inside = row >= step
        before = jnp.where(inside, pltpu.roll(mass, step, 0), 0.0)
        mass = keep * before + mass
        before = jnp.where(inside, pltpu.roll(weight, step, 0), 0.0)
        weight = keep * before + weight
        keep = keep * jnp.where(inside, pltpu.roll(keep, step, 0), 1.0)
        step *= 2
    return keep, mass, weight


def scan_kernel(feat_ref, forget_ref, keep_ref, mass_ref, weight_ref, carry_ref):
    rows = feat_ref.shape[0]
    values = scan(feat_ref[...], forget_ref[...])
    for k, (ref, value) in enumerate(zip((keep_ref, mass_ref, weight_ref), values)):
        ref[...] = value
        carry_ref[k : k + 1, :] = value[rows - 1 :]


def pack_kernel(feat_ref, forget_ref, conv_ref, res_ref, in_ref, out_ref,
                keep_ref, mass_ref, weight_ref, carry_ref, first_ref, second_ref):
    scan_kernel(feat_ref, forget_ref, keep_ref, mass_ref, weight_ref, carry_ref)
    conv, res, more, c = conv_ref.shape[1], res_ref.shape[1], in_ref.shape[0], first_ref.shape[1]
    for layer, ref in enumerate((first_ref, second_ref)):
        ref[:conv, :] = conv_ref[layer, :, :c]
        ref[conv : 2 * conv, :] = conv_ref[layer, :, c:]
        ref[2 * conv : 2 * conv + res, :] = res_ref[layer]
    at = 2 * conv + res
    first_ref[at : at + more, :] = in_ref[...]
    first_ref[at + more : at + 2 * more, :] = jnp.concatenate(
        [out_ref[k * more : (k + 1) * more, :] for k in range(c // out_ref.shape[1])], axis=1)


def norm_kernel(scalar_ref, feat_ref, keep_ref, mass_ref, weight_ref, carry_ref, label_ref, out_ref, wide_ref, high_ref):
    bands = feat_ref.shape[1]
    mass0 = jnp.zeros((1, bands), F32)
    weight0 = jnp.zeros((1, bands), F32)
    for tm in range(carry_ref.shape[0]):
        before = tm < scalar_ref[1]
        keep, mass, weight = (carry_ref[tm, k : k + 1, :] for k in range(3))
        mass0 = jnp.where(before, keep * mass0 + mass, mass0)
        weight0 = jnp.where(before, keep * weight0 + weight, weight0)
    keep = keep_ref[...]
    mass = keep * mass0 + mass_ref[...]
    weight = keep * weight0 + weight_ref[...]
    normed = (feat_ref[...] / jnp.sqrt(mass / weight + LEVEL_FLOOR)).astype(BF16)
    label = jnp.concatenate(
        [label_ref[...].astype(F32), jnp.zeros((LABEL_ROWS - label_ref.shape[0], bands), F32)]).astype(BF16)
    part = high_ref.shape[0] - LABEL_ROWS
    first, last = normed[:part], normed[normed.shape[0] - part :]
    upper = (scalar_ref[1] >> 1) & 1 == 1
    for ref, value in ((out_ref, normed), (high_ref, jnp.where(upper, last, first))):
        ref[:LABEL_ROWS, :] = label
        ref[LABEL_ROWS:, :] = value
    high = normed.shape[0] * bands // wide_ref.shape[1]
    wide_ref[high:, :] = jnp.zeros((WIDE_ROWS, wide_ref.shape[1]), BF16)
    for q in range(wide_ref.shape[1] // bands):
        lanes = slice(q * bands, (q + 1) * bands)
        wide_ref[:high, lanes] = normed[q * high : (q + 1) * high]
        wide_ref[high : high + 1, lanes] = label_ref[q : q + 1, :].astype(F32).astype(BF16)


def rows_of(value):
    return value.reshape(-1, value.shape[-1]).astype(BF16)


def halves(conv_ref, gate):
    half = conv_ref.shape[1] // 2
    return rows_of(conv_ref[gate, :half]), rows_of(conv_ref[gate, half:])


def place(core, pair, conv_ref, res_ref, in_ref=None, out_ref=None):
    conv, res = conv_ref.shape[2], res_ref.shape[1]
    for ref, own in zip(pair, (True, False)):
        s = core if own else 1 - core
        rest = ref.shape[0] // 4
        bits = rest.bit_length() - 1
        for second, first in itertools.product((0, 1), repeat=2):

            def put(p, _, second=second, first=first, ref=ref, s=s):
                high = sum(((p >> (bits - 1 - b)) & 1) << b for b in range(bits))
                device = 2 * (4 * high + 2 * by_core(s, second, first) + by_core(s, first, second)) + s
                k = (2 * second + first) * rest + p
                conv_ref[0, device] = ref[k, :conv, :].astype(conv_ref.dtype)
                conv_ref[1, device] = ref[k, conv : 2 * conv, :].astype(conv_ref.dtype)
                res_ref[device] = ref[k, 2 * conv : 2 * conv + res, :].astype(res_ref.dtype)
                if in_ref is not None:
                    value = ref[k, 2 * conv + res :, :].astype(F32)
                    count, classes = value.shape[0] // 2, out_ref.shape[2]
                    in_ref[device] = value[:count]
                    for q in range(value.shape[1] // classes):
                        out_ref[device, q * count : (q + 1) * count, :] = (
                            value[count:, q * classes : (q + 1) * classes])
                return 0

            if rest <= 2:
                for p in range(rest):
                    put(p, 0)
            else:
                lax.fori_loop(0, rest, put, 0)


def activate(past, now, conv_ref):
    joined = jnp.concatenate([past, now], axis=1)
    t = jnp.tanh(dot(joined, rows_of(conv_ref[0])))
    s = 0.5 + 0.5 * jnp.tanh(0.5 * dot(joined, rows_of(conv_ref[1])))
    return t, s


def slopes(t, s):
    return s * (1.0 - t * t), t * s * (1.0 - s)


def tile_of(i, offset=0):
    return slice(i * TILE + offset, (i + 1) * TILE + offset)


def halo(scalar_ref, own_ref, first_ref, second_ref, odd_ref, high_ref, window_ref, label_ref):
    part, lane = high_ref.shape[0] - LABEL_ROWS, own_ref.shape[1]
    core = scalar_ref[0]
    odd, upper = scalar_ref[1] & 1 == 1, (scalar_ref[1] >> 1) & 1 == 1

    def rows_form(wide):
        count = wide.shape[0] - WIDE_ROWS
        groups = [slice(q * lane, (q + 1) * lane) for q in range(wide.shape[1] // lane)]
        rows = jnp.concatenate([wide[:count, g] for g in groups])
        labels = jnp.concatenate([wide[count:, g].astype(F32)[:1] for g in groups])
        return rows, labels

    first, second = first_ref[...], second_ref[...]
    near, near_labels = rows_form(jnp.where(core == 0, first, second))
    far, far_labels = rows_form(jnp.where(core == 0, second, first))
    high, far_high = high_ref[LABEL_ROWS:, :], far.shape[0] - part
    uneven = odd_ref[LABEL_ROWS:, :]
    count = part // lane

    def labels_of(ref):
        return ref[:LABEL_ROWS, :].astype(F32)

    parts = [
        (jnp.where(upper, far[far_high:], high), None),
        (jnp.where(odd, near, uneven), None),
        (own_ref[LABEL_ROWS:, :], labels_of(own_ref)[: near_labels.shape[0]]),
        (jnp.where(odd, uneven, near), jnp.where(odd, labels_of(odd_ref)[: near_labels.shape[0]], near_labels)),
        (jnp.where(upper, high, far[:part]), jnp.where(upper, labels_of(high_ref)[:count], far_labels[:count])),
    ]
    at, row = 0, 0
    for value, labels in parts:
        window_ref[at : at + value.shape[0], :] = value
        at += value.shape[0]
        if labels is not None:
            label_ref[row : row + labels.shape[0], :] = labels
            row += labels.shape[0]


def forward_first(before, steps, scalar_ref, own_ref, near_ref, far_ref, odd_ref, high_ref,
                  here_ref, there_ref, h1_ref, w_out_ref, label_ref, kept_ref, gated_ref, slope_ref, conv_ref, res_ref,
                  norm_ref, h0_ref, in_ref, out_ref):
    rows = h0_ref.shape[0]
    kept = slope_ref.shape[1]
    d = rows - h1_ref.shape[0]
    core = scalar_ref[0]
    place(core, (here_ref, there_ref), conv_ref, res_ref, in_ref, out_ref)
    halo(scalar_ref, own_ref, near_ref, far_ref, odd_ref, high_ref, norm_ref, label_ref)
    w_out_ref[...] = rows_of(out_ref[...])
    w_in = rows_of(in_ref[...])
    for i in range(rows // steps):
        at = slice(i * steps, (i + 1) * steps)
        h0_ref[at, :] = dot(norm_ref[at, :], w_in).astype(BF16)
    kept_ref[...] = h0_ref[before : before + kept, :]
    cuts = [0, before, before + steps, before + kept, h1_ref.shape[0]]
    for start, end in zip(cuts, cuts[1:]):
        at = slice(start, end)
        now = h0_ref[start + d : end + d, :]
        t, s = activate(h0_ref[at, :], now, conv_ref)
        gated = (t * s).astype(BF16)
        h1_ref[at, :] = (now.astype(F32) + dot(gated, rows_of(res_ref[...]))).astype(BF16)
        if before <= start < before + kept:
            own = slice(start - before, end - before)
            slope_ref[0, own, :], slope_ref[1, own, :] = (v.astype(BF16) for v in slopes(t, s))
            if start == before:
                gated_ref[...] = gated


def store_terms(core, keep_ref, send_ref, row, value, first, size, start, count, lane=0):
    at = (slice(row, row + count), slice(lane, lane + value.shape[1]))
    for k in range(value.shape[0] // (2 * size)):
        low = value[2 * k * size + start : 2 * k * size + start + count]
        high = value[(2 * k + 1) * size + start : (2 * k + 1) * size + start + count]
        one, two = spots(first + k, keep_ref.shape[0])
        keep_ref[(by_core(core, one, two),) + at] = jnp.where(core == 0, low, high).astype(keep_ref.dtype)
        send_ref[(by_core(core, two, one),) + at] = jnp.where(core == 0, high, low).astype(send_ref.dtype)


def conv_terms(targets, first, size, value):
    c = value.shape[1] // 2
    store_terms(*targets, 0, value[:, :c], first, size, 0, size)
    store_terms(*targets, size, value[:, c:], first, size, 0, size)


def second_kernel(steps, scale, sizes, scalar_ref, h1_ref, w_out_ref, label_ref, here_ref, there_ref,
                  slope0_ref, res0_ref,
                  loss_ref, keep_ref, send_ref, grad0_ref, round0_ref, back0_ref,
                  back_ref, grad_ref, conv_ref, res_ref, gated_ref, h2_ref, lgrad_ref, round_ref):
    rows, c = back_ref.shape[0], grad_ref.shape[1]
    d = h1_ref.shape[0] - rows
    classes = w_out_ref.shape[1]
    conv, res, _, out = sizes
    core = scalar_ref[0]
    place(core, (here_ref, there_ref), conv_ref, res_ref)

    lanes = label_ref.shape[1]
    class_row = lax.broadcasted_iota(jnp.int32, (classes, lanes), 0).astype(F32)
    unit = class_row == lax.broadcasted_iota(jnp.int32, (lanes, lanes), 1).astype(F32)
    cuts = [0, steps, 2 * steps, rows]
    left = scalar_ref[2] - scalar_ref[1] * steps

    for start, end in zip(cuts, cuts[1:]):
        at = slice(start, end)
        row = lax.broadcasted_iota(jnp.int32, (end - start, 1), 0)
        now = h1_ref[start + d : end + d, :]
        t, s = activate(h1_ref[at, :], now, conv_ref)
        gated = (t * s).astype(BF16)
        h2 = (now.astype(F32) + dot(gated, rows_of(res_ref[...]))).astype(BF16)
        logits = dot(h2, w_out_ref[...])
        total = jnp.log(jnp.sum(jnp.exp(logits), axis=1, keepdims=True))
        groups = range(start // lanes, end // lanes)
        hot = jnp.concatenate(
            [(class_row == label_ref[k : k + 1, :]).astype(F32).T for k in groups])
        valid = (row + start < left).astype(F32)
        lgrad = ((jnp.exp(logits - total) - hot) * (valid * scale)).astype(BF16)
        grad = dot_t(lgrad, w_out_ref[...])
        rounded = grad.astype(BF16)
        back = dot_t(rounded, rows_of(res_ref[...]))
        filter_slope, gate_slope = slopes(t, s)
        back_ref[at, :c] = (back * filter_slope).astype(BF16)
        back_ref[at, c:] = (back * gate_slope).astype(BF16)
        kept = min(end, grad_ref.shape[0])
        if start < kept:
            grad_ref[start:kept, :] = grad[: kept - start]
        if start < steps:
            loss = (total - jnp.sum(logits * hot, axis=1, keepdims=True)) * valid
            for j, k in enumerate(groups):
                part = jnp.where(unit, loss[j * lanes : (j + 1) * lanes], 0.0)
                loss_ref[k : k + 1, :] = jnp.sum(part, axis=0, keepdims=True)
            gated_ref[at, :] = gated
            h2_ref[at, :] = h2
            lgrad_ref[at, :] = lgrad
            round_ref[at, :] = rounded

    own = slice(0, steps)
    targets = (core, keep_ref, send_ref)
    for i in range(c // TILE):
        at = tile_of(i)
        first, per = i * (TILE // (2 * conv)), c // (2 * conv)
        conv_terms(targets, first, conv, t_dot(h1_ref[0:steps, at], back_ref[own, :]))
        conv_terms(targets, first + per, conv, t_dot(h1_ref[d : d + steps, at], back_ref[own, :]))
        value = t_dot(gated_ref[own, at], round_ref[own, :])
        store_terms(*targets, 2 * conv, value, i * (TILE // (2 * res)), res, 0, res)
        value = t_dot(h2_ref[own, at], lgrad_ref[own, :])
        count = out * classes // c
        for q in range(c // classes):
            store_terms(*targets, 2 * conv + res, value, i * (TILE // (2 * out)), out, q * count, count, q * classes)

    rows0 = back0_ref.shape[0]
    weights = halves(conv_ref, 0), halves(conv_ref, 1)
    for i in range(rows0 // TILE):
        at = tile_of(i)
        grad = grad_below(grad_ref[at, :], back_ref, i, rows - rows0, weights)
        rounded = grad.astype(BF16)
        back = dot_t(rounded, rows_of(res0_ref[...]))
        back0_ref[at, :c] = (back * slope0_ref[0, at, :].astype(F32)).astype(BF16)
        back0_ref[at, c:] = (back * slope0_ref[1, at, :].astype(F32)).astype(BF16)
        if i * TILE < steps:
            grad0_ref[at, :] = grad
            round0_ref[at, :] = rounded


def grad_below(grad, back_ref, i, d, weights):
    c = back_ref.shape[1] // 2
    (filt_past, filt_now), (gate_past, gate_now) = weights
    grad = grad + dot_t(back_ref[tile_of(i), :c], filt_now) + dot_t(back_ref[tile_of(i), c:], gate_now)
    return grad + dot_t(back_ref[tile_of(i, d), :c], filt_past) + dot_t(back_ref[tile_of(i, d), c:], gate_past)


def terms_first(sizes, scalar_ref, back_ref, grad_ref, round_ref, norm_ref, h0_ref, gated_ref, conv_ref,
                keep_ref, send_ref, last_ref):
    steps, c = grad_ref.shape
    d0 = back_ref.shape[0] - steps
    conv, res, enter, _ = sizes
    own = slice(0, steps)
    targets = (scalar_ref[0], keep_ref, send_ref)
    for i in range(c // TILE):
        at = tile_of(i)
        first, per = i * (TILE // (2 * conv)), c // (2 * conv)
        conv_terms(targets, first, conv, t_dot(h0_ref[0:steps, at], back_ref[own, :]))
        conv_terms(targets, first + per, conv, t_dot(h0_ref[d0 : d0 + steps, at], back_ref[own, :]))
        value = t_dot(gated_ref[:, at], round_ref[...])
        store_terms(*targets, 2 * conv, value, i * (TILE // (2 * res)), res, 0, res)
    weights = halves(conv_ref, 0), halves(conv_ref, 1)
    for i in range(steps // TILE):
        last_ref[tile_of(i), :] = grad_below(grad_ref[tile_of(i), :], back_ref, i, d0, weights).astype(BF16)
    value = t_dot(norm_ref[LABEL_ROWS:, :], last_ref[...])
    store_terms(*targets, 2 * conv + res, value, 0, enter, 0, enter)


def finish_kernel(sizes, one0_ref, two0_ref, one1_ref, two1_ref, conv_ref, res_ref, in_ref, out_ref):
    conv, res, _, _ = sizes
    for layer, (one, two) in enumerate(((one0_ref, two0_ref), (one1_ref, two1_ref))):
        total = one[...].astype(F32) + two[...].astype(F32)
        c = total.shape[1]
        conv_ref[layer, :, :c] = total[:conv]
        conv_ref[layer, :, c:] = total[conv : 2 * conv]
        res_ref[layer] = total[2 * conv : 2 * conv + res]
        rest = total[2 * conv + res :]
        if layer == 0:
            in_ref[...] = rest
        else:
            count, classes = rest.shape[0], out_ref.shape[1]
            for q in range(c // classes):
                out_ref[q * count : (q + 1) * count, :] = rest[:, q * classes : (q + 1) * classes]


NEAR, FAR = ("tm", 0), ("tm", 1)
CORE = ("site", 0)


def swap(value, links):
    count, pairs = lax.axis_size("site"), []
    for tm, site in itertools.product(range(lax.axis_size("tm")), range(count)):
        axis, bit = links[site]
        to = (tm ^ (1 << bit), site) if axis == "tm" else (tm, site ^ (1 << bit))
        pairs.append((tm * count + site, to[0] * count + to[1]))
    return lax.ppermute(value, ("tm", "site"), pairs)


def my_bit(links):
    first, second = ((lax.axis_index(axis) >> bit) & 1 for axis, bit in links)
    return jnp.where(lax.axis_index("site") == 0, first, second)


def time_bits():
    return lax.axis_size("tm").bit_length() - 1


def arranged(held, other, links):
    return jnp.where(
        my_bit(links) == 0, jnp.concatenate([held, other]), jnp.concatenate([other, held]))


def grow(held, links):
    return arranged(held, swap(held, links), links)


def together(*values):
    return lax.optimization_barrier(values)


def half_kernel(bits, sent, scalar_ref, one_ref, two_ref, out_ref):
    position = scalar_ref[1]
    mine = by_core(scalar_ref[0], (position >> bits[0]) & 1, (position >> bits[1]) & 1)
    index = 1 - mine if sent else mine
    for p in range(out_ref.shape[0]):
        out_ref[p] = (one_ref[p, index].astype(F32) + two_ref[p, index].astype(F32)).astype(BF16)


def halves_of(addends, scalars, links, dim):
    shape = addends[0].shape
    outer, rows = math.prod(shape[:dim]), math.prod(shape[dim + 1 : -1])
    flat = [v.reshape(outer, 2, rows, shape[-1]) for v in addends]

    def half(sent):
        bits = tuple(bit for _, bit in links)
        (value,) = call(functools.partial(half_kernel, bits, sent), [((outer, rows, shape[-1]), BF16)], [],
                        2 * 10**8, scalars, *flat)
        return value.reshape(shape[:dim] + (1,) + shape[dim + 1 :])

    return half(False), half(True)


def sum_steps():
    bits = time_bits()
    rest = [((("tm", bit),) * 2, 1 + bits - bit) for bit in range(2, bits)]
    return [((NEAR, FAR), 0), ((FAR, NEAR), 1)] + rest


def exchange(value, reach):
    size, pairs = lax.axis_size("tm"), []
    for i in range(size - reach):
        if (i // reach) % 2 == 1:
            pairs += [(i, i + reach), (i + reach, i)]
    return lax.ppermute(value, "tm", pairs)


def on_device(features, forget, labels, lengths, w_conv, w_res, w_in, w_out):
    _, steps, bands = features.shape
    time_devices, site_devices = lax.axis_size("tm"), lax.axis_size("site")
    devices = time_devices * site_devices
    c = w_res.shape[2]
    classes = w_out.shape[1]
    conv, res, enter, out = sizes = (w_conv.shape[1], w_res.shape[1], w_in.shape[0], w_out.shape[0])
    aligned = conv % 64 == 0 and res % 32 == 0
    kind = BF16 if aligned else F32
    d0, d1 = BASE_DILATION, 2 * BASE_DILATION
    reach = d0 + d1
    scalars = jnp.stack([lax.axis_index("site"), lax.axis_index("tm"), lengths[0]]).astype(jnp.int32)

    feat = features[0]
    scanned = [((steps, bands), F32)] * 3 + [((3, bands), F32)]
    if aligned:
        keep, mass, weight, carry, held0, held1 = call(
            pack_kernel, scanned + [((2 * conv + res + 2 * enter, c), BF16), ((2 * conv + res, c), BF16)], [],
            2 * 10**9, feat, forget[0], w_conv, w_res, w_in, w_out, limit=FIRST_LIMIT)
    else:
        keep, mass, weight, carry = call(scan_kernel, scanned, [], 2 * 10**9, feat, forget[0], limit=FIRST_LIMIT)
        out_own = jnp.concatenate([w_out[k * enter : (k + 1) * enter] for k in range(c // classes)], axis=1)
        held0, held1 = (jnp.concatenate([w_conv[k, :, :c], w_conv[k, :, c:], w_res[k]] + more)
                        for k, more in ((0, [w_in, out_own]), (1, [])))
    held0, held1 = held0[None], held1[None]
    carry = carry[None]
    far = [(("tm", bit),) * 2 for bit in reversed(range(2, time_bits()))]
    turns = [(NEAR, FAR), (FAR, NEAR)]
    for links in far:
        held0 = grow(held0, links)
    for link in (NEAR, FAR):
        carry = grow(carry, (link, link))
    held0, carry, held1 = together(held0, carry, held1)
    held0 = grow(held0, turns[0])
    for links in reversed(far):
        carry = grow(carry, links)
    for links in far:
        held1 = grow(held1, links)
    label_rows = steps // bands
    wide_rows = steps * bands // c + WIDE_ROWS
    normed, wide, high = call(
        norm_kernel,
        [((LABEL_ROWS + steps, bands), BF16), ((wide_rows, c), BF16), ((LABEL_ROWS + reach - steps, bands), BF16)],
                             [], 10**8,
                     scalars, feat, keep, mass, weight, carry, labels[0].reshape(label_rows, bands), limit=FIRST_LIMIT)
    held0, normed, wide, high, held1 = together(held0, normed, wide, high, held1)

    def grow_with(held, links):
        rows = held.shape[0] * held.shape[1]
        other = swap(jnp.concatenate([held.reshape(rows, c), wide]), links)
        return arranged(held, other[:rows].reshape(held.shape), links), other[rows:]

    held0, second_wide = grow_with(held0, turns[1])
    held1, first_wide = grow_with(held1, turns[0])
    around = [first_wide, second_wide, exchange(normed, 1), exchange(high, 2)]
    held0, held1, around = together(held0, held1, around)

    def both_cores(held):
        return held.astype(kind), swap(held, (CORE, CORE)).astype(kind)

    first, other1 = both_cores(held0), swap(held1, turns[1])

    total_rows, rows0, rows1 = steps + 2 * reach, steps + d0, steps + reach
    conv_all, res_all = ((2, devices, conv, c), kind), ((devices, res, c), kind)
    V = pltpu.VMEM
    h1, out_all, label_window, h0, gated0, slope0, conv0, res0 = call(
        functools.partial(forward_first, d1, steps),
        [((total_rows - d0, c), BF16), ((c, classes), BF16), ((rows1 // bands, bands), F32), ((rows0, c), BF16), ((steps, c), BF16),
         ((2, rows0, c), BF16), conv_all, res_all],
        [V((total_rows, bands), BF16), V((total_rows, c), BF16), V((devices, enter, c), F32), V((devices, out, classes), F32)],
        2 * total_rows * c * (bands + 5 * c), scalars, normed, *around, *first)

    other1, h1 = together(other1, h1)
    second = both_cores(arranged(held1, other1, turns[1]))
    scale = 1.0 / math.sqrt(site_devices * steps * time_devices)
    package = [((time_devices, 2 * conv + res + enter, c), kind)] * 2
    loss, keep1, send1, grad1, round0, back0 = call(
        functools.partial(second_kernel, steps, scale, sizes),
        [((label_rows, bands), F32)] + package + [((steps, c), F32), ((steps, c), BF16), ((rows0, 2 * c), BF16)],
        [V((rows1, 2 * c), BF16), V((rows0, c), F32), V(*conv_all), V(*res_all),
         V((steps, c), BF16), V((steps, c), BF16), V((steps, classes), BF16), V((steps, c), BF16)],
        2 * rows1 * c * 6 * c + 2 * steps * 5 * c * c + 2 * rows0 * c * 5 * c,
        scalars, h1, out_all, label_window, *second, slope0, res0)

    def core_step(keep, send):
        other = swap(send.astype(BF16), (CORE, CORE))
        shape = (2,) * time_bits() + keep.shape[1:]
        return [keep.reshape(shape), other.reshape(shape)]

    sums1 = core_step(keep1, send1)
    keep0, send0 = call(
        functools.partial(terms_first, sizes), package, [V((steps, c), BF16)],
        2 * steps * 9 * c * c, scalars, back0, grad1, round0, normed, h0, gated0, conv0)
    sums1, keep0, send0 = together(sums1, keep0, send0)

    order = sum_steps()
    kept1, sent1 = halves_of(sums1, scalars, *order[0])
    other1 = swap(sent1, order[0][0])
    kept0, sent0 = halves_of(core_step(keep0, send0), scalars, *order[0])
    other1, sent0 = together(other1, sent0)
    for step, (links, _) in enumerate(order):
        if step + 1 < len(order):
            kept1, sent1 = halves_of([kept1, other1], scalars, *order[step + 1])
            sent1, sent0 = together(sent1, sent0)
            other1 = swap(sent1, order[step + 1][0])
        other0 = swap(sent0, links)
        if step + 1 < len(order):
            kept0, sent0 = halves_of([kept0, other0], scalars, *order[step + 1])
    sums0, sums1 = [kept0, other0], [kept1, other1]
    rows = 2 * conv + res + enter
    parts = [v.reshape(rows, c) for v in sums0 + sums1]
    grad_conv, grad_res, grad_in, grad_out = call(
        functools.partial(finish_kernel, sizes),
        [((2, conv, 2 * c), F32), ((2, res, c), F32), ((enter, c), F32), ((out, classes), F32)], [], 1,
        *parts)
    return loss.reshape(1, steps), grad_conv, grad_res, grad_in, grad_out


def solution(mesh):
    return jax.shard_map(
        on_device,
        mesh=mesh,
        in_specs=(
            P(("groups", "site"), "tm", None),
            P(("groups", "site"), "tm", None),
            P(("groups", "site"), "tm"),
            P(("groups", "site")),
            P(None, ("tm", "site"), None),
            P(None, ("tm", "site"), None),
            P(("tm", "site"), None),
            P(("tm", "site"), None),
        ),
        out_specs=(
            P(("groups", "site"), "tm"),
            P("groups", ("tm", "site"), None),
            P("groups", ("tm", "site"), None),
            P(("tm", "site"), "groups"),
            P(("tm", "site"), "groups"),
        ),
        check_vma=False,
    )
```

```python
import functools
import itertools
import math

import jax
import jax.numpy as jnp
from jax import lax
from jax.experimental import pallas as pl
from jax.experimental.pallas import tpu as pltpu
from jax.sharding import PartitionSpec as P

BASE_DILATION = 256
LEVEL_FLOOR = 0.1
F32 = jnp.float32
BF16 = jnp.bfloat16
TILE = 256
VMEM_LIMIT = 24 * 1024 * 1024
FIRST_LIMIT = 56 * 1024 * 1024
WHOLE = pl.BlockSpec(memory_space=pltpu.VMEM)
SCALAR = pl.BlockSpec(memory_space=pltpu.SMEM)


def dot(a, b):
    return lax.dot_general(a, b, (((1,), (0,)), ((), ())), preferred_element_type=F32)


def dot_t(a, b):
    return lax.dot_general(a, b, (((1,), (1,)), ((), ())), preferred_element_type=F32)


def t_dot(a, b):
    return lax.dot_general(a, b, (((0,), (0,)), ((), ())), preferred_element_type=F32)


def call(kernel, outs, scratch, flops, *args, limit=VMEM_LIMIT):
    moved = sum(a.size * a.dtype.itemsize for a in args)
    moved += sum(math.prod(s) * jnp.dtype(d).itemsize for s, d in outs)
    return pl.pallas_call(
        kernel,
        out_shape=[jax.ShapeDtypeStruct(s, d) for s, d in outs],
        in_specs=[SCALAR if a.dtype == jnp.int32 and a.ndim == 1 else WHOLE for a in args],
        out_specs=[WHOLE] * len(outs),
        scratch_shapes=scratch,
        compiler_params=pltpu.CompilerParams(vmem_limit_bytes=limit),
        cost_estimate=pl.CostEstimate(flops=flops, bytes_accessed=moved, transcendentals=0),
    )(*args)


def by_core(core, first, second):
    return first + core * (second - first)


def spots(tm, count):
    near, far, rest, step = tm & 1, (tm >> 1) & 1, tm >> 2, count // 4
    return (2 * near + far) * step + rest, (2 * far + near) * step + rest


LABEL_ROWS = 16
WIDE_ROWS = 8


def scan(feat, forget):
    rows = feat.shape[0]
    keep, mass, weight = 1.0 - forget, forget * (feat * feat), forget
    row = lax.broadcasted_iota(jnp.int32, feat.shape, 0)
    step = 1
    while step < rows:
        inside = row >= step
        before = jnp.where(inside, pltpu.roll(mass, step, 0), 0.0)
        mass = keep * before + mass
        before = jnp.where(inside, pltpu.roll(weight, step, 0), 0.0)
        weight = keep * before + weight
        keep = keep * jnp.where(inside, pltpu.roll(keep, step, 0), 1.0)
        step *= 2
    return keep, mass, weight


def scan_kernel(feat_ref, forget_ref, keep_ref, mass_ref, weight_ref, carry_ref):
    rows = feat_ref.shape[0]
    values = scan(feat_ref[...], forget_ref[...])
    for k, (ref, value) in enumerate(zip((keep_ref, mass_ref, weight_ref), values)):
        ref[...] = value
        carry_ref[k : k + 1, :] = value[rows - 1 :]


def pack_kernel(feat_ref, forget_ref, conv_ref, res_ref, in_ref, out_ref,
                keep_ref, mass_ref, weight_ref, carry_ref, first_ref, second_ref):
    scan_kernel(feat_ref, forget_ref, keep_ref, mass_ref, weight_ref, carry_ref)
    conv, res, more, c = conv_ref.shape[1], res_ref.shape[1], in_ref.shape[0], first_ref.shape[1]
    for layer, ref in enumerate((first_ref, second_ref)):
        ref[:conv, :] = conv_ref[layer, :, :c]
        ref[conv : 2 * conv, :] = conv_ref[layer, :, c:]
        ref[2 * conv : 2 * conv + res, :] = res_ref[layer]
    at = 2 * conv + res
    first_ref[at : at + more, :] = in_ref[...]
    first_ref[at + more : at + 2 * more, :] = jnp.concatenate(
        [out_ref[k * more : (k + 1) * more, :] for k in range(c // out_ref.shape[1])], axis=1)


def norm_kernel(scalar_ref, feat_ref, keep_ref, mass_ref, weight_ref, carry_ref, label_ref, out_ref, wide_ref, high_ref):
    bands = feat_ref.shape[1]
    mass0 = jnp.zeros((1, bands), F32)
    weight0 = jnp.zeros((1, bands), F32)
    for tm in range(carry_ref.shape[0]):
        before = tm < scalar_ref[1]
        keep, mass, weight = (carry_ref[tm, k : k + 1, :] for k in range(3))
        mass0 = jnp.where(before, keep * mass0 + mass, mass0)
        weight0 = jnp.where(before, keep * weight0 + weight, weight0)
    keep = keep_ref[...]
    mass = keep * mass0 + mass_ref[...]
    weight = keep * weight0 + weight_ref[...]
    normed = (feat_ref[...] / jnp.sqrt(mass / weight + LEVEL_FLOOR)).astype(BF16)
    label = jnp.concatenate(
        [label_ref[...].astype(F32), jnp.zeros((LABEL_ROWS - label_ref.shape[0], bands), F32)]).astype(BF16)
    part = high_ref.shape[0] - LABEL_ROWS
    first, last = normed[:part], normed[normed.shape[0] - part :]
    upper = (scalar_ref[1] >> 1) & 1 == 1
    for ref, value in ((out_ref, normed), (high_ref, jnp.where(upper, last, first))):
        ref[:LABEL_ROWS, :] = label
        ref[LABEL_ROWS:, :] = value
    high = normed.shape[0] * bands // wide_ref.shape[1]
    wide_ref[high:, :] = jnp.zeros((WIDE_ROWS, wide_ref.shape[1]), BF16)
    for q in range(wide_ref.shape[1] // bands):
        lanes = slice(q * bands, (q + 1) * bands)
        wide_ref[:high, lanes] = normed[q * high : (q + 1) * high]
        wide_ref[high : high + 1, lanes] = label_ref[q : q + 1, :].astype(F32).astype(BF16)


def rows_of(value):
    return value.reshape(-1, value.shape[-1]).astype(BF16)


def halves(conv_ref, gate):
    half = conv_ref.shape[1] // 2
    return rows_of(conv_ref[gate, :half]), rows_of(conv_ref[gate, half:])


def place(core, pair, conv_ref, res_ref, in_ref=None, out_ref=None):
    conv, res = conv_ref.shape[2], res_ref.shape[1]
    for ref, own in zip(pair, (True, False)):
        s = core if own else 1 - core
        rest = ref.shape[0] // 4
        bits = rest.bit_length() - 1
        for second, first in itertools.product((0, 1), repeat=2):

            def put(p, _, second=second, first=first, ref=ref, s=s):
                high = sum(((p >> (bits - 1 - b)) & 1) << b for b in range(bits))
                device = 2 * (4 * high + 2 * by_core(s, second, first) + by_core(s, first, second)) + s
                k = (2 * second + first) * rest + p
                conv_ref[0, device] = ref[k, :conv, :].astype(conv_ref.dtype)
                conv_ref[1, device] = ref[k, conv : 2 * conv, :].astype(conv_ref.dtype)
                res_ref[device] = ref[k, 2 * conv : 2 * conv + res, :].astype(res_ref.dtype)
                if in_ref is not None:
                    value = ref[k, 2 * conv + res :, :].astype(F32)
                    count, classes = value.shape[0] // 2, out_ref.shape[2]
                    in_ref[device] = value[:count]
                    for q in range(value.shape[1] // classes):
                        out_ref[device, q * count : (q + 1) * count, :] = (
                            value[count:, q * classes : (q + 1) * classes])
                return 0

            if rest <= 2:
                for p in range(rest):
                    put(p, 0)
            else:
                lax.fori_loop(0, rest, put, 0)


def activate(past, now, conv_ref):
    joined = jnp.concatenate([past, now], axis=1)
    t = jnp.tanh(dot(joined, rows_of(conv_ref[0])))
    s = 0.5 + 0.5 * jnp.tanh(0.5 * dot(joined, rows_of(conv_ref[1])))
    return t, s


def slopes(t, s):
    return s * (1.0 - t * t), t * s * (1.0 - s)


def tile_of(i, offset=0):
    return slice(i * TILE + offset, (i + 1) * TILE + offset)


def halo(scalar_ref, own_ref, first_ref, second_ref, odd_ref, high_ref, window_ref, label_ref):
    part, lane = high_ref.shape[0] - LABEL_ROWS, own_ref.shape[1]
    core = scalar_ref[0]
    odd, upper = scalar_ref[1] & 1 == 1, (scalar_ref[1] >> 1) & 1 == 1

    def rows_form(wide):
        count = wide.shape[0] - WIDE_ROWS
        groups = [slice(q * lane, (q + 1) * lane) for q in range(wide.shape[1] // lane)]
        rows = jnp.concatenate([wide[:count, g] for g in groups])
        labels = jnp.concatenate([wide[count:, g].astype(F32)[:1] for g in groups])
        return rows, labels

    first, second = first_ref[...], second_ref[...]
    near, near_labels = rows_form(jnp.where(core == 0, first, second))
    far, far_labels = rows_form(jnp.where(core == 0, second, first))
    high, far_high = high_ref[LABEL_ROWS:, :], far.shape[0] - part
    uneven = odd_ref[LABEL_ROWS:, :]
    count = part // lane

    def labels_of(ref):
        return ref[:LABEL_ROWS, :].astype(F32)

    parts = [
        (jnp.where(upper, far[far_high:], high), None),
        (jnp.where(odd, near, uneven), None),
        (own_ref[LABEL_ROWS:, :], labels_of(own_ref)[: near_labels.shape[0]]),
        (jnp.where(odd, uneven, near), jnp.where(odd, labels_of(odd_ref)[: near_labels.shape[0]], near_labels)),
        (jnp.where(upper, high, far[:part]), jnp.where(upper, labels_of(high_ref)[:count], far_labels[:count])),
    ]
    at, row = 0, 0
    for value, labels in parts:
        window_ref[at : at + value.shape[0], :] = value
        at += value.shape[0]
        if labels is not None:
            label_ref[row : row + labels.shape[0], :] = labels
            row += labels.shape[0]


def forward_first(before, steps, scalar_ref, own_ref, near_ref, far_ref, odd_ref, high_ref,
                  here_ref, there_ref, h1_ref, w_out_ref, label_ref, kept_ref, gated_ref, slope_ref, conv_ref, res_ref,
                  norm_ref, h0_ref, in_ref, out_ref):
    rows = h0_ref.shape[0]
    kept = slope_ref.shape[1]
    d = rows - h1_ref.shape[0]
    core = scalar_ref[0]
    place(core, (here_ref, there_ref), conv_ref, res_ref, in_ref, out_ref)
    halo(scalar_ref, own_ref, near_ref, far_ref, odd_ref, high_ref, norm_ref, label_ref)
    w_out_ref[...] = rows_of(out_ref[...])
    w_in = rows_of(in_ref[...])
    for i in range(rows // steps):
        at = slice(i * steps, (i + 1) * steps)
        h0_ref[at, :] = dot(norm_ref[at, :], w_in).astype(BF16)
    kept_ref[...] = h0_ref[before : before + kept, :]
    cuts = [0, before, before + steps, before + kept, h1_ref.shape[0]]
    for start, end in zip(cuts, cuts[1:]):
        at = slice(start, end)
        now = h0_ref[start + d : end + d, :]
        t, s = activate(h0_ref[at, :], now, conv_ref)
        gated = (t * s).astype(BF16)
        h1_ref[at, :] = (now.astype(F32) + dot(gated, rows_of(res_ref[...]))).astype(BF16)
        if before <= start < before + kept:
            own = slice(start - before, end - before)
            slope_ref[0, own, :], slope_ref[1, own, :] = (v.astype(BF16) for v in slopes(t, s))
            if start == before:
                gated_ref[...] = gated


def store_terms(core, keep_ref, send_ref, row, value, first, size, start, count, lane=0):
    at = (slice(row, row + count), slice(lane, lane + value.shape[1]))
    for k in range(value.shape[0] // (2 * size)):
        low = value[2 * k * size + start : 2 * k * size + start + count]
        high = value[(2 * k + 1) * size + start : (2 * k + 1) * size + start + count]
        one, two = spots(first + k, keep_ref.shape[0])
        keep_ref[(by_core(core, one, two),) + at] = jnp.where(core == 0, low, high).astype(keep_ref.dtype)
        send_ref[(by_core(core, two, one),) + at] = jnp.where(core == 0, high, low).astype(send_ref.dtype)


def conv_terms(targets, first, size, value):
    c = value.shape[1] // 2
    store_terms(*targets, 0, value[:, :c], first, size, 0, size)
    store_terms(*targets, size, value[:, c:], first, size, 0, size)


def second_kernel(steps, scale, sizes, scalar_ref, h1_ref, w_out_ref, label_ref, here_ref, there_ref,
                  slope0_ref, res0_ref,
                  loss_ref, keep_ref, send_ref, grad0_ref, round0_ref, back0_ref,
                  back_ref, grad_ref, conv_ref, res_ref, gated_ref, h2_ref, lgrad_ref, round_ref):
    rows, c = back_ref.shape[0], grad_ref.shape[1]
    d = h1_ref.shape[0] - rows
    classes = w_out_ref.shape[1]
    conv, res, _, out = sizes
    core = scalar_ref[0]
    place(core, (here_ref, there_ref), conv_ref, res_ref)

    lanes = label_ref.shape[1]
    class_row = lax.broadcasted_iota(jnp.int32, (classes, lanes), 0).astype(F32)
    unit = class_row == lax.broadcasted_iota(jnp.int32, (lanes, lanes), 1).astype(F32)
    cuts = [0, steps, 2 * steps, rows]
    left = scalar_ref[2] - scalar_ref[1] * steps

    for start, end in zip(cuts, cuts[1:]):
        at = slice(start, end)
        row = lax.broadcasted_iota(jnp.int32, (end - start, 1), 0)
        now = h1_ref[start + d : end + d, :]
        t, s = activate(h1_ref[at, :], now, conv_ref)
        gated = (t * s).astype(BF16)
        h2 = (now.astype(F32) + dot(gated, rows_of(res_ref[...]))).astype(BF16)
        logits = dot(h2, w_out_ref[...])
        total = jnp.log(jnp.sum(jnp.exp(logits), axis=1, keepdims=True))
        groups = range(start // lanes, end // lanes)
        hot = jnp.concatenate(
            [(class_row == label_ref[k : k + 1, :]).astype(F32).T for k in groups])
        valid = (row + start < left).astype(F32)
        lgrad = ((jnp.exp(logits - total) - hot) * (valid * scale)).astype(BF16)
        grad = dot_t(lgrad, w_out_ref[...])
        rounded = grad.astype(BF16)
        back = dot_t(rounded, rows_of(res_ref[...]))
        filter_slope, gate_slope = slopes(t, s)
        back_ref[at, :c] = (back * filter_slope).astype(BF16)
        back_ref[at, c:] = (back * gate_slope).astype(BF16)
        kept = min(end, grad_ref.shape[0])
        if start < kept:
            grad_ref[start:kept, :] = grad[: kept - start]
        if start < steps:
            loss = (total - jnp.sum(logits * hot, axis=1, keepdims=True)) * valid
            for j, k in enumerate(groups):
                part = jnp.where(unit, loss[j * lanes : (j + 1) * lanes], 0.0)
                loss_ref[k : k + 1, :] = jnp.sum(part, axis=0, keepdims=True)
            gated_ref[at, :] = gated
            h2_ref[at, :] = h2
            lgrad_ref[at, :] = lgrad
            round_ref[at, :] = rounded

    own = slice(0, steps)
    targets = (core, keep_ref, send_ref)
    for i in range(c // TILE):
        at = tile_of(i)
        first, per = i * (TILE // (2 * conv)), c // (2 * conv)
        conv_terms(targets, first, conv, t_dot(h1_ref[0:steps, at], back_ref[own, :]))
        conv_terms(targets, first + per, conv, t_dot(h1_ref[d : d + steps, at], back_ref[own, :]))
        value = t_dot(gated_ref[own, at], round_ref[own, :])
        store_terms(*targets, 2 * conv, value, i * (TILE // (2 * res)), res, 0, res)
        value = t_dot(h2_ref[own, at], lgrad_ref[own, :])
        count = out * classes // c
        for q in range(c // classes):
            store_terms(*targets, 2 * conv + res, value, i * (TILE // (2 * out)), out, q * count, count, q * classes)

    rows0 = back0_ref.shape[0]
    weights = halves(conv_ref, 0), halves(conv_ref, 1)
    for i in range(rows0 // TILE):
        at = tile_of(i)
        grad = grad_below(grad_ref[at, :], back_ref, i, rows - rows0, weights)
        rounded = grad.astype(BF16)
        back = dot_t(rounded, rows_of(res0_ref[...]))
        back0_ref[at, :c] = (back * slope0_ref[0, at, :].astype(F32)).astype(BF16)
        back0_ref[at, c:] = (back * slope0_ref[1, at, :].astype(F32)).astype(BF16)
        if i * TILE < steps:
            grad0_ref[at, :] = grad
            round0_ref[at, :] = rounded


def grad_below(grad, back_ref, i, d, weights):
    c = back_ref.shape[1] // 2
    (filt_past, filt_now), (gate_past, gate_now) = weights
    grad = grad + dot_t(back_ref[tile_of(i), :c], filt_now) + dot_t(back_ref[tile_of(i), c:], gate_now)
    return grad + dot_t(back_ref[tile_of(i, d), :c], filt_past) + dot_t(back_ref[tile_of(i, d), c:], gate_past)


def terms_first(sizes, scalar_ref, back_ref, grad_ref, round_ref, norm_ref, h0_ref, gated_ref, conv_ref,
                keep_ref, send_ref, last_ref):
    steps, c = grad_ref.shape
    d0 = back_ref.shape[0] - steps
    conv, res, enter, _ = sizes
    own = slice(0, steps)
    targets = (scalar_ref[0], keep_ref, send_ref)
    for i in range(c // TILE):
        at = tile_of(i)
        first, per = i * (TILE // (2 * conv)), c // (2 * conv)
        conv_terms(targets, first, conv, t_dot(h0_ref[0:steps, at], back_ref[own, :]))
        conv_terms(targets, first + per, conv, t_dot(h0_ref[d0 : d0 + steps, at], back_ref[own, :]))
        value = t_dot(gated_ref[:, at], round_ref[...])
        store_terms(*targets, 2 * conv, value, i * (TILE // (2 * res)), res, 0, res)
    weights = halves(conv_ref, 0), halves(conv_ref, 1)
    for i in range(steps // TILE):
        last_ref[tile_of(i), :] = grad_below(grad_ref[tile_of(i), :], back_ref, i, d0, weights).astype(BF16)
    value = t_dot(norm_ref[LABEL_ROWS:, :], last_ref[...])
    store_terms(*targets, 2 * conv + res, value, 0, enter, 0, enter)


def finish_kernel(sizes, one0_ref, two0_ref, one1_ref, two1_ref, conv_ref, res_ref, in_ref, out_ref):
    conv, res, _, _ = sizes
    for layer, (one, two) in enumerate(((one0_ref, two0_ref), (one1_ref, two1_ref))):
        total = one[...].astype(F32) + two[...].astype(F32)
        c = total.shape[1]
        conv_ref[layer, :, :c] = total[:conv]
        conv_ref[layer, :, c:] = total[conv : 2 * conv]
        res_ref[layer] = total[2 * conv : 2 * conv + res]
        rest = total[2 * conv + res :]
        if layer == 0:
            in_ref[...] = rest
        else:
            count, classes = rest.shape[0], out_ref.shape[1]
            for q in range(c // classes):
                out_ref[q * count : (q + 1) * count, :] = rest[:, q * classes : (q + 1) * classes]


NEAR, FAR = ("tm", 0), ("tm", 1)
CORE = ("site", 0)


def swap(value, links):
    count, pairs = lax.axis_size("site"), []
    for tm, site in itertools.product(range(lax.axis_size("tm")), range(count)):
        axis, bit = links[site]
        to = (tm ^ (1 << bit), site) if axis == "tm" else (tm, site ^ (1 << bit))
        pairs.append((tm * count + site, to[0] * count + to[1]))
    return lax.ppermute(value, ("tm", "site"), pairs)


def my_bit(links):
    first, second = ((lax.axis_index(axis) >> bit) & 1 for axis, bit in links)
    return jnp.where(lax.axis_index("site") == 0, first, second)


def time_bits():
    return lax.axis_size("tm").bit_length() - 1


def arranged(held, other, links):
    return jnp.where(
        my_bit(links) == 0, jnp.concatenate([held, other]), jnp.concatenate([other, held]))


def grow(held, links):
    return arranged(held, swap(held, links), links)


def together(*values):
    return lax.optimization_barrier(values)


def half_kernel(bits, sent, scalar_ref, one_ref, two_ref, out_ref):
    position = scalar_ref[1]
    mine = by_core(scalar_ref[0], (position >> bits[0]) & 1, (position >> bits[1]) & 1)
    index = 1 - mine if sent else mine
    for p in range(out_ref.shape[0]):
        out_ref[p] = (one_ref[p, index].astype(F32) + two_ref[p, index].astype(F32)).astype(BF16)


def halves_of(addends, scalars, links, dim):
    shape = addends[0].shape
    outer, rows = math.prod(shape[:dim]), math.prod(shape[dim + 1 : -1])
    flat = [v.reshape(outer, 2, rows, shape[-1]) for v in addends]

    def half(sent):
        bits = tuple(bit for _, bit in links)
        (value,) = call(functools.partial(half_kernel, bits, sent), [((outer, rows, shape[-1]), BF16)], [],
                        2 * 10**8, scalars, *flat)
        return value.reshape(shape[:dim] + (1,) + shape[dim + 1 :])

    return half(False), half(True)


def sum_steps():
    bits = time_bits()
    rest = [((("tm", bit),) * 2, 1 + bits - bit) for bit in range(2, bits)]
    return [((NEAR, FAR), 0), ((FAR, NEAR), 1)] + rest


def exchange(value, reach):
    size, pairs = lax.axis_size("tm"), []
    for i in range(size - reach):
        if (i // reach) % 2 == 1:
            pairs += [(i, i + reach), (i + reach, i)]
    return lax.ppermute(value, "tm", pairs)


def on_device(features, forget, labels, lengths, w_conv, w_res, w_in, w_out):
    _, steps, bands = features.shape
    time_devices, site_devices = lax.axis_size("tm"), lax.axis_size("site")
    devices = time_devices * site_devices
    c = w_res.shape[2]
    classes = w_out.shape[1]
    conv, res, enter, out = sizes = (w_conv.shape[1], w_res.shape[1], w_in.shape[0], w_out.shape[0])
    aligned = conv % 64 == 0 and res % 32 == 0
    kind = BF16 if aligned else F32
    d0, d1 = BASE_DILATION, 2 * BASE_DILATION
    reach = d0 + d1
    scalars = jnp.stack([lax.axis_index("site"), lax.axis_index("tm"), lengths[0]]).astype(jnp.int32)

    feat = features[0]
    scanned = [((steps, bands), F32)] * 3 + [((3, bands), F32)]
    if aligned:
        keep, mass, weight, carry, held0, held1 = call(
            pack_kernel, scanned + [((2 * conv + res + 2 * enter, c), BF16), ((2 * conv + res, c), BF16)], [],
            2 * 10**9, feat, forget[0], w_conv, w_res, w_in, w_out, limit=FIRST_LIMIT)
    else:
        keep, mass, weight, carry = call(scan_kernel, scanned, [], 2 * 10**9, feat, forget[0], limit=FIRST_LIMIT)
        out_own = jnp.concatenate([w_out[k * enter : (k + 1) * enter] for k in range(c // classes)], axis=1)
        held0, held1 = (jnp.concatenate([w_conv[k, :, :c], w_conv[k, :, c:], w_res[k]] + more)
                        for k, more in ((0, [w_in, out_own]), (1, [])))
    held0, held1 = held0[None], held1[None]
    carry = carry[None]
    far = [(("tm", bit),) * 2 for bit in reversed(range(2, time_bits()))]
    turns = [(NEAR, FAR), (FAR, NEAR)]
    for links in far:
        held0 = grow(held0, links)
    for link in (NEAR, FAR):
        carry = grow(carry, (link, link))
    held0, carry, held1 = together(held0, carry, held1)
    held0 = grow(held0, turns[0])
    for links in reversed(far):
        carry = grow(carry, links)
    for links in far:
        held1 = grow(held1, links)
    label_rows = steps // bands
    wide_rows = steps * bands // c + WIDE_ROWS
    normed, wide, high = call(
        norm_kernel,
        [((LABEL_ROWS + steps, bands), BF16), ((wide_rows, c), BF16), ((LABEL_ROWS + reach - steps, bands), BF16)],
                             [], 10**8,
                     scalars, feat, keep, mass, weight, carry, labels[0].reshape(label_rows, bands), limit=FIRST_LIMIT)
    held0, normed, wide, high, held1 = together(held0, normed, wide, high, held1)

    def grow_with(held, links):
        rows = held.shape[0] * held.shape[1]
        other = swap(jnp.concatenate([held.reshape(rows, c), wide]), links)
        return arranged(held, other[:rows].reshape(held.shape), links), other[rows:]

    def grow_split(held, links):
        groups, count = lax.axis_size("groups"), held.shape[1] // 2
        if groups % 2 or held.shape[1] % 2:
            return grow_with(held, links)
        plane = lax.axis_index("groups") & 1
        part = lax.dynamic_slice_in_dim(held, plane * count, count, 1)
        rows = part.shape[0] * count
        other = swap(jnp.concatenate([part.reshape(rows, c), wide]), links)
        came = other[:rows].reshape(part.shape)
        passed = lax.ppermute(came, "groups", [(i, i ^ 1) for i in range(groups)])
        full = jnp.where(
            plane == 0, jnp.concatenate([came, passed], axis=1), jnp.concatenate([passed, came], axis=1))
        return arranged(held, full, links), other[rows:]

    held0, second_wide = grow_with(held0, turns[1])
    held1, first_wide = grow_split(held1, turns[0])
    around = [first_wide, second_wide, exchange(normed, 1), exchange(high, 2)]
    held0, held1, around = together(held0, held1, around)

    def both_cores(held):
        return held.astype(kind), swap(held, (CORE, CORE)).astype(kind)

    first, other1 = both_cores(held0), swap(held1, turns[1])

    total_rows, rows0, rows1 = steps + 2 * reach, steps + d0, steps + reach
    conv_all, res_all = ((2, devices, conv, c), kind), ((devices, res, c), kind)
    V = pltpu.VMEM
    h1, out_all, label_window, h0, gated0, slope0, conv0, res0 = call(
        functools.partial(forward_first, d1, steps),
        [((total_rows - d0, c), BF16), ((c, classes), BF16), ((rows1 // bands, bands), F32), ((rows0, c), BF16), ((steps, c), BF16),
         ((2, rows0, c), BF16), conv_all, res_all],
        [V((total_rows, bands), BF16), V((total_rows, c), BF16), V((devices, enter, c), F32), V((devices, out, classes), F32)],
        2 * total_rows * c * (bands + 5 * c), scalars, normed, *around, *first)

    other1, h1 = together(other1, h1)
    second = both_cores(arranged(held1, other1, turns[1]))
    scale = 1.0 / math.sqrt(site_devices * steps * time_devices)
    package = [((time_devices, 2 * conv + res + enter, c), kind)] * 2
    loss, keep1, send1, grad1, round0, back0 = call(
        functools.partial(second_kernel, steps, scale, sizes),
        [((label_rows, bands), F32)] + package + [((steps, c), F32), ((steps, c), BF16), ((rows0, 2 * c), BF16)],
        [V((rows1, 2 * c), BF16), V((rows0, c), F32), V(*conv_all), V(*res_all),
         V((steps, c), BF16), V((steps, c), BF16), V((steps, classes), BF16), V((steps, c), BF16)],
        2 * rows1 * c * 6 * c + 2 * steps * 5 * c * c + 2 * rows0 * c * 5 * c,
        scalars, h1, out_all, label_window, *second, slope0, res0)

    def core_step(keep, send):
        other = swap(send.astype(BF16), (CORE, CORE))
        shape = (2,) * time_bits() + keep.shape[1:]
        return [keep.reshape(shape), other.reshape(shape)]

    sums1 = core_step(keep1, send1)
    keep0, send0 = call(
        functools.partial(terms_first, sizes), package, [V((steps, c), BF16)],
        2 * steps * 9 * c * c, scalars, back0, grad1, round0, normed, h0, gated0, conv0)
    sums1, keep0, send0 = together(sums1, keep0, send0)

    order = sum_steps()
    kept1, sent1 = halves_of(sums1, scalars, *order[0])
    other1 = swap(sent1, order[0][0])
    kept0, sent0 = halves_of(core_step(keep0, send0), scalars, *order[0])
    other1, sent0 = together(other1, sent0)
    for step, (links, _) in enumerate(order):
        if step + 1 < len(order):
            kept1, sent1 = halves_of([kept1, other1], scalars, *order[step + 1])
            sent1, sent0 = together(sent1, sent0)
            other1 = swap(sent1, order[step + 1][0])
        other0 = swap(sent0, links)
        if step + 1 < len(order):
            kept0, sent0 = halves_of([kept0, other0], scalars, *order[step + 1])
    sums0, sums1 = [kept0, other0], [kept1, other1]
    rows = 2 * conv + res + enter
    parts = [v.reshape(rows, c) for v in sums0 + sums1]
    grad_conv, grad_res, grad_in, grad_out = call(
        functools.partial(finish_kernel, sizes),
        [((2, conv, 2 * c), F32), ((2, res, c), F32), ((enter, c), F32), ((out, classes), F32)], [], 1,
        *parts)
    return loss.reshape(1, steps), grad_conv, grad_res, grad_in, grad_out


def solution(mesh):
    return jax.shard_map(
        on_device,
        mesh=mesh,
        in_specs=(
            P(("groups", "site"), "tm", None),
            P(("groups", "site"), "tm", None),
            P(("groups", "site"), "tm"),
            P(("groups", "site")),
            P(None, ("tm", "site"), None),
            P(None, ("tm", "site"), None),
            P(("tm", "site"), None),
            P(("tm", "site"), None),
        ),
        out_specs=(
            P(("groups", "site"), "tm"),
            P("groups", ("tm", "site"), None),
            P("groups", ("tm", "site"), None),
            P(("tm", "site"), "groups"),
            P(("tm", "site"), "groups"),
        ),
        check_vma=False,
    )
```

```python
import functools
import itertools
import math

import jax
import jax.numpy as jnp
from jax import lax
from jax.experimental import pallas as pl
from jax.experimental.pallas import tpu as pltpu
from jax.sharding import PartitionSpec as P

BASE_DILATION = 256
LEVEL_FLOOR = 0.1
F32 = jnp.float32
BF16 = jnp.bfloat16
TILE = 256
VMEM_LIMIT = 24 * 1024 * 1024
FIRST_LIMIT = 56 * 1024 * 1024
WHOLE = pl.BlockSpec(memory_space=pltpu.VMEM)
SCALAR = pl.BlockSpec(memory_space=pltpu.SMEM)


def dot(a, b):
    return lax.dot_general(a, b, (((1,), (0,)), ((), ())), preferred_element_type=F32)


def dot_t(a, b):
    return lax.dot_general(a, b, (((1,), (1,)), ((), ())), preferred_element_type=F32)


def t_dot(a, b):
    return lax.dot_general(a, b, (((0,), (0,)), ((), ())), preferred_element_type=F32)


def call(kernel, outs, scratch, flops, *args, limit=VMEM_LIMIT):
    moved = sum(a.size * a.dtype.itemsize for a in args)
    moved += sum(math.prod(s) * jnp.dtype(d).itemsize for s, d in outs)
    return pl.pallas_call(
        kernel,
        out_shape=[jax.ShapeDtypeStruct(s, d) for s, d in outs],
        in_specs=[SCALAR if a.dtype == jnp.int32 and a.ndim == 1 else WHOLE for a in args],
        out_specs=[WHOLE] * len(outs),
        scratch_shapes=scratch,
        compiler_params=pltpu.CompilerParams(vmem_limit_bytes=limit),
        cost_estimate=pl.CostEstimate(flops=flops, bytes_accessed=moved, transcendentals=0),
    )(*args)


def by_core(core, first, second):
    return first + core * (second - first)


def spots(tm, count):
    near, far, rest, step = tm & 1, (tm >> 1) & 1, tm >> 2, count // 4
    return (2 * near + far) * step + rest, (2 * far + near) * step + rest


LABEL_ROWS = 16
WIDE_ROWS = 8


def scan(feat, forget):
    rows = feat.shape[0]
    keep, mass, weight = 1.0 - forget, forget * (feat * feat), forget
    row = lax.broadcasted_iota(jnp.int32, feat.shape, 0)
    step = 1
    while step < rows:
        inside = row >= step
        before = jnp.where(inside, pltpu.roll(mass, step, 0), 0.0)
        mass = keep * before + mass
        before = jnp.where(inside, pltpu.roll(weight, step, 0), 0.0)
        weight = keep * before + weight
        keep = keep * jnp.where(inside, pltpu.roll(keep, step, 0), 1.0)
        step *= 2
    return keep, mass, weight


def scan_kernel(feat_ref, forget_ref, keep_ref, mass_ref, weight_ref, carry_ref):
    rows = feat_ref.shape[0]
    values = scan(feat_ref[...], forget_ref[...])
    for k, (ref, value) in enumerate(zip((keep_ref, mass_ref, weight_ref), values)):
        ref[...] = value
        carry_ref[k : k + 1, :] = value[rows - 1 :]


def pack_kernel(feat_ref, forget_ref, conv_ref, res_ref, in_ref, out_ref,
                keep_ref, mass_ref, weight_ref, carry_ref, first_ref, second_ref):
    scan_kernel(feat_ref, forget_ref, keep_ref, mass_ref, weight_ref, carry_ref)
    conv, res, more, c = conv_ref.shape[1], res_ref.shape[1], in_ref.shape[0], first_ref.shape[1]
    for layer, ref in enumerate((first_ref, second_ref)):
        ref[:conv, :] = conv_ref[layer, :, :c]
        ref[conv : 2 * conv, :] = conv_ref[layer, :, c:]
        ref[2 * conv : 2 * conv + res, :] = res_ref[layer]
    at = 2 * conv + res
    first_ref[at : at + more, :] = in_ref[...]
    first_ref[at + more : at + 2 * more, :] = jnp.concatenate(
        [out_ref[k * more : (k + 1) * more, :] for k in range(c // out_ref.shape[1])], axis=1)


def norm_kernel(scalar_ref, feat_ref, keep_ref, mass_ref, weight_ref, carry_ref, label_ref, out_ref, wide_ref, high_ref):
    bands = feat_ref.shape[1]
    mass0 = jnp.zeros((1, bands), F32)
    weight0 = jnp.zeros((1, bands), F32)
    for tm in range(carry_ref.shape[0]):
        before = tm < scalar_ref[1]
        keep, mass, weight = (carry_ref[tm, k : k + 1, :] for k in range(3))
        mass0 = jnp.where(before, keep * mass0 + mass, mass0)
        weight0 = jnp.where(before, keep * weight0 + weight, weight0)
    keep = keep_ref[...]
    mass = keep * mass0 + mass_ref[...]
    weight = keep * weight0 + weight_ref[...]
    normed = (feat_ref[...] / jnp.sqrt(mass / weight + LEVEL_FLOOR)).astype(BF16)
    label = jnp.concatenate(
        [label_ref[...].astype(F32), jnp.zeros((LABEL_ROWS - label_ref.shape[0], bands), F32)]).astype(BF16)
    part = high_ref.shape[0] - LABEL_ROWS
    first, last = normed[:part], normed[normed.shape[0] - part :]
    upper = (scalar_ref[1] >> 1) & 1 == 1
    for ref, value in ((out_ref, normed), (high_ref, jnp.where(upper, last, first))):
        ref[:LABEL_ROWS, :] = label
        ref[LABEL_ROWS:, :] = value
    high = normed.shape[0] * bands // wide_ref.shape[1]
    wide_ref[high:, :] = jnp.zeros((WIDE_ROWS, wide_ref.shape[1]), BF16)
    for q in range(wide_ref.shape[1] // bands):
        lanes = slice(q * bands, (q + 1) * bands)
        wide_ref[:high, lanes] = normed[q * high : (q + 1) * high]
        wide_ref[high : high + 1, lanes] = label_ref[q : q + 1, :].astype(F32).astype(BF16)


def rows_of(value):
    return value.reshape(-1, value.shape[-1]).astype(BF16)


def halves(conv_ref, gate):
    half = conv_ref.shape[1] // 2
    return rows_of(conv_ref[gate, :half]), rows_of(conv_ref[gate, half:])


def place(core, pair, conv_ref, res_ref, in_ref=None, out_ref=None):
    conv, res = conv_ref.shape[2], res_ref.shape[1]
    for ref, own in zip(pair, (True, False)):
        s = core if own else 1 - core
        rest = ref.shape[0] // 4
        bits = rest.bit_length() - 1
        for second, first in itertools.product((0, 1), repeat=2):

            def put(p, _, second=second, first=first, ref=ref, s=s):
                high = sum(((p >> (bits - 1 - b)) & 1) << b for b in range(bits))
                device = 2 * (4 * high + 2 * by_core(s, second, first) + by_core(s, first, second)) + s
                k = (2 * second + first) * rest + p
                conv_ref[0, device] = ref[k, :conv, :].astype(conv_ref.dtype)
                conv_ref[1, device] = ref[k, conv : 2 * conv, :].astype(conv_ref.dtype)
                res_ref[device] = ref[k, 2 * conv : 2 * conv + res, :].astype(res_ref.dtype)
                if in_ref is not None:
                    value = ref[k, 2 * conv + res :, :].astype(F32)
                    count, classes = value.shape[0] // 2, out_ref.shape[2]
                    in_ref[device] = value[:count]
                    for q in range(value.shape[1] // classes):
                        out_ref[device, q * count : (q + 1) * count, :] = (
                            value[count:, q * classes : (q + 1) * classes])
                return 0

            if rest <= 2:
                for p in range(rest):
                    put(p, 0)
            else:
                lax.fori_loop(0, rest, put, 0)


def activate(past, now, conv_ref):
    joined = jnp.concatenate([past, now], axis=1)
    t = jnp.tanh(dot(joined, rows_of(conv_ref[0])))
    s = 0.5 + 0.5 * jnp.tanh(0.5 * dot(joined, rows_of(conv_ref[1])))
    return t, s


def slopes(t, s):
    return s * (1.0 - t * t), t * s * (1.0 - s)


def tile_of(i, offset=0):
    return slice(i * TILE + offset, (i + 1) * TILE + offset)


def halo(scalar_ref, own_ref, first_ref, second_ref, odd_ref, high_ref, window_ref, label_ref):
    part, lane = high_ref.shape[0] - LABEL_ROWS, own_ref.shape[1]
    core = scalar_ref[0]
    odd, upper = scalar_ref[1] & 1 == 1, (scalar_ref[1] >> 1) & 1 == 1

    def rows_form(wide):
        count = wide.shape[0] - WIDE_ROWS
        groups = [slice(q * lane, (q + 1) * lane) for q in range(wide.shape[1] // lane)]
        rows = jnp.concatenate([wide[:count, g] for g in groups])
        labels = jnp.concatenate([wide[count:, g].astype(F32)[:1] for g in groups])
        return rows, labels

    first, second = first_ref[...], second_ref[...]
    near, near_labels = rows_form(jnp.where(core == 0, first, second))
    far, far_labels = rows_form(jnp.where(core == 0, second, first))
    high, far_high = high_ref[LABEL_ROWS:, :], far.shape[0] - part
    uneven = odd_ref[LABEL_ROWS:, :]
    count = part // lane

    def labels_of(ref):
        return ref[:LABEL_ROWS, :].astype(F32)

    parts = [
        (jnp.where(upper, far[far_high:], high), None),
        (jnp.where(odd, near, uneven), None),
        (own_ref[LABEL_ROWS:, :], labels_of(own_ref)[: near_labels.shape[0]]),
        (jnp.where(odd, uneven, near), jnp.where(odd, labels_of(odd_ref)[: near_labels.shape[0]], near_labels)),
        (jnp.where(upper, high, far[:part]), jnp.where(upper, labels_of(high_ref)[:count], far_labels[:count])),
    ]
    at, row = 0, 0
    for value, labels in parts:
        window_ref[at : at + value.shape[0], :] = value
        at += value.shape[0]
        if labels is not None:
            label_ref[row : row + labels.shape[0], :] = labels
            row += labels.shape[0]


def forward_first(before, steps, scalar_ref, own_ref, near_ref, far_ref, odd_ref, high_ref,
                  here_ref, there_ref, h1_ref, w_out_ref, label_ref, kept_ref, gated_ref, slope_ref, conv_ref, res_ref,
                  norm_ref, h0_ref, in_ref, out_ref):
    rows = h0_ref.shape[0]
    kept = slope_ref.shape[1]
    d = rows - h1_ref.shape[0]
    core = scalar_ref[0]
    place(core, (here_ref, there_ref), conv_ref, res_ref, in_ref, out_ref)
    halo(scalar_ref, own_ref, near_ref, far_ref, odd_ref, high_ref, norm_ref, label_ref)
    w_out_ref[...] = rows_of(out_ref[...])
    w_in = rows_of(in_ref[...])
    for i in range(rows // steps):
        at = slice(i * steps, (i + 1) * steps)
        h0_ref[at, :] = dot(norm_ref[at, :], w_in).astype(BF16)
    kept_ref[...] = h0_ref[before : before + kept, :]
    cuts = [0, before, before + steps, before + kept, h1_ref.shape[0]]
    for start, end in zip(cuts, cuts[1:]):
        at = slice(start, end)
        now = h0_ref[start + d : end + d, :]
        t, s = activate(h0_ref[at, :], now, conv_ref)
        gated = (t * s).astype(BF16)
        h1_ref[at, :] = (now.astype(F32) + dot(gated, rows_of(res_ref[...]))).astype(BF16)
        if before <= start < before + kept:
            own = slice(start - before, end - before)
            slope_ref[0, own, :], slope_ref[1, own, :] = (v.astype(BF16) for v in slopes(t, s))
            if start == before:
                gated_ref[...] = gated


def store_terms(core, keep_ref, send_ref, row, value, first, size, start, count, lane=0):
    at = (slice(row, row + count), slice(lane, lane + value.shape[1]))
    for k in range(value.shape[0] // (2 * size)):
        low = value[2 * k * size + start : 2 * k * size + start + count]
        high = value[(2 * k + 1) * size + start : (2 * k + 1) * size + start + count]
        one, two = spots(first + k, keep_ref.shape[0])
        keep_ref[(by_core(core, one, two),) + at] = jnp.where(core == 0, low, high).astype(keep_ref.dtype)
        send_ref[(by_core(core, two, one),) + at] = jnp.where(core == 0, high, low).astype(send_ref.dtype)


def conv_terms(targets, first, size, value):
    c = value.shape[1] // 2
    store_terms(*targets, 0, value[:, :c], first, size, 0, size)
    store_terms(*targets, size, value[:, c:], first, size, 0, size)


def second_kernel(steps, scale, sizes, scalar_ref, h1_ref, w_out_ref, label_ref, here_ref, there_ref,
                  slope0_ref, res0_ref,
                  loss_ref, keep_ref, send_ref, grad0_ref, round0_ref, back0_ref,
                  back_ref, grad_ref, conv_ref, res_ref, gated_ref, h2_ref, lgrad_ref, round_ref):
    rows, c = back_ref.shape[0], grad_ref.shape[1]
    d = h1_ref.shape[0] - rows
    classes = w_out_ref.shape[1]
    conv, res, _, out = sizes
    core = scalar_ref[0]
    place(core, (here_ref, there_ref), conv_ref, res_ref)

    lanes = label_ref.shape[1]
    class_row = lax.broadcasted_iota(jnp.int32, (classes, lanes), 0).astype(F32)
    unit = class_row == lax.broadcasted_iota(jnp.int32, (lanes, lanes), 1).astype(F32)
    cuts = [0, steps, rows]
    left = scalar_ref[2] - scalar_ref[1] * steps

    for start, end in zip(cuts, cuts[1:]):
        at = slice(start, end)
        row = lax.broadcasted_iota(jnp.int32, (end - start, 1), 0)
        now = h1_ref[start + d : end + d, :]
        t, s = activate(h1_ref[at, :], now, conv_ref)
        gated = (t * s).astype(BF16)
        h2 = (now.astype(F32) + dot(gated, rows_of(res_ref[...]))).astype(BF16)
        logits = dot(h2, w_out_ref[...])
        total = jnp.log(jnp.sum(jnp.exp(logits), axis=1, keepdims=True))
        groups = range(start // lanes, end // lanes)
        hot = jnp.concatenate(
            [(class_row == label_ref[k : k + 1, :]).astype(F32).T for k in groups])
        valid = (row + start < left).astype(F32)
        lgrad = ((jnp.exp(logits - total) - hot) * (valid * scale)).astype(BF16)
        grad = dot_t(lgrad, w_out_ref[...])
        rounded = grad.astype(BF16)
        back = dot_t(rounded, rows_of(res_ref[...]))
        filter_slope, gate_slope = slopes(t, s)
        back_ref[at, :c] = (back * filter_slope).astype(BF16)
        back_ref[at, c:] = (back * gate_slope).astype(BF16)
        kept = min(end, grad_ref.shape[0])
        if start < kept:
            grad_ref[start:kept, :] = grad[: kept - start]
        if start < steps:
            loss = (total - jnp.sum(logits * hot, axis=1, keepdims=True)) * valid
            for j, k in enumerate(groups):
                part = jnp.where(unit, loss[j * lanes : (j + 1) * lanes], 0.0)
                loss_ref[k : k + 1, :] = jnp.sum(part, axis=0, keepdims=True)
            gated_ref[at, :] = gated
            h2_ref[at, :] = h2
            lgrad_ref[at, :] = lgrad
            round_ref[at, :] = rounded

    own = slice(0, steps)
    targets = (core, keep_ref, send_ref)
    for i in range(c // TILE):
        at = tile_of(i)
        first, per = i * (TILE // (2 * conv)), c // (2 * conv)
        conv_terms(targets, first, conv, t_dot(h1_ref[0:steps, at], back_ref[own, :]))
        conv_terms(targets, first + per, conv, t_dot(h1_ref[d : d + steps, at], back_ref[own, :]))
        value = t_dot(gated_ref[own, at], round_ref[own, :])
        store_terms(*targets, 2 * conv, value, i * (TILE // (2 * res)), res, 0, res)
        value = t_dot(h2_ref[own, at], lgrad_ref[own, :])
        count = out * classes // c
        for q in range(c // classes):
            store_terms(*targets, 2 * conv + res, value, i * (TILE // (2 * out)), out, q * count, count, q * classes)

    rows0 = back0_ref.shape[0]
    weights = halves(conv_ref, 0), halves(conv_ref, 1)
    for i in range(rows0 // TILE):
        at = tile_of(i)
        grad = grad_below(grad_ref[at, :], back_ref, i, rows - rows0, weights)
        rounded = grad.astype(BF16)
        back = dot_t(rounded, rows_of(res0_ref[...]))
        back0_ref[at, :c] = (back * slope0_ref[0, at, :].astype(F32)).astype(BF16)
        back0_ref[at, c:] = (back * slope0_ref[1, at, :].astype(F32)).astype(BF16)
        if i * TILE < steps:
            grad0_ref[at, :] = grad
            round0_ref[at, :] = rounded


def grad_below(grad, back_ref, i, d, weights):
    c = back_ref.shape[1] // 2
    (filt_past, filt_now), (gate_past, gate_now) = weights
    grad = grad + dot_t(back_ref[tile_of(i), :c], filt_now) + dot_t(back_ref[tile_of(i), c:], gate_now)
    return grad + dot_t(back_ref[tile_of(i, d), :c], filt_past) + dot_t(back_ref[tile_of(i, d), c:], gate_past)


def terms_first(sizes, scalar_ref, back_ref, grad_ref, round_ref, norm_ref, h0_ref, gated_ref, conv_ref,
                keep_ref, send_ref, last_ref):
    steps, c = grad_ref.shape
    d0 = back_ref.shape[0] - steps
    conv, res, enter, _ = sizes
    own = slice(0, steps)
    targets = (scalar_ref[0], keep_ref, send_ref)
    for i in range(c // TILE):
        at = tile_of(i)
        first, per = i * (TILE // (2 * conv)), c // (2 * conv)
        conv_terms(targets, first, conv, t_dot(h0_ref[0:steps, at], back_ref[own, :]))
        conv_terms(targets, first + per, conv, t_dot(h0_ref[d0 : d0 + steps, at], back_ref[own, :]))
        value = t_dot(gated_ref[:, at], round_ref[...])
        store_terms(*targets, 2 * conv, value, i * (TILE // (2 * res)), res, 0, res)
    weights = halves(conv_ref, 0), halves(conv_ref, 1)
    for i in range(steps // TILE):
        last_ref[tile_of(i), :] = grad_below(grad_ref[tile_of(i), :], back_ref, i, d0, weights).astype(BF16)
    value = t_dot(norm_ref[LABEL_ROWS:, :], last_ref[...])
    store_terms(*targets, 2 * conv + res, value, 0, enter, 0, enter)


def finish_kernel(sizes, one0_ref, two0_ref, one1_ref, two1_ref, conv_ref, res_ref, in_ref, out_ref):
    conv, res, _, _ = sizes
    for layer, (one, two) in enumerate(((one0_ref, two0_ref), (one1_ref, two1_ref))):
        total = one[...].astype(F32) + two[...].astype(F32)
        c = total.shape[1]
        conv_ref[layer, :, :c] = total[:conv]
        conv_ref[layer, :, c:] = total[conv : 2 * conv]
        res_ref[layer] = total[2 * conv : 2 * conv + res]
        rest = total[2 * conv + res :]
        if layer == 0:
            in_ref[...] = rest
        else:
            count, classes = rest.shape[0], out_ref.shape[1]
            for q in range(c // classes):
                out_ref[q * count : (q + 1) * count, :] = rest[:, q * classes : (q + 1) * classes]


NEAR, FAR = ("tm", 0), ("tm", 1)
CORE = ("site", 0)


def swap(value, links):
    count, pairs = lax.axis_size("site"), []
    for tm, site in itertools.product(range(lax.axis_size("tm")), range(count)):
        axis, bit = links[site]
        to = (tm ^ (1 << bit), site) if axis == "tm" else (tm, site ^ (1 << bit))
        pairs.append((tm * count + site, to[0] * count + to[1]))
    return lax.ppermute(value, ("tm", "site"), pairs)


def my_bit(links):
    first, second = ((lax.axis_index(axis) >> bit) & 1 for axis, bit in links)
    return jnp.where(lax.axis_index("site") == 0, first, second)


def time_bits():
    return lax.axis_size("tm").bit_length() - 1


def arranged(held, other, links):
    return jnp.where(
        my_bit(links) == 0, jnp.concatenate([held, other]), jnp.concatenate([other, held]))


def grow(held, links):
    return arranged(held, swap(held, links), links)


def together(*values):
    return lax.optimization_barrier(values)


def half_kernel(bits, sent, scalar_ref, one_ref, two_ref, out_ref):
    position = scalar_ref[1]
    mine = by_core(scalar_ref[0], (position >> bits[0]) & 1, (position >> bits[1]) & 1)
    index = 1 - mine if sent else mine
    for p in range(out_ref.shape[0]):
        out_ref[p] = (one_ref[p, index].astype(F32) + two_ref[p, index].astype(F32)).astype(BF16)


def halves_of(addends, scalars, links, dim):
    shape = addends[0].shape
    outer, rows = math.prod(shape[:dim]), math.prod(shape[dim + 1 : -1])
    flat = [v.reshape(outer, 2, rows, shape[-1]) for v in addends]

    def half(sent):
        bits = tuple(bit for _, bit in links)
        (value,) = call(functools.partial(half_kernel, bits, sent), [((outer, rows, shape[-1]), BF16)], [],
                        2 * 10**8, scalars, *flat)
        return value.reshape(shape[:dim] + (1,) + shape[dim + 1 :])

    return half(False), half(True)


def sum_steps():
    bits = time_bits()
    rest = [((("tm", bit),) * 2, 1 + bits - bit) for bit in range(2, bits)]
    return [((NEAR, FAR), 0), ((FAR, NEAR), 1)] + rest


def exchange(value, reach):
    size, pairs = lax.axis_size("tm"), []
    for i in range(size - reach):
        if (i // reach) % 2 == 1:
            pairs += [(i, i + reach), (i + reach, i)]
    return lax.ppermute(value, "tm", pairs)


def on_device(features, forget, labels, lengths, w_conv, w_res, w_in, w_out):
    _, steps, bands = features.shape
    time_devices, site_devices = lax.axis_size("tm"), lax.axis_size("site")
    devices = time_devices * site_devices
    c = w_res.shape[2]
    classes = w_out.shape[1]
    conv, res, enter, out = sizes = (w_conv.shape[1], w_res.shape[1], w_in.shape[0], w_out.shape[0])
    aligned = conv % 64 == 0 and res % 32 == 0
    kind = BF16 if aligned else F32
    d0, d1 = BASE_DILATION, 2 * BASE_DILATION
    reach = d0 + d1
    scalars = jnp.stack([lax.axis_index("site"), lax.axis_index("tm"), lengths[0]]).astype(jnp.int32)

    feat = features[0]
    scanned = [((steps, bands), F32)] * 3 + [((3, bands), F32)]
    if aligned:
        keep, mass, weight, carry, held0, held1 = call(
            pack_kernel, scanned + [((2 * conv + res + 2 * enter, c), BF16), ((2 * conv + res, c), BF16)], [],
            2 * 10**9, feat, forget[0], w_conv, w_res, w_in, w_out, limit=FIRST_LIMIT)
    else:
        keep, mass, weight, carry = call(scan_kernel, scanned, [], 2 * 10**9, feat, forget[0], limit=FIRST_LIMIT)
        out_own = jnp.concatenate([w_out[k * enter : (k + 1) * enter] for k in range(c // classes)], axis=1)
        held0, held1 = (jnp.concatenate([w_conv[k, :, :c], w_conv[k, :, c:], w_res[k]] + more)
                        for k, more in ((0, [w_in, out_own]), (1, [])))
    held0, held1 = held0[None], held1[None]
    carry = carry[None]
    far = [(("tm", bit),) * 2 for bit in reversed(range(2, time_bits()))]
    turns = [(NEAR, FAR), (FAR, NEAR)]
    for links in far:
        held0 = grow(held0, links)
    for link in (NEAR, FAR):
        carry = grow(carry, (link, link))
    held0, carry, held1 = together(held0, carry, held1)
    held0 = grow(held0, turns[0])
    for links in reversed(far):
        carry = grow(carry, links)
    for links in far:
        held1 = grow(held1, links)
    label_rows = steps // bands
    wide_rows = steps * bands // c + WIDE_ROWS
    normed, wide, high = call(
        norm_kernel,
        [((LABEL_ROWS + steps, bands), BF16), ((wide_rows, c), BF16), ((LABEL_ROWS + reach - steps, bands), BF16)],
                             [], 10**8,
                     scalars, feat, keep, mass, weight, carry, labels[0].reshape(label_rows, bands), limit=FIRST_LIMIT)
    held0, normed, wide, high, held1 = together(held0, normed, wide, high, held1)

    def grow_with(held, links):
        rows = held.shape[0] * held.shape[1]
        other = swap(jnp.concatenate([held.reshape(rows, c), wide]), links)
        return arranged(held, other[:rows].reshape(held.shape), links), other[rows:]

    held0, second_wide = grow_with(held0, turns[1])
    held1, first_wide = grow_with(held1, turns[0])
    around = [first_wide, second_wide, exchange(normed, 1), exchange(high, 2)]
    held0, held1, around = together(held0, held1, around)

    def both_cores(held):
        return held.astype(kind), swap(held, (CORE, CORE)).astype(kind)

    first, other1 = both_cores(held0), swap(held1, turns[1])

    total_rows, rows0, rows1 = steps + 2 * reach, steps + d0, steps + reach
    conv_all, res_all = ((2, devices, conv, c), kind), ((devices, res, c), kind)
    V = pltpu.VMEM
    h1, out_all, label_window, h0, gated0, slope0, conv0, res0 = call(
        functools.partial(forward_first, d1, steps),
        [((total_rows - d0, c), BF16), ((c, classes), BF16), ((rows1 // bands, bands), F32), ((rows0, c), BF16), ((steps, c), BF16),
         ((2, rows0, c), BF16), conv_all, res_all],
        [V((total_rows, bands), BF16), V((total_rows, c), BF16), V((devices, enter, c), F32), V((devices, out, classes), F32)],
        2 * total_rows * c * (bands + 5 * c), scalars, normed, *around, *first)

    other1, h1 = together(other1, h1)
    second = both_cores(arranged(held1, other1, turns[1]))
    scale = 1.0 / math.sqrt(site_devices * steps * time_devices)
    package = [((time_devices, 2 * conv + res + enter, c), kind)] * 2
    loss, keep1, send1, grad1, round0, back0 = call(
        functools.partial(second_kernel, steps, scale, sizes),
        [((label_rows, bands), F32)] + package + [((steps, c), F32), ((steps, c), BF16), ((rows0, 2 * c), BF16)],
        [V((rows1, 2 * c), BF16), V((rows0, c), F32), V(*conv_all), V(*res_all),
         V((steps, c), BF16), V((steps, c), BF16), V((steps, classes), BF16), V((steps, c), BF16)],
        2 * rows1 * c * 6 * c + 2 * steps * 5 * c * c + 2 * rows0 * c * 5 * c,
        scalars, h1, out_all, label_window, *second, slope0, res0)

    def core_step(keep, send):
        other = swap(send.astype(BF16), (CORE, CORE))
        shape = (2,) * time_bits() + keep.shape[1:]
        return [keep.reshape(shape), other.reshape(shape)]

    sums1 = core_step(keep1, send1)
    keep0, send0 = call(
        functools.partial(terms_first, sizes), package, [V((steps, c), BF16)],
        2 * steps * 9 * c * c, scalars, back0, grad1, round0, normed, h0, gated0, conv0)
    sums1, keep0, send0 = together(sums1, keep0, send0)

    order = sum_steps()
    kept1, sent1 = halves_of(sums1, scalars, *order[0])
    other1 = swap(sent1, order[0][0])
    kept0, sent0 = halves_of(core_step(keep0, send0), scalars, *order[0])
    other1, sent0 = together(other1, sent0)
    for step, (links, _) in enumerate(order):
        if step + 1 < len(order):
            kept1, sent1 = halves_of([kept1, other1], scalars, *order[step + 1])
            sent1, sent0 = together(sent1, sent0)
            other1 = swap(sent1, order[step + 1][0])
        other0 = swap(sent0, links)
        if step + 1 < len(order):
            kept0, sent0 = halves_of([kept0, other0], scalars, *order[step + 1])
    sums0, sums1 = [kept0, other0], [kept1, other1]
    rows = 2 * conv + res + enter
    parts = [v.reshape(rows, c) for v in sums0 + sums1]
    grad_conv, grad_res, grad_in, grad_out = call(
        functools.partial(finish_kernel, sizes),
        [((2, conv, 2 * c), F32), ((2, res, c), F32), ((enter, c), F32), ((out, classes), F32)], [], 1,
        *parts)
    return loss.reshape(1, steps), grad_conv, grad_res, grad_in, grad_out


def solution(mesh):
    return jax.shard_map(
        on_device,
        mesh=mesh,
        in_specs=(
            P(("groups", "site"), "tm", None),
            P(("groups", "site"), "tm", None),
            P(("groups", "site"), "tm"),
            P(("groups", "site")),
            P(None, ("tm", "site"), None),
            P(None, ("tm", "site"), None),
            P(("tm", "site"), None),
            P(("tm", "site"), None),
        ),
        out_specs=(
            P(("groups", "site"), "tm"),
            P("groups", ("tm", "site"), None),
            P("groups", ("tm", "site"), None),
            P(("tm", "site"), "groups"),
            P(("tm", "site"), "groups"),
        ),
        check_vma=False,
    )
```
